128 devices in a mesh: dp: 8 (over x, core), fsdp: 16 (over y, z).
Axes of the slice: x: 4, y: 4, z: 4, core: 2. Of those that a mesh axis runs over, the one named last changes fastest.
Arguments:
- latents: bfloat16 [256, 512, 512], P(('dp', 'fsdp')), may hold values from -6 to 6
- task_ids: int32 [256], P(('dp', 'fsdp')), may hold values from 0 to 17
- slot_counts: int32 [256], P(('dp', 'fsdp')), may hold values from 128 to 512, as said below
- cotangent: bfloat16 [256, 512, 512], P(('dp', 'fsdp')), may hold values from -6 to 6
- task_embed: bfloat16 [18, 512], P(None, ('dp', 'fsdp')), may hold values from -3 to 3
- norms: bfloat16 [4, 512], P(None, ('dp', 'fsdp')), may hold values from 0.5 to 1.5
- attn_in: bfloat16 [512, 1536], P(('dp', 'fsdp')), may hold values from -0.25 to 0.25
- attn_out: bfloat16 [512, 512], P(('dp', 'fsdp')), may hold values from -2 to 2
- out_biases: bfloat16 [2, 512], P(None, ('dp', 'fsdp')), may hold values from -2 to 2
- mlp_in: bfloat16 [512, 2048], P(('dp', 'fsdp')), may hold values from -0.25 to 0.25
- mlp_in_bias: bfloat16 [2048], P(('dp', 'fsdp')), may hold values from -3 to 3
- mlp_out: bfloat16 [2048, 512], P(('dp', 'fsdp')), may hold values from -0.125 to 0.125
Outputs:
- latents_out: bfloat16 [256, 512, 512], P(('dp', 'fsdp'))
- grad_latents: bfloat16 [256, 512, 512], P(('dp', 'fsdp'))
- grad_task_embed: float32 [18, 512], P(None, ('dp', 'fsdp'))
- grad_norms: float32 [4, 512], P(None, ('dp', 'fsdp'))
- grad_attn_in: float32 [512, 1536], P(('dp', 'fsdp'))
- grad_attn_out: float32 [512, 512], P(('dp', 'fsdp'))
- grad_out_biases: float32 [2, 512], P(None, ('dp', 'fsdp'))
- grad_mlp_in: float32 [512, 2048], P(('dp', 'fsdp'))
- grad_mlp_in_bias: float32 [2048], P(('dp', 'fsdp'))
- grad_mlp_out: float32 [2048, 512], P(('dp', 'fsdp'))
The draws below stay inside these ranges and needn't reach their ends.
Inputs may be any that keep to these rules, and one draw needn't show every extreme that they name: `slot_counts`: some array has exactly 512 valid slots and some has exactly 128.
All inputs are finite; a program needn't handle non-finite values.
Results may differ from the reference program's by a relative error of at most 0.012.
Values may be sent and summed in bfloat16 or wider, within the bound.
A program may use at most 192 MiB of HBM per device.

```python
import math
import jax
import jax.numpy as jnp
import numpy as np
from jax import lax

D = 512
FF = 2048
HEADS = 8
LAT = 512
TASKS = 18
ARRAYS = 256


def draw_slot_counts(key, part):
    key = jax.random.fold_in(key, 5)
    first, second, third = jax.random.split(key, 3)
    counts = jax.random.randint(first, (ARRAYS,), LAT // 4, LAT + 1)
    place_full = jax.random.randint(second, (), 0, ARRAYS)
    offset = jax.random.randint(third, (), 1, ARRAYS)
    place_least = (place_full + offset) % ARRAYS
    counts = counts.at[place_full].set(LAT).at[place_least].set(LAT // 4)
    return counts.astype(jnp.int32)


def set_ends(values, rng, low, top_value):
    shape = values.shape
    index_at = [jax.random.randint(jax.random.fold_in(rng, axis), (), 0, shape[axis]) for axis in range(len(shape))]
    values = values.at[tuple(index_at)].set(low)
    longest = shape.index(max(shape))
    index_at[longest] = (index_at[longest] + 1) % shape[longest]
    return values.at[tuple(index_at)].set(top_value)


def steps_of(own_key, dims, shards, low, top_value):
    def one(position, parts):
        heights = jax.random.uniform(jax.random.fold_in(jax.random.fold_in(own_key, 6), position), (parts,), jnp.float32, low / len(shards), top_value / len(shards))
        return jnp.repeat(jnp.exp(heights), dims[position] // parts).reshape((-1,) + (1,) * (len(dims) - position - 1))

    level = one(*shards[0])
    for cut in shards[1:]:
        level = level * one(*cut)
    return level


def cumulative_ranks(amount, skew):
    weights = [(1 << 20) // math.isqrt(grade ** skew) + 1 for grade in range(1, amount + 1)]
    scale = 1 + sum(weights) // (1 << 30)
    return np.cumsum(np.array([max(1, weight // scale) for weight in weights]))


def skewed_ids(key, extent, count, lean):
    table = cumulative_ranks(count, lean)
    ticket = jax.random.randint(jax.random.fold_in(key, 1), extent, 0, int(table[count - 1]))
    grade = jnp.searchsorted(jnp.asarray(table, jnp.int32), ticket, side="right")
    return jax.random.permutation(jax.random.fold_in(key, 2), count)[grade].astype(jnp.int32)


def bell_draw(stream_key, shape, spread, most, shards=(), dtype=jnp.bfloat16):
    loudness = steps_of(stream_key, shape, shards, -0.22, 0.18) if shards else 1.0
    values = jax.random.normal(stream_key, shape, jnp.float32) * spread * loudness
    return jnp.minimum(jnp.maximum(values, -most), most).astype(dtype)


def setup_inputs(seed: int = 0) -> dict:
    streams_of = jax.random.split(jax.random.key(seed), 13)
    return {
        "latents": bell_draw(streams_of[0], (ARRAYS, LAT, D), 1.0, 6.0, ((0, 128),)),
        "task_ids": set_ends(skewed_ids(streams_of[1], (ARRAYS,), TASKS, 2), jax.random.fold_in(streams_of[1], 3), 0, TASKS - 1).astype(jnp.int32),
        "slot_counts": draw_slot_counts(jax.random.fold_in(streams_of[12], 71), 0),
        "cotangent": bell_draw(streams_of[3], (ARRAYS, LAT, D), 1.0, 6.0, ((0, 128),)),
        "task_embed": bell_draw(streams_of[4], (TASKS, D), 0.5, 3.0, ((1, 128),)),
        "norms": jnp.clip(0.5 + 1.0 * jax.random.uniform(streams_of[5], (4, D), jnp.float32) ** steps_of(streams_of[5], (4, D), ((1, 128),), -0.2, 0.2), 0.5, 1.5).astype(jnp.bfloat16),
        "attn_in": bell_draw(streams_of[6], (D, 3 * D), D ** -0.5, 0.25, ((0, 128),)),
        "attn_out": bell_draw(streams_of[7], (D, D), (D // 64) ** -0.5, 2.0, ((0, 128),)),
        "out_biases": bell_draw(streams_of[8], (2, D), 0.3, 2.0, ((1, 128),)),
        "mlp_in": bell_draw(streams_of[9], (D, FF), D ** -0.5, 0.25, ((0, 128),)),
        "mlp_in_bias": bell_draw(streams_of[10], (FF,), 0.5, 3.0, ((0, 128),)),
        "mlp_out": bell_draw(streams_of[11], (FF, D), FF ** -0.5, 0.125, ((0, 128),)),
    }


@jax.custom_vjp
def low(v):
    return lax.optimization_barrier(v.astype(jnp.bfloat16)).astype(jnp.float32)

@jax.custom_vjp
def low_back(v):
    return v

def low_keep(v):
    return (low(v), None)

def low_pass(kept, grad):
    return (grad,)

def back_keep(v):
    return (v, None)

def back_low(kept, grad):
    return (low(grad),)
low.defvjp(low_keep, low_pass)
low_back.defvjp(back_keep, back_low)
EPS = 1e-05
BEST = lax.Precision.HIGHEST

def matmul(left, right):
    return jnp.dot(left, right, precision=BEST, preferred_element_type=jnp.float32)

def normalize(h, gain, shift):
    mean = lax.optimization_barrier(jnp.mean(h, axis=-1, keepdims=True))
    centred = h - mean
    var = lax.optimization_barrier(jnp.mean(centred * centred, axis=-1, keepdims=True))
    return centred * lax.rsqrt(var + EPS) * gain + shift

def attend(block):
    query, key, value, count = block
    length = query.shape[0]
    scale = 1.0 / math.sqrt(query.shape[2])
    raw = low_back(jnp.einsum('lhe,mhe->hlm', query, key, precision=BEST))
    scores = raw * scale
    valid = jnp.arange(length)[None, None, :] < count
    scores = jnp.where(valid, scores, -1000000000.0)
    top = lax.optimization_barrier(jnp.max(scores, axis=-1, keepdims=True))
    expo = jnp.exp(scores - top)
    probs = expo / lax.optimization_barrier(jnp.sum(expo, axis=-1, keepdims=True))
    mixed = jnp.einsum('hlm,mhe->lhe', low(probs), value, precision=BEST)
    return mixed.reshape(length, -1)

def layer(latents, task_embed, norms, attn_in, attn_out, out_biases, mlp_in, mlp_in_bias, mlp_out, task_rows, counts):
    group, length, width = latents.shape
    size_head = width // HEADS
    start = latents + task_embed[task_rows][:, None, :]
    flat0 = start.reshape(group * length, width)
    input1 = low(normalize(flat0, norms[0], norms[1]))
    joined = low(low_back(matmul(input1, attn_in)))
    joined = joined.reshape(group, length, 3, HEADS, size_head)
    mixed = lax.map(jax.checkpoint(attend), (joined[:, :, 0], joined[:, :, 1], joined[:, :, 2], counts))
    mixed = low(low_back(mixed.reshape(group * length, width)))
    branch = low_back(matmul(mixed, attn_out) + out_biases[0])
    flat1 = flat0 + branch
    input2 = low(normalize(flat1, norms[2], norms[3]))
    hidden = low_back(matmul(input2, mlp_in) + mlp_in_bias)
    active = low(jax.nn.gelu(hidden))
    flat2 = flat1 + matmul(active, mlp_out) + out_biases[1]
    return flat2.reshape(group, length, width)

def reference(latents, task_ids, slot_counts, cotangent, task_embed, norms, attn_in, attn_out, out_biases, mlp_in, mlp_in_bias, mlp_out):
    weights = tuple((w.astype(jnp.float32) for w in (task_embed, norms, attn_in, attn_out, out_biases, mlp_in, mlp_in_bias, mlp_out)))
    arrays, length, width = latents.shape
    group = min(8, arrays)
    count_steps = arrays // group
    items = (latents.reshape(count_steps, group, length, width), task_ids.reshape(count_steps, group), slot_counts.reshape(count_steps, group), cotangent.reshape(count_steps, group, length, width))

    def one(totals, item):
        lat, rows, cnt, cot = item

        def run(x, *params):
            return layer(x, *params, rows, cnt)
        result, pull = jax.vjp(run, lat.astype(jnp.float32), *weights)
        grads = pull(cot.astype(jnp.float32))
        new_totals = tuple((t + g for t, g in zip(totals, grads[1:])))
        return (new_totals, (result.astype(jnp.bfloat16), grads[0].astype(jnp.bfloat16)))
    zeros = tuple((jnp.zeros(w.shape, jnp.float32) for w in weights))
    totals, (outs, grad_in) = lax.scan(one, zeros, items)
    return (outs.reshape(arrays, length, width), grad_in.reshape(arrays, length, width), totals[0], totals[1], totals[2], totals[3], totals[4], totals[5], totals[6], totals[7])
```

```python
import functools
import math

import jax
import jax.numpy as jnp
from jax import lax
from jax.experimental import pallas as pl
from jax.experimental.pallas import tpu as pltpu
from jax.sharding import PartitionSpec as P

HEADS = 8
EPS = 1e-05
BEST = lax.Precision.HIGHEST
MESH = pl.DeviceIdType.MESH
ALL = slice(None)
ORDERS = (("z", "y", "x"), ("y", "x", "z"), ("x", "z", "y"))
TILES = 12
WAVES = (((0, 1), (1, 1), (2, 1)), ((3, 3), (6, 3), (9, 3)))


def my_position():
    dp, fsdp = lax.axis_index("dp"), lax.axis_index("fsdp")
    return {
        "x": lax.div(dp, 2),
        "c": lax.rem(dp, 2),
        "y": lax.div(fsdp, 4),
        "z": lax.rem(fsdp, 4),
    }


def moved(pos, axis, step):
    size = 2 if axis == "c" else 4
    return {**pos, axis: lax.rem(pos[axis] + step, size)}


def device_of(pos):
    return (pos["x"] * 2 + pos["c"], pos["y"] * 4 + pos["z"])


def greet(pos):
    barrier = pltpu.get_barrier_semaphore()
    partners = [moved(pos, axis, k) for axis in "xyz" for k in (1, 2, 3)] + [moved(pos, "c", 1)]
    for other in partners:
        pl.semaphore_signal(barrier, inc=1, device_id=device_of(other), device_id_type=MESH)
    pl.semaphore_wait(barrier, len(partners))


def remote(src, dst, send, recv, pos):
    return pltpu.make_async_remote_copy(
        src_ref=src, dst_ref=dst, send_sem=send, recv_sem=recv,
        device_id=device_of(pos), device_id_type=MESH,
    )


class Gather:
    def __init__(self, wave, own, tiles, send, recv, pos):
        self.wave, self.own, self.tiles, self.pos = wave, own, tiles, pos
        self.send, self.recv = send, recv

    def slab(self, part, free, at=None):
        first, count = WAVES[self.wave][part]
        place = {**self.pos, **(at or {})}
        index = [ALL if axis in free else place[axis] for axis in "xcyz"]
        return self.tiles.at[(pl.ds(first, count), *index)]

    def stage_copy(self, part, stage, k):
        order = ORDERS[part]
        slab = self.slab(part, order[:stage])
        src = slab
        if stage == 0:
            first, count = WAVES[self.wave][part]
            src = self.own.at[pl.ds(first, count)]
        slot = (self.wave, part, stage * 3 + k - 1)
        return remote(src, slab, self.send.at[slot], self.recv.at[slot], moved(self.pos, order[stage], k))

    def pair_copy(self, part, k):
        order = ORDERS[part]
        at = {order[2]: lax.rem(self.pos[order[2]] + 4 - k, 4)} if k else None
        slab = self.slab(part, order[:2], at)
        slot = (self.wave, part, 9 + k)
        return remote(slab, slab, self.send.at[slot], self.recv.at[slot], moved(self.pos, "c", 1))

    def start(self, stage):
        for part in range(3):
            for k in (2, 1, 3):
                self.stage_copy(part, stage, k).start()
            if stage == 2:
                self.pair_copy(part, 0).start()

    def arrive(self, stage):
        for part in range(3):
            for k in (1, 3, 2):
                self.stage_copy(part, stage, k).wait_recv()
                if stage == 2:
                    self.pair_copy(part, k).start()

    def arrive_pair(self):
        for part in range(3):
            for k in range(4):
                self.pair_copy(part, k).wait_recv()

    def settle(self):
        for part in range(3):
            for stage in range(3):
                for k in (1, 2, 3):
                    self.stage_copy(part, stage, k).wait_send()
            for k in range(4):
                self.pair_copy(part, k).wait_send()


class SmallGather:
    def __init__(self, own, slots, kept, pair, send, recv, pos):
        self.own, self.slots, self.kept, self.pair = own, slots, kept, pair
        self.send, self.recv, self.pos = send, recv, pos

    def copy(self, stage, k):
        here = self.kept.at[self.pos["x"]]
        src = self.own if stage == 0 else here
        dst = here if stage == 2 else self.slots.at[stage, k - 1]
        slot = stage * 3 + k - 1
        return remote(src, dst, self.send.at[slot], self.recv.at[slot], moved(self.pos, "zyx"[stage], k))

    def pair_copy(self):
        return remote(self.kept, self.pair, self.send.at[9], self.recv.at[9], moved(self.pos, "c", 1))

    def start(self, stage):
        for k in (2, 1, 3):
            self.copy(stage, k).start()

    def arrive(self, stage):
        for k in (1, 3, 2):
            self.copy(stage, k).wait_recv()
        if stage == 2:
            self.pair_copy().start()
            return
        total = self.own[...] if stage == 0 else self.kept[self.pos["x"]]
        if stage == 1:
            for k in (1, 2, 3):
                self.copy(1, k).wait_send()
        for k in range(3):
            total = total + self.slots[stage, k]
        self.kept[self.pos["x"]] = total

    def arrive_pair(self, out):
        self.pair_copy().wait_recv()
        for x in range(4):
            out[:, x * 128 : (x + 1) * 128] = self.kept[x].astype(jnp.float32) + self.pair[x].astype(jnp.float32)

    def settle(self):
        for stage in (0, 2):
            for k in (1, 2, 3):
                self.copy(stage, k).wait_send()
        self.pair_copy().wait_send()


class Scatter:
    def __init__(self, wave, tiles, from_pair, from1, from2, from3, send, recv, pos):
        self.wave, self.tiles, self.pos = wave, tiles, pos
        self.from_pair, self.from_stage = from_pair, (from1, from2, from3)
        self.send, self.recv = send, recv

    def order(self, part):
        return ORDERS[part][::-1]

    def span(self, part):
        return WAVES[self.wave][part]

    def pair_copy(self, part):
        first, count = self.span(part)
        other = moved(self.pos, "c", 1)
        slot = (self.wave, part, 9)
        return remote(
            self.tiles.at[pl.ds(first, count), :, other["c"]], self.from_pair.at[pl.ds(first, count)],
            self.send.at[slot], self.recv.at[slot], other,
        )

    def index(self, part, stage, at=None):
        place = {**self.pos, **(at or {})}
        held = self.order(part)[: stage + 1]
        return tuple(place[axis] if axis in held or axis == "c" else ALL for axis in "xcyz")

    def stage_copy(self, part, stage, k):
        first, count = self.span(part)
        axis = self.order(part)[stage]
        other = moved(self.pos, axis, k)
        slot = (self.wave, part, stage * 3 + k - 1)
        src = self.tiles.at[(pl.ds(first, count), *self.index(part, stage, other))]
        dst = self.from_stage[stage].at[pl.ds(first, count), k - 1]
        return remote(src, dst, self.send.at[slot], self.recv.at[slot], other)

    def start_pair(self, part):
        self.pair_copy(part).start()

    def add_pair(self, part):
        first, count = self.span(part)
        self.pair_copy(part).wait_recv()
        core = self.pos["c"]

        def add(i, carry):
            t, x = first + lax.div(i, 4), lax.rem(i, 4)
            total = self.tiles[t, x, core].astype(jnp.float32) + self.from_pair[t, x].astype(jnp.float32)
            self.tiles[t, x, core] = total.astype(jnp.bfloat16)
            return carry

        lax.fori_loop(0, count * 4, add, 0)

    def start(self, part, stage):
        for k in (2, 1, 3):
            self.stage_copy(part, stage, k).start()

    def add(self, part, stage, out=None):
        first, count = self.span(part)
        for k in (1, 3, 2):
            self.stage_copy(part, stage, k).wait_recv()
        index = self.index(part, stage)

        def add(t):
            total = self.tiles[(t, *index)].astype(jnp.float32)
            for k in range(3):
                total = total + self.from_stage[stage][t, k].astype(jnp.float32)
            if stage == 2:
                out[t] = total
            else:
                self.tiles[(t, *index)] = total.astype(jnp.bfloat16)

        for t in range(first, first + count):
            add(t)

    def settle(self):
        for part in range(3):
            self.pair_copy(part).wait_send()
            for stage in range(3):
                for k in (1, 2, 3):
                    self.stage_copy(part, stage, k).wait_send()


class SmallScatter:
    def __init__(self, own, pair, slots, held, send, recv, pos):
        self.own, self.pair, self.slots, self.held = own, pair, slots, held
        self.send, self.recv, self.pos = send, recv, pos

    def pair_copy(self):
        return remote(self.own, self.pair, self.send.at[9], self.recv.at[9], moved(self.pos, "c", 1))

    def copy(self, stage, k):
        other = moved(self.pos, "xyz"[stage], k)
        src = self.held.at[other["x"]] if stage == 0 else self.held.at[3 + stage]
        slot = stage * 3 + k - 1
        return remote(src, self.slots.at[stage, k - 1], self.send.at[slot], self.recv.at[slot], other)

    def add_pair(self):
        self.pair_copy().wait_recv()
        self.held[0:4] = self.own[...] + self.pair[...]

    def start(self, stage):
        for k in (2, 1, 3):
            self.copy(stage, k).start()

    def add(self, stage):
        for k in (1, 3, 2):
            self.copy(stage, k).wait_recv()
        total = self.held[self.pos["x"]] if stage == 0 else self.held[3 + stage]
        for k in range(3):
            total = total + self.slots[stage, k]
        self.held[4 + stage] = total

    def settle(self):
        self.pair_copy().wait_send()
        for stage in range(3):
            for k in (1, 2, 3):
                self.copy(stage, k).wait_send()


def quarter_order(transposed=False):
    a = lax.broadcasted_iota(jnp.int32, (256, 256), 1 if transposed else 0)
    b = lax.broadcasted_iota(jnp.int32, (256, 256), 0 if transposed else 1)
    source = ((a % 64) // 4) * 16 + (a // 64) * 4 + a % 4
    return (source == b).astype(jnp.float32).astype(jnp.bfloat16)


def unfold(tiles, first, count, out):
    order = quarter_order()

    def one(i, carry):
        x, c = lax.div(i, 2), lax.rem(i, 2)
        blocks = [tiles[first + t, x, c].reshape(256, 128) for t in range(count)]
        rows = jnp.dot(order, jnp.concatenate(blocks, 1), preferred_element_type=jnp.float32).astype(jnp.bfloat16)
        for q in range(4):
            out[pl.ds(pl.multiple_of(i * 64, 64), 64), q * count * 128 : (q + 1) * count * 128] = rows[q * 64 : (q + 1) * 64]
        return carry

    lax.fori_loop(0, 8, one, 0)


def unfold_plain(tiles, first, count, out):
    def one(i, carry):
        x, c = lax.div(i, 2), lax.rem(i, 2)
        for t in range(count):
            out[pl.ds(pl.multiple_of(i * 256, 256), 256), t * 128 : (t + 1) * 128] = tiles[first + t, x, c].reshape(256, 128)
        return carry

    lax.fori_loop(0, 8, one, 0)


def fold(grad, tiles, first, count):
    order = quarter_order(True)

    def one(i, carry):
        x, c = lax.div(i, 2), lax.rem(i, 2)
        rows = [
            grad[pl.ds(pl.multiple_of(i * 64, 64), 64), q * count * 128 : (q + 1) * count * 128].astype(jnp.bfloat16)
            for q in range(4)
        ]
        blocks = jnp.dot(order, jnp.concatenate(rows, 0), preferred_element_type=jnp.float32).astype(jnp.bfloat16)
        for t in range(count):
            tiles[first + t, x, c] = blocks[:, t * 128 : (t + 1) * 128].reshape(4, 4, 16, 128)
        return carry

    lax.fori_loop(0, 8, one, 0)


def fold_plain(grad, tiles, first, count):
    def one(i, carry):
        x, c = lax.div(i, 2), lax.rem(i, 2)
        for t in range(count):
            block = grad[pl.ds(pl.multiple_of(i * 256, 256), 256), t * 128 : (t + 1) * 128]
            tiles[first + t, x, c] = block.astype(jnp.bfloat16).reshape(4, 4, 16, 128)
        return carry

    lax.fori_loop(0, 8, one, 0)


def shard_tiles(attn_in, attn_out, mlp_in, mlp_out):
    def quarters(w, count):
        return w.reshape(4, 4, count, 128).transpose(2, 1, 0, 3).reshape(count, 16, 128)

    return jnp.concatenate(
        (
            quarters(attn_in, 3),
            quarters(attn_out, 1),
            quarters(mlp_in, 4),
            mlp_out.reshape(16, 4, 128).transpose(1, 0, 2),
        )
    )


def shard_small(task_embed, norms, out_biases, mlp_in_bias):
    pos = my_position()
    ring = pos["y"] * 4 + pos["z"]
    block = jnp.zeros((32, 128), jnp.bfloat16)
    rows = jnp.concatenate((task_embed, norms, out_biases))
    block = lax.dynamic_update_slice(block, rows, (0, pos["c"] * 64 + ring * 4))
    at = (24 + pos["c"] * 2 + lax.div(ring, 8), 16 * lax.rem(ring, 8))
    return lax.dynamic_update_slice(block, mlp_in_bias[None, :], at)


def own_small(block):
    pos = my_position()
    ring = pos["y"] * 4 + pos["z"]
    columns = lax.dynamic_slice(block, (0, pos["c"] * 64 + ring * 4), (24, 4))
    at = (24 + pos["c"] * 2 + lax.div(ring, 8), 16 * lax.rem(ring, 8))
    bias = lax.dynamic_slice(block, at, (1, 16))[0]
    return columns[0:18], columns[18:22], columns[22:24], bias


def own_weights(total):
    def quarters(t, count):
        return t.reshape(count, 4, 4, 128).transpose(2, 1, 0, 3).reshape(4, 4 * count * 128)

    return quarters(total[0:3], 3), quarters(total[3:4], 1), quarters(total[4:8], 4), total[8:12].transpose(1, 0, 2).reshape(16, 512)


def gather_kernel(own, small, w_qkv, w_out, w_up, w_down, params, tiles, slots, kept, pair, send, recv, s_send, s_recv):
    pos = my_position()
    greet(pos)
    tiny = SmallGather(small, slots, kept, pair, s_send, s_recv, pos)
    waves = [Gather(w, own, tiles, send, recv, pos) for w in range(2)]
    waves[0].start(0)
    tiny.start(0)
    waves[1].start(0)
    for t in range(TILES):
        tiles[t, pos["x"], pos["c"], pos["y"], pos["z"]] = own[t]
    for stage in range(3):
        waves[0].arrive(stage)
        tiny.arrive(stage)
        if stage < 2:
            waves[0].start(stage + 1)
            tiny.start(stage + 1)
        waves[1].arrive(stage)
        if stage < 2:
            waves[1].start(stage + 1)
    waves[0].arrive_pair()
    tiny.arrive_pair(params)
    unfold(tiles, 0, 3, w_qkv)
    waves[1].arrive_pair()
    unfold(tiles, 3, 1, w_out)
    unfold(tiles, 4, 4, w_up)
    unfold_plain(tiles, 8, 4, w_down)
    waves[0].settle()
    waves[1].settle()
    tiny.settle()


def gather_all(own, small):
    bf = jnp.bfloat16
    vmem = pl.BlockSpec(memory_space=pltpu.VMEM)
    dma = pltpu.SemaphoreType.DMA
    return pl.pallas_call(
        gather_kernel,
        out_shape=[
            jax.ShapeDtypeStruct((512, 1536), bf),
            jax.ShapeDtypeStruct((512, 512), bf),
            jax.ShapeDtypeStruct((512, 2048), bf),
            jax.ShapeDtypeStruct((2048, 512), bf),
            jax.ShapeDtypeStruct((32, 512), jnp.float32),
        ],
        in_specs=[vmem] * 2,
        out_specs=[vmem] * 5,
        scratch_shapes=[
            pltpu.VMEM((TILES, 4, 2, 4, 4, 16, 128), bf),
            pltpu.VMEM((2, 3, 32, 128), bf),
            pltpu.VMEM((4, 32, 128), bf),
            pltpu.VMEM((4, 32, 128), bf),
            dma((2, 3, 13)),
            dma((2, 3, 13)),
            dma((10,)),
            dma((10,)),
        ],
        compiler_params=pltpu.CompilerParams(collective_id=0, has_side_effects=True, vmem_limit_bytes=40 * 2**20),
    )(own, small)


def scatter_kernel(g_qkv, g_out, g_up, g_down, small, total, s_total, tiles, from_pair, from1, from2, from3, s_pair, slots, held, send, recv, s_send, s_recv):
    pos = my_position()
    greet(pos)
    waves = [Scatter(w, tiles, from_pair, from1, from2, from3, send, recv, pos) for w in range(2)]
    tiny = SmallScatter(small, s_pair, slots, held, s_send, s_recv, pos)
    fold(g_out, tiles, 3, 1)
    fold(g_up, tiles, 4, 4)
    fold_plain(g_down, tiles, 8, 4)
    for part in range(3):
        waves[1].start_pair(part)
    fold(g_qkv, tiles, 0, 3)
    for part in range(3):
        waves[0].start_pair(part)
    tiny.pair_copy().start()
    for w in (1, 0):
        for part in range(3):
            waves[w].add_pair(part)
            waves[w].start(part, 0)
    tiny.add_pair()
    tiny.start(0)
    for stage in range(3):
        for w in (1, 0):
            for part in range(3):
                waves[w].add(part, stage, total)
                if stage < 2:
                    waves[w].start(part, stage + 1)
        tiny.add(stage)
        if stage < 2:
            tiny.start(stage + 1)
    s_total[...] = held[6]
    waves[0].settle()
    waves[1].settle()
    tiny.settle()


def scatter_all(g_qkv, g_out, g_up, g_down, small):
    bf = jnp.bfloat16
    vmem = pl.BlockSpec(memory_space=pltpu.VMEM)
    dma = pltpu.SemaphoreType.DMA
    return pl.pallas_call(
        scatter_kernel,
        out_shape=[
            jax.ShapeDtypeStruct((TILES, 16, 128), jnp.float32),
            jax.ShapeDtypeStruct((32, 128), jnp.float32),
        ],
        in_specs=[vmem] * 5,
        out_specs=[vmem] * 2,
        scratch_shapes=[
            pltpu.VMEM((TILES, 4, 2, 4, 4, 16, 128), bf),
            pltpu.VMEM((TILES, 4, 4, 4, 16, 128), bf),
            pltpu.VMEM((TILES, 3, 4, 4, 16, 128), bf),
            pltpu.VMEM((TILES, 3, 4, 16, 128), bf),
            pltpu.VMEM((TILES, 3, 16, 128), bf),
            pltpu.VMEM((4, 32, 128), jnp.float32),
            pltpu.VMEM((3, 3, 32, 128), jnp.float32),
            pltpu.VMEM((7, 32, 128), jnp.float32),
            dma((2, 3, 10)),
            dma((2, 3, 10)),
            dma((10,)),
            dma((10,)),
        ],
        compiler_params=pltpu.CompilerParams(collective_id=1, has_side_effects=True, vmem_limit_bytes=50 * 2**20),
    )(g_qkv, g_out, g_up, g_down, small)


def product(left, right):
    return jnp.dot(left, right, preferred_element_type=jnp.float32)


def product_tn(left, right):
    return lax.dot_general(
        left, right, (((0,), (0,)), ((), ())), preferred_element_type=jnp.float32
    )


def product_nt(left, right):
    return lax.dot_general(
        left, right, (((1,), (1,)), ((), ())), preferred_element_type=jnp.float32
    )


def normalize(h, gain, shift):
    mean = jnp.mean(h, axis=-1, keepdims=True)
    centred = h - mean
    var = jnp.mean(centred * centred, axis=-1, keepdims=True)
    factor = lax.rsqrt(var + EPS)
    unit = centred * factor
    return (unit * gain + shift, unit, factor)


def normalize_back(grad, unit, factor, gain):
    scaled = grad * gain
    inner = jnp.mean(scaled, axis=-1, keepdims=True)
    along = jnp.mean(scaled * unit, axis=-1, keepdims=True)
    return (factor * (scaled - inner - unit * along), jnp.sum(grad * unit, 0), jnp.sum(grad, 0))


def scores_of(query, key, counts, scale):
    raw = jnp.einsum("alhe,amhe->ahlm", query, key, preferred_element_type=jnp.float32)
    scores = raw * scale
    slots = lax.broadcasted_iota(jnp.int32, (1, 1, 1, key.shape[1]), 3)
    valid = slots < counts[:, None, None, None]
    return jnp.where(valid, scores, -1000000000.0)


def body(
    latents,
    task_ids,
    slot_counts,
    cotangent,
    task_embed,
    norms,
    attn_in,
    attn_out,
    out_biases,
    mlp_in,
    mlp_in_bias,
    mlp_out,
):
    own = shard_tiles(attn_in, attn_out, mlp_in, mlp_out)
    small = shard_small(task_embed, norms, out_biases, mlp_in_bias)
    w_qkv, w_out, w_up, w_down, params = gather_all(own, small)
    table, gains, branch_bias = params[0:18].astype(jnp.bfloat16), params[18:22], params[22:24]
    up_bias = params[24:28].reshape(4, 4, 128).transpose(1, 0, 2).reshape(2048)
    arrays, length, width = latents.shape
    size_head = width // HEADS
    scale = 1.0 / math.sqrt(size_head)
    rows = arrays * length
    tasks = table.shape[0]
    onehot = (task_ids[:, None] == lax.broadcasted_iota(jnp.int32, (1, tasks), 1)).astype(
        jnp.bfloat16
    )
    offsets = product(onehot, table)
    flat0 = (latents.astype(jnp.float32) + offsets[:, None, :]).reshape(rows, width)
    norm1, unit1, factor1 = normalize(flat0, gains[0], gains[1])
    input1 = norm1.astype(jnp.bfloat16)
    joined = (
        product(input1, w_qkv).astype(jnp.bfloat16).reshape(arrays, length, 3, HEADS, size_head)
    )
    query, key, value = (joined[:, :, 0], joined[:, :, 1], joined[:, :, 2])
    scores = scores_of(query, key, slot_counts, scale)
    top = jnp.max(scores, axis=-1, keepdims=True)
    expo = jnp.exp(scores - top)
    total = jnp.sum(expo, axis=-1, keepdims=True)
    probs = (expo / total).astype(jnp.bfloat16)
    mixed = jnp.einsum("ahlm,amhe->alhe", probs, value, preferred_element_type=jnp.float32)
    mixed = mixed.astype(jnp.bfloat16).reshape(rows, width)
    flat1 = flat0 + (product(mixed, w_out) + branch_bias[0])
    norm2, unit2, factor2 = normalize(flat1, gains[2], gains[3])
    input2 = norm2.astype(jnp.bfloat16)
    hidden = product(input2, w_up) + up_bias
    active = jax.nn.gelu(hidden).astype(jnp.bfloat16)
    flat2 = flat1 + product(active, w_down) + branch_bias[1]
    result = flat2.astype(jnp.bfloat16).reshape(arrays, length, width)
    grad_out = cotangent.reshape(rows, width)
    grad_out_f = grad_out.astype(jnp.float32)
    grad_down = product_tn(active, grad_out)
    grad_tail = jnp.sum(grad_out_f, 0)
    grad_act = product_nt(grad_out, w_down)
    _, pull = jax.vjp(jax.nn.gelu, hidden)
    grad_hidden = pull(grad_act)[0].astype(jnp.bfloat16)
    grad_up = product_tn(input2, grad_hidden)
    grad_up_bias = jnp.sum(grad_hidden.astype(jnp.float32), 0)
    grad_input2 = product_nt(grad_hidden, w_up)
    back2, grad_gain2, grad_shift2 = normalize_back(grad_input2, unit2, factor2, gains[2])
    grad_flat1 = grad_out_f + back2
    grad_branch = grad_flat1.astype(jnp.bfloat16)
    grad_wout = product_tn(mixed, grad_branch)
    grad_head = jnp.sum(grad_branch.astype(jnp.float32), 0)
    grad_mixed = (
        product_nt(grad_branch, w_out)
        .astype(jnp.bfloat16)
        .reshape(arrays, length, HEADS, size_head)
    )
    scores = scores_of(query, key, slot_counts, scale)
    probs_f = jnp.exp(scores - top) / total
    grad_probs = jnp.einsum(
        "alhe,amhe->ahlm", grad_mixed, value, preferred_element_type=jnp.float32
    )
    delta = jnp.sum(probs_f * grad_probs, axis=-1, keepdims=True)
    grad_raw = (probs_f * (grad_probs - delta) * scale).astype(jnp.bfloat16)
    grad_query = jnp.einsum("ahlm,amhe->alhe", grad_raw, key, preferred_element_type=jnp.float32)
    grad_key = jnp.einsum("ahlm,alhe->amhe", grad_raw, query, preferred_element_type=jnp.float32)
    grad_value = jnp.einsum(
        "ahlm,alhe->amhe",
        probs_f.astype(jnp.bfloat16),
        grad_mixed,
        preferred_element_type=jnp.float32,
    )
    grad_joined = (
        jnp.stack((grad_query, grad_key, grad_value), 2)
        .astype(jnp.bfloat16)
        .reshape(rows, 3 * width)
    )
    grad_qkv = product_tn(input1, grad_joined)
    grad_input1 = product_nt(grad_joined, w_qkv)
    back1, grad_gain1, grad_shift1 = normalize_back(grad_input1, unit1, factor1, gains[0])
    grad_flat0 = grad_flat1 + back1
    grad_lat = grad_flat0.astype(jnp.bfloat16).reshape(arrays, length, width)
    per_array = jnp.sum(grad_flat0.reshape(arrays, length, width), 1)
    grad_table = lax.dot_general(
        onehot.astype(jnp.float32),
        per_array,
        (((0,), (0,)), ((), ())),
        precision=BEST,
        preferred_element_type=jnp.float32,
    )
    grad_norms = jnp.stack((grad_gain1, grad_shift1, grad_gain2, grad_shift2))
    grad_biases = jnp.stack((grad_head, grad_tail))
    up4 = grad_up_bias.reshape(4, 4, 128)
    rows24 = jnp.concatenate((grad_table, grad_norms, grad_biases)).reshape(24, 4, 128).transpose(1, 0, 2)
    small = jnp.concatenate((rows24, up4, jnp.zeros((4, 4, 128), jnp.float32)), 1)
    bf = jnp.bfloat16
    total, s_total = scatter_all(grad_qkv.astype(bf), grad_wout.astype(bf), grad_up.astype(bf), grad_down.astype(bf), small)
    s_qkv, s_out, s_up, s_down = own_weights(total)
    s_table, s_norms, s_biases, s_bias = own_small(s_total)
    return (result, grad_lat, s_table, s_norms, s_qkv, s_out, s_biases, s_up, s_bias, s_down)


def solution(mesh):
    in_specs = (
        P(("dp", "fsdp"), None, None),
        P(("dp", "fsdp")),
        P(("dp", "fsdp")),
        P(("dp", "fsdp"), None, None),
        P(None, ("dp", "fsdp")),
        P(None, ("dp", "fsdp")),
        P(("dp", "fsdp"), None),
        P(("dp", "fsdp"), None),
        P(None, ("dp", "fsdp")),
        P(("dp", "fsdp"), None),
        P(("dp", "fsdp")),
        P(("dp", "fsdp"), None),
    )
    out_specs = (
        P(("dp", "fsdp"), None, None),
        P(("dp", "fsdp"), None, None),
        P(None, ("dp", "fsdp")),
        P(None, ("dp", "fsdp")),
        P(("dp", "fsdp"), None),
        P(("dp", "fsdp"), None),
        P(None, ("dp", "fsdp")),
        P(("dp", "fsdp"), None),
        P(("dp", "fsdp")),
        P(("dp", "fsdp"), None),
    )
    return jax.shard_map(body, mesh=mesh, in_specs=in_specs, out_specs=out_specs, check_vma=False)
```

```python
import functools
import math

import jax
import jax.numpy as jnp
from jax import lax
from jax.experimental import pallas as pl
from jax.experimental.pallas import tpu as pltpu
from jax.sharding import PartitionSpec as P

HEADS = 8
EPS = 1e-05
BEST = lax.Precision.HIGHEST
MESH = pl.DeviceIdType.MESH
ALL = slice(None)
ORDERS = (("z", "y", "x"), ("y", "x", "z"), ("x", "z", "y"))
TILES = 12
WAVES = (((0, 1), (1, 1), (2, 1)), ((3, 3), (6, 3), (9, 3)))


def my_position():
    dp, fsdp = lax.axis_index("dp"), lax.axis_index("fsdp")
    return {
        "x": lax.div(dp, 2),
        "c": lax.rem(dp, 2),
        "y": lax.div(fsdp, 4),
        "z": lax.rem(fsdp, 4),
    }


def moved(pos, axis, step):
    size = 2 if axis == "c" else 4
    return {**pos, axis: lax.rem(pos[axis] + step, size)}


def device_of(pos):
    return (pos["x"] * 2 + pos["c"], pos["y"] * 4 + pos["z"])


def greet(pos):
    barrier = pltpu.get_barrier_semaphore()
    partners = [moved(pos, axis, k) for axis in "xyz" for k in (1, 2, 3)] + [moved(pos, "c", 1)]
    for other in partners:
        pl.semaphore_signal(barrier, inc=1, device_id=device_of(other), device_id_type=MESH)
    pl.semaphore_wait(barrier, len(partners))


def remote(src, dst, send, recv, pos):
    return pltpu.make_async_remote_copy(
        src_ref=src, dst_ref=dst, send_sem=send, recv_sem=recv,
        device_id=device_of(pos), device_id_type=MESH,
    )


class Gather:
    def __init__(self, wave, own, tiles, send, recv, pos):
        self.wave, self.own, self.tiles, self.pos = wave, own, tiles, pos
        self.send, self.recv = send, recv

    def slab(self, part, free, at=None):
        first, count = WAVES[self.wave][part]
        place = {**self.pos, **(at or {})}
        index = [ALL if axis in free else place[axis] for axis in "xcyz"]
        return self.tiles.at[(pl.ds(first, count), *index)]

    def stage_copy(self, part, stage, k):
        order = ORDERS[part]
        slab = self.slab(part, order[:stage])
        src = slab
        if stage == 0:
            first, count = WAVES[self.wave][part]
            src = self.own.at[pl.ds(first, count)]
        slot = (self.wave, part, stage * 3 + k - 1)
        return remote(src, slab, self.send.at[slot], self.recv.at[slot], moved(self.pos, order[stage], k))

    def pair_copy(self, part, k):
        order = ORDERS[part]
        at = {order[2]: lax.rem(self.pos[order[2]] + 4 - k, 4)} if k else None
        slab = self.slab(part, order[:2], at)
        slot = (self.wave, part, 9 + k)
        return remote(slab, slab, self.send.at[slot], self.recv.at[slot], moved(self.pos, "c", 1))

    def start(self, stage):
        for part in range(3):
            for k in (2, 1, 3):
                self.stage_copy(part, stage, k).start()
            if stage == 2:
                self.pair_copy(part, 0).start()

    def arrive(self, stage):
        for part in range(3):
            for k in (1, 3, 2):
                self.stage_copy(part, stage, k).wait_recv()
                if stage == 2:
                    self.pair_copy(part, k).start()

    def arrive_pair(self):
        for part in range(3):
            for k in range(4):
                self.pair_copy(part, k).wait_recv()

    def settle(self):
        for part in range(3):
            for stage in range(3):
                for k in (1, 2, 3):
                    self.stage_copy(part, stage, k).wait_send()
            for k in range(4):
                self.pair_copy(part, k).wait_send()


class SmallGather:
    def __init__(self, own, slots, kept, pair, send, recv, pos):
        self.own, self.slots, self.kept, self.pair = own, slots, kept, pair
        self.send, self.recv, self.pos = send, recv, pos

    def copy(self, stage, k):
        here = self.kept.at[self.pos["x"]]
        src = self.own if stage == 0 else here
        dst = here if stage == 2 else self.slots.at[stage, k - 1]
        slot = stage * 3 + k - 1
        return remote(src, dst, self.send.at[slot], self.recv.at[slot], moved(self.pos, "zyx"[stage], k))

    def pair_copy(self):
        return remote(self.kept, self.pair, self.send.at[9], self.recv.at[9], moved(self.pos, "c", 1))

    def start(self, stage):
        for k in (2, 1, 3):
            self.copy(stage, k).start()

    def arrive(self, stage):
        for k in (1, 3, 2):
            self.copy(stage, k).wait_recv()
        if stage == 2:
            self.pair_copy().start()
            return
        total = self.own[...] if stage == 0 else self.kept[self.pos["x"]]
        if stage == 1:
            for k in (1, 2, 3):
                self.copy(1, k).wait_send()
        for k in range(3):
            total = total + self.slots[stage, k]
        self.kept[self.pos["x"]] = total

    def arrive_pair(self, out):
        self.pair_copy().wait_recv()
        for x in range(4):
            out[:, x * 128 : (x + 1) * 128] = self.kept[x].astype(jnp.float32) + self.pair[x].astype(jnp.float32)

    def settle(self):
        for stage in (0, 2):
            for k in (1, 2, 3):
                self.copy(stage, k).wait_send()
        self.pair_copy().wait_send()


class Scatter:
    def __init__(self, wave, tiles, from_pair, from1, from2, from3, send, recv, pos):
        self.wave, self.tiles, self.pos = wave, tiles, pos
        self.from_pair, self.from_stage = from_pair, (from1, from2, from3)
        self.send, self.recv = send, recv

    def order(self, part):
        return ORDERS[part][::-1]

    def span(self, part):
        return WAVES[self.wave][part]

    def pair_copy(self, part):
        first, count = self.span(part)
        other = moved(self.pos, "c", 1)
        slot = (self.wave, part, 9)
        return remote(
            self.tiles.at[pl.ds(first, count), :, other["c"]], self.from_pair.at[pl.ds(first, count)],
            self.send.at[slot], self.recv.at[slot], other,
        )

    def index(self, part, stage, at=None):
        place = {**self.pos, **(at or {})}
        held = self.order(part)[: stage + 1]
        return tuple(place[axis] if axis in held or axis == "c" else ALL for axis in "xcyz")

    def stage_copy(self, part, stage, k):
        first, count = self.span(part)
        axis = self.order(part)[stage]
        other = moved(self.pos, axis, k)
        slot = (self.wave, part, stage * 3 + k - 1)
        src = self.tiles.at[(pl.ds(first, count), *self.index(part, stage, other))]
        dst = self.from_stage[stage].at[pl.ds(first, count), k - 1]
        return remote(src, dst, self.send.at[slot], self.recv.at[slot], other)

    def start_pair(self, part):
        self.pair_copy(part).start()

    def add_pair(self, part):
        first, count = self.span(part)
        self.pair_copy(part).wait_recv()
        core = self.pos["c"]

        def add(i, carry):
            t, x = first + lax.div(i, 4), lax.rem(i, 4)
            total = self.tiles[t, x, core].astype(jnp.float32) + self.from_pair[t, x].astype(jnp.float32)
            self.tiles[t, x, core] = total.astype(jnp.bfloat16)
            return carry

        lax.fori_loop(0, count * 4, add, 0)

    def start(self, part, stage):
        for k in (2, 1, 3):
            self.stage_copy(part, stage, k).start()

    def add(self, part, stage, out=None):
        first, count = self.span(part)
        for k in (1, 3, 2):
            self.stage_copy(part, stage, k).wait_recv()
        index = self.index(part, stage)

        def add(t):
            total = self.tiles[(t, *index)].astype(jnp.float32)
            for k in range(3):
                total = total + self.from_stage[stage][t, k].astype(jnp.float32)
            if stage == 2:
                out[t] = total
            else:
                self.tiles[(t, *index)] = total.astype(jnp.bfloat16)

        for t in range(first, first + count):
            add(t)

    def settle(self):
        for part in range(3):
            self.pair_copy(part).wait_send()
            for stage in range(3):
                for k in (1, 2, 3):
                    self.stage_copy(part, stage, k).wait_send()


class SmallScatter:
    def __init__(self, own, pair, slots, held, send, recv, pos):
        self.own, self.pair, self.slots, self.held = own, pair, slots, held
        self.send, self.recv, self.pos = send, recv, pos

    def pair_copy(self):
        return remote(self.own, self.pair, self.send.at[9], self.recv.at[9], moved(self.pos, "c", 1))

    def copy(self, stage, k):
        other = moved(self.pos, "xyz"[stage], k)
        src = self.held.at[other["x"]] if stage == 0 else self.held.at[3 + stage]
        slot = stage * 3 + k - 1
        return remote(src, self.slots.at[stage, k - 1], self.send.at[slot], self.recv.at[slot], other)

    def add_pair(self):
        self.pair_copy().wait_recv()
        self.held[0:4] = self.own[...] + self.pair[...]

    def start(self, stage):
        for k in (2, 1, 3):
            self.copy(stage, k).start()

    def add(self, stage):
        for k in (1, 3, 2):
            self.copy(stage, k).wait_recv()
        total = self.held[self.pos["x"]] if stage == 0 else self.held[3 + stage]
        for k in range(3):
            total = total + self.slots[stage, k]
        self.held[4 + stage] = total

    def settle(self):
        self.pair_copy().wait_send()
        for stage in range(3):
            for k in (1, 2, 3):
                self.copy(stage, k).wait_send()


def quarter_order(transposed=False):
    a = lax.broadcasted_iota(jnp.int32, (256, 256), 1 if transposed else 0)
    b = lax.broadcasted_iota(jnp.int32, (256, 256), 0 if transposed else 1)
    source = ((a % 64) // 4) * 16 + (a // 64) * 4 + a % 4
    return (source == b).astype(jnp.float32).astype(jnp.bfloat16)


def unfold(tiles, first, count, out):
    order = quarter_order()

    def one(i, carry):
        x, c = lax.div(i, 2), lax.rem(i, 2)
        blocks = [tiles[first + t, x, c].reshape(256, 128) for t in range(count)]
        rows = jnp.dot(order, jnp.concatenate(blocks, 1), preferred_element_type=jnp.float32).astype(jnp.bfloat16)
        for q in range(4):
            out[pl.ds(pl.multiple_of(i * 64, 64), 64), q * count * 128 : (q + 1) * count * 128] = rows[q * 64 : (q + 1) * 64]
        return carry

    lax.fori_loop(0, 8, one, 0)


def unfold_plain(tiles, first, count, out):
    def one(i, carry):
        x, c = lax.div(i, 2), lax.rem(i, 2)
        for t in range(count):
            out[pl.ds(pl.multiple_of(i * 256, 256), 256), t * 128 : (t + 1) * 128] = tiles[first + t, x, c].reshape(256, 128)
        return carry

    lax.fori_loop(0, 8, one, 0)


def fold(grad, tiles, first, count):
    order = quarter_order(True)

    def one(i, carry):
        x, c = lax.div(i, 2), lax.rem(i, 2)
        rows = [
            grad[pl.ds(pl.multiple_of(i * 64, 64), 64), q * count * 128 : (q + 1) * count * 128].astype(jnp.bfloat16)
            for q in range(4)
        ]
        blocks = jnp.dot(order, jnp.concatenate(rows, 0), preferred_element_type=jnp.float32).astype(jnp.bfloat16)
        for t in range(count):
            tiles[first + t, x, c] = blocks[:, t * 128 : (t + 1) * 128].reshape(4, 4, 16, 128)
        return carry

    lax.fori_loop(0, 8, one, 0)


def fold_plain(grad, tiles, first, count):
    def one(i, carry):
        x, c = lax.div(i, 2), lax.rem(i, 2)
        for t in range(count):
            block = grad[pl.ds(pl.multiple_of(i * 256, 256), 256), t * 128 : (t + 1) * 128]
            tiles[first + t, x, c] = block.astype(jnp.bfloat16).reshape(4, 4, 16, 128)
        return carry

    lax.fori_loop(0, 8, one, 0)


def shard_tiles(attn_in, attn_out, mlp_in, mlp_out):
    def quarters(w, count):
        return w.reshape(4, 4, count, 128).transpose(2, 1, 0, 3).reshape(count, 16, 128)

    return jnp.concatenate(
        (
            quarters(attn_in, 3),
            quarters(attn_out, 1),
            quarters(mlp_in, 4),
            mlp_out.reshape(16, 4, 128).transpose(1, 0, 2),
        )
    )


def shard_small(task_embed, norms, out_biases, mlp_in_bias):
    pos = my_position()
    ring = pos["y"] * 4 + pos["z"]
    block = jnp.zeros((32, 128), jnp.bfloat16)
    rows = jnp.concatenate((task_embed, norms, out_biases))
    block = lax.dynamic_update_slice(block, rows, (0, pos["c"] * 64 + ring * 4))
    at = (24 + pos["c"] * 2 + lax.div(ring, 8), 16 * lax.rem(ring, 8))
    return lax.dynamic_update_slice(block, mlp_in_bias[None, :], at)


def own_small(block):
    pos = my_position()
    ring = pos["y"] * 4 + pos["z"]
    columns = lax.dynamic_slice(block, (0, pos["c"] * 64 + ring * 4), (24, 4))
    at = (24 + pos["c"] * 2 + lax.div(ring, 8), 16 * lax.rem(ring, 8))
    bias = lax.dynamic_slice(block, at, (1, 16))[0]
    return columns[0:18], columns[18:22], columns[22:24], bias


def own_weights(total):
    def quarters(t, count):
        return t.reshape(count, 4, 4, 128).transpose(2, 1, 0, 3).reshape(4, 4 * count * 128)

    return quarters(total[0:3], 3), quarters(total[3:4], 1), quarters(total[4:8], 4), total[8:12].transpose(1, 0, 2).reshape(16, 512)


F32, BF16 = jnp.float32, jnp.bfloat16
GELU0 = math.sqrt(2.0 / math.pi)
GELU1 = GELU0 * 0.044715


def nn(a, b):
    return jnp.dot(a, b, preferred_element_type=F32)


def nt(a, b):
    return lax.dot_general(a, b, (((1,), (1,)), ((), ())), preferred_element_type=F32)


def tn(a, b):
    return lax.dot_general(a, b, (((0,), (0,)), ((), ())), preferred_element_type=F32)


def rows_of(i):
    return pl.ds(pl.multiple_of(i * 512, 512), 512)


def normalized(h):
    centred = h - jnp.mean(h, axis=-1, keepdims=True)
    factor = lax.rsqrt(jnp.mean(centred * centred, axis=-1, keepdims=True) + EPS)
    return centred * factor, factor


def normalized_back(grad, unit, factor, gain):
    scaled = grad * gain
    inner = jnp.mean(scaled, axis=-1, keepdims=True)
    along = jnp.mean(scaled * unit, axis=-1, keepdims=True)
    return factor * (scaled - inner - unit * along)


def column_sum(v):
    return jnp.sum(v, axis=0, keepdims=True)


def embedding(r, i):
    row = lax.broadcasted_iota(jnp.int32, (24, 1), 0)
    return column_sum(jnp.where(row == r.task_ids[i], r.params[0:24], 0.0))


def head_lanes(h):
    lane = lax.broadcasted_iota(jnp.int32, (1, 128), 1)
    return ((lane >= 64) == (h == 1)).astype(F32).astype(BF16)


def first_norm(r, i):
    unit, factor = normalized(r.lat[i].astype(F32) + embedding(r, i))
    a1 = (unit * r.params[18:19] + r.params[19:20]).astype(BF16)
    r.a1[rows_of(i)] = a1
    r.u1[rows_of(i)] = unit
    r.r1[rows_of(i)] = factor
    for part in range(3):
        columns = slice(part * 512, (part + 1) * 512)
        result = nn(a1, r.w_qkv[:, columns])
        if part == 0:
            result = result * 0.125
        r.qkv[rows_of(i), columns] = result.astype(BF16)


def pair_of(r, i, hp, part):
    return r.qkv[rows_of(i), pl.ds(pl.multiple_of(part * 512 + hp * 128, 128), 128)]


def attend(r, i, hp):
    q, k, v = (pair_of(r, i, hp, part) for part in range(3))
    slots = lax.broadcasted_iota(jnp.int32, (1, 512), 1)
    bias = jnp.where(slots < r.counts[i], 0.0, -1000000000.0)
    mixed = None
    for h in range(2):
        lanes = head_lanes(h)
        scores = nt(q, k * lanes) + bias
        expo = jnp.exp(scores - jnp.max(scores, axis=-1, keepdims=True)).astype(BF16)
        r.expo[i * 8 + hp * 2 + h] = expo
        wide = jnp.concatenate((v * lanes, jnp.broadcast_to(lanes, (512, 128))), 1)
        term = nn(expo, wide)
        mixed = term if mixed is None else mixed + term
    inverse = 1.0 / mixed[:, 128:]
    columns = pl.ds(pl.multiple_of(hp * 128, 128), 128)
    r.inverse[rows_of(i), columns] = inverse
    mean = mixed[:, :128] * inverse
    r.o32[rows_of(i), columns] = mean
    r.o[rows_of(i), columns] = mean.astype(BF16)


def second_norm(r, i):
    h1 = r.lat[i].astype(F32) + embedding(r, i) + (nn(r.o[rows_of(i)], r.w_out[...]) + r.params[22:23])
    unit, factor = normalized(h1)
    r.a2[rows_of(i)] = (unit * r.params[20:21] + r.params[21:22]).astype(BF16)
    r.u2[rows_of(i)] = unit
    r.r2[rows_of(i)] = factor
    r.result[rows_of(i)] = h1


def feed_forward(r, j):
    units = pl.ds(pl.multiple_of(j * 512, 512), 512)
    tile = pl.ds(pl.multiple_of(j * 128, 128), 128)
    bias = jnp.concatenate([r.params[24 + m : 25 + m, tile] for m in range(4)], 1)
    sums = None
    for i in range(2):
        z = nn(r.a2[rows_of(i)], r.w_up[:, units]) + bias
        z2 = z * z
        half = 0.5 + 0.5 * jnp.tanh(z * (GELU0 + GELU1 * z2))
        act = (z * half).astype(BF16)
        slope = half + z * (2 * GELU0 + 6 * GELU1 * z2) * (half * (1.0 - half))
        gz = (nt(r.y[i], r.w_down[units, :]) * slope).astype(BF16)
        r.act[rows_of(i)] = act
        r.gz[rows_of(i)] = gz
        down = nn(act, r.w_down[units, :])
        back = nt(gz, r.w_up[:, units])
        r.result[rows_of(i)] = r.result[rows_of(i)] + down

        @pl.when(j == 0)
        def _():
            r.back[rows_of(i)] = back

        @pl.when(j > 0)
        def _():
            r.back[rows_of(i)] = r.back[rows_of(i)] + back

        total = column_sum(gz.astype(F32))
        sums = total if sums is None else sums + total
    for m in range(4):
        r.small[j, 24 + m : 25 + m] = sums[:, m * 128 : (m + 1) * 128]
    g_down = tn(r.act[...], r.y[...].reshape(1024, 512)).astype(BF16)
    for c in range(2):
        for t in range(4):
            r.tiles[8 + t, j, c] = g_down[c * 256 : (c + 1) * 256, t * 128 : (t + 1) * 128].reshape(4, 4, 16, 128)
    r.g_up[:, units] = tn(r.a2[...], r.gz[...]).astype(BF16)


def add_small(r, row, value):
    for x in range(4):
        r.small[x, row : row + 1] = r.small[x, row : row + 1] + value[:, x * 128 : (x + 1) * 128]


def second_norm_back(r, i):
    grad, unit = r.back[rows_of(i)], r.u2[rows_of(i)]
    add_small(r, 20, column_sum(grad * unit))
    add_small(r, 21, column_sum(grad))
    y = r.y[i].astype(F32)
    add_small(r, 23, column_sum(y))
    gh1 = y + normalized_back(grad, unit, r.r2[rows_of(i)], r.params[20:21])
    r.back[rows_of(i)] = gh1
    gb = gh1.astype(BF16)
    r.gb[rows_of(i)] = gb
    add_small(r, 22, column_sum(gb.astype(F32)))
    go = (nt(gb, r.w_out[...]) * r.inverse[rows_of(i)]).astype(BF16)
    r.go[rows_of(i)] = go
    product = go.astype(F32) * r.o32[rows_of(i)]
    high = product.astype(BF16).astype(F32)
    low = product - high
    first = lax.broadcasted_iota(jnp.int32, (1, 128), 1) < 64
    for hp in range(4):
        columns = slice(hp * 128, (hp + 1) * 128)
        swapped = pltpu.roll(low[:, columns], 64, 1)
        r.god0[rows_of(i), columns] = jnp.where(first, high[:, columns], swapped).astype(BF16)
        r.god1[rows_of(i), columns] = jnp.where(first, swapped, high[:, columns]).astype(BF16)
    r.out[i] = (r.result[rows_of(i)] + r.params[23:24]).astype(BF16)


def out_gradient(r):
    r.g_out[...] = tn(r.o[...], r.gb[...]).astype(BF16)


def attend_back(r, i, hp):
    q, k, v = (pair_of(r, i, hp, part) for part in range(3))
    columns = pl.ds(pl.multiple_of(hp * 128, 128), 128)
    go = r.go[rows_of(i), columns]
    gq = gk = gv = 0.0
    for h in range(2):
        lanes = head_lanes(h)
        both = jnp.concatenate((go, (r.god0, r.god1)[h][rows_of(i), columns]), 1)
        wide = jnp.concatenate((v * lanes, jnp.full((512, 128), -1.0, BF16)), 1)
        expo = r.expo[i * 8 + hp * 2 + h]
        gs = (expo.astype(F32) * nt(both, wide)).astype(BF16)
        gq = gq + nn(gs, k * lanes)
        gk = gk + tn(gs, q * lanes)
        gv = gv + tn(expo, go * lanes)
    for part, value in enumerate((gq * 0.125, gk, gv)):
        r.qkv[rows_of(i), pl.ds(pl.multiple_of(part * 512 + hp * 128, 128), 128)] = value.astype(BF16)


def first_norm_back(r, i):
    grad, unit = nt(r.qkv[rows_of(i)], r.w_qkv[...]), r.u1[rows_of(i)]
    add_small(r, 18, column_sum(grad * unit))
    add_small(r, 19, column_sum(grad))
    gh0 = r.back[rows_of(i)] + normalized_back(grad, unit, r.r1[rows_of(i)], r.params[18:19])
    r.glat[i] = gh0.astype(BF16)
    total = column_sum(gh0)
    row = lax.broadcasted_iota(jnp.int32, (18, 1), 0)
    for x in range(4):
        mine = jnp.where(row == r.task_ids[i], total[:, x * 128 : (x + 1) * 128], 0.0)
        r.small[x, 0:18] = r.small[x, 0:18] + mine


def in_gradient(r):
    a1 = r.a1[...]
    for part in range(3):
        columns = slice(part * 512, (part + 1) * 512)
        r.g_qkv[:, columns] = tn(a1, r.qkv[:, columns]).astype(BF16)


class Refs:
    def __init__(self, names, refs):
        for name, ref in zip(names, refs, strict=True):
            setattr(self, name, ref)


INPUTS = ("task_ids", "counts", "lat_hbm", "y_hbm", "own", "own_small")
OUTPUTS = ("out_hbm", "glat_hbm", "total", "s_total")
BLOCKS = (TILES, 4, 2, 4, 4, 16, 128)
SCRATCH = {
    "lat": ((2, 512, 512), BF16),
    "y": ((2, 512, 512), BF16),
    "out": ((2, 512, 512), BF16),
    "w_qkv": ((512, 1536), BF16),
    "w_out": ((512, 512), BF16),
    "w_up": ((512, 2048), BF16),
    "w_down": ((2048, 512), BF16),
    "params": ((32, 512), F32),
    "a1": ((1024, 512), BF16),
    "u1": ((1024, 512), F32),
    "r1": ((1024, 1), F32),
    "qkv": ((1024, 1536), BF16),
    "expo": ((16, 512, 512), BF16),
    "o": ((1024, 512), BF16),
    "o32": ((1024, 512), F32),
    "inverse": ((1024, 512), F32),
    "result": ((1024, 512), F32),
    "a2": ((1024, 512), BF16),
    "u2": ((1024, 512), F32),
    "r2": ((1024, 1), F32),
    "act": ((1024, 512), BF16),
    "gz": ((1024, 512), BF16),
    "back": ((1024, 512), F32),
    "gb": ((1024, 512), BF16),
    "g_up": ((512, 2048), BF16),
    "g_qkv": ((512, 1536), BF16),
    "g_out": ((512, 512), BF16),
    "small": ((4, 32, 128), F32),
    "tiles": (BLOCKS, BF16),
    "slots": ((2, 3, 32, 128), BF16),
    "kept": ((4, 32, 128), BF16),
    "pair": ((4, 32, 128), BF16),
    "from_pair": ((TILES, 4, 4, 4, 16, 128), BF16),
    "from1": ((TILES, 3, 4, 4, 16, 128), BF16),
    "from2": ((TILES, 3, 4, 16, 128), BF16),
    "from3": ((TILES, 3, 16, 128), BF16),
    "s_pair": ((4, 32, 128), F32),
    "s_slots": ((3, 3, 32, 128), F32),
    "s_held": ((7, 32, 128), F32),
}
SEMAPHORES = {
    "g_send": (2, 3, 13),
    "g_recv": (2, 3, 13),
    "gs_send": (10,),
    "gs_recv": (10,),
    "r_send": (2, 3, 10),
    "r_recv": (2, 3, 10),
    "rs_send": (10,),
    "rs_recv": (10,),
    "local": (4,),
}


def kernel(*refs):
    r = Refs((*INPUTS, *OUTPUTS, *SCRATCH, *SEMAPHORES), refs)
    r.go, r.god0, r.god1, r.glat = r.act, r.gz, r.a2, r.y
    pos = my_position()
    load_lat = pltpu.make_async_copy(r.lat_hbm, r.lat, r.local.at[0])
    load_y = pltpu.make_async_copy(r.y_hbm, r.y, r.local.at[1])
    store_out = pltpu.make_async_copy(r.out, r.out_hbm, r.local.at[2])
    store_glat = pltpu.make_async_copy(r.glat, r.glat_hbm, r.local.at[3])
    load_lat.start()
    load_y.start()
    greet(pos)
    gathers = [Gather(w, r.own, r.tiles, r.g_send, r.g_recv, pos) for w in range(2)]
    tiny = SmallGather(r.own_small, r.slots, r.kept, r.pair, r.gs_send, r.gs_recv, pos)
    scatters = [
        Scatter(w, r.tiles, r.from_pair, r.from1, r.from2, r.from3, r.r_send, r.r_recv, pos) for w in range(2)
    ]
    tiny_sum = SmallScatter(r.small, r.s_pair, r.s_slots, r.s_held, r.rs_send, r.rs_recv, pos)

    gathers[0].start(0)
    tiny.start(0)
    gathers[1].start(0)
    for t in range(TILES):
        r.tiles[t, pos["x"], pos["c"], pos["y"], pos["z"]] = r.own[t]
    r.small[...] = jnp.zeros_like(r.small)
    for stage in range(3):
        gathers[0].arrive(stage)
        if stage < 2:
            gathers[0].start(stage + 1)
        tiny.arrive(stage)
        if stage < 2:
            tiny.start(stage + 1)
    gathers[1].arrive(0)
    gathers[1].start(1)
    tiny.arrive_pair(r.params)
    gathers[0].arrive_pair()
    unfold(r.tiles, 0, 3, r.w_qkv)
    load_lat.wait()
    lax.fori_loop(0, 2, lambda i, n: (first_norm(r, i), n)[1], 0)
    gathers[1].arrive(1)
    gathers[1].start(2)

    def forward(n, carry):
        attend(r, lax.div(n, 4), lax.rem(n, 4))
        return carry

    lax.fori_loop(0, 4, forward, 0)
    gathers[1].arrive(2)
    lax.fori_loop(4, 8, forward, 0)
    gathers[1].arrive_pair()
    unfold(r.tiles, 3, 1, r.w_out)
    unfold(r.tiles, 4, 4, r.w_up)
    unfold_plain(r.tiles, 8, 4, r.w_down)
    gathers[0].settle()
    gathers[1].settle()
    tiny.settle()
    lax.fori_loop(0, 2, lambda i, n: (second_norm(r, i), n)[1], 0)
    load_y.wait()
    lax.fori_loop(0, 4, lambda j, n: (feed_forward(r, j), n)[1], 0)
    fold(r.g_up, r.tiles, 4, 4)
    for part in (1, 2):
        scatters[1].start_pair(part)
    lax.fori_loop(0, 2, lambda i, n: (second_norm_back(r, i), n)[1], 0)
    store_out.start()
    out_gradient(r)
    fold(r.g_out, r.tiles, 3, 1)
    scatters[1].start_pair(0)
    for part in (1, 2):
        scatters[1].add_pair(part)
        scatters[1].start(part, 0)

    def backward(n, carry):
        attend_back(r, lax.div(n, 4), lax.rem(n, 4))

        @pl.when(n == 0)
        def _():
            scatters[1].add_pair(0)
            scatters[1].start(0, 0)

        @pl.when(n == 4)
        def _():
            for part in (1, 2, 0):
                scatters[1].add(part, 0)
                scatters[1].start(part, 1)

        @pl.when(n == 6)
        def _():
            for part in (1, 2, 0):
                scatters[1].add(part, 1)
                scatters[1].start(part, 2)

        return carry

    lax.fori_loop(0, 8, backward, 0)
    in_gradient(r)
    fold(r.g_qkv, r.tiles, 0, 3)
    for part in range(3):
        scatters[0].start_pair(part)
    for part in range(3):
        scatters[1].add(part, 2, r.total)
    lax.fori_loop(0, 2, lambda i, n: (first_norm_back(r, i), n)[1], 0)
    tiny_sum.pair_copy().start()
    store_glat.start()
    for part in range(3):
        scatters[0].add_pair(part)
        scatters[0].start(part, 0)
    tiny_sum.add_pair()
    tiny_sum.start(0)
    for stage in range(3):
        for part in range(3):
            scatters[0].add(part, stage, r.total)
            if stage < 2:
                scatters[0].start(part, stage + 1)
        tiny_sum.add(stage)
        if stage < 2:
            tiny_sum.start(stage + 1)
    r.s_total[...] = r.s_held[6]
    scatters[0].settle()
    scatters[1].settle()
    tiny_sum.settle()
    store_out.wait()
    store_glat.wait()


def whole(task_ids, counts, latents, cotangent, own, small):
    vmem = pl.BlockSpec(memory_space=pltpu.VMEM)
    smem = pl.BlockSpec(memory_space=pltpu.SMEM)
    hbm = pl.BlockSpec(memory_space=pl.ANY)
    array = jax.ShapeDtypeStruct(latents.shape, BF16)
    return pl.pallas_call(
        kernel,
        out_shape=[
            array,
            array,
            jax.ShapeDtypeStruct((TILES, 16, 128), F32),
            jax.ShapeDtypeStruct((32, 128), F32),
        ],
        in_specs=[smem, smem, hbm, hbm, vmem, vmem],
        out_specs=[hbm, hbm, vmem, vmem],
        scratch_shapes=[pltpu.VMEM(shape, dtype) for shape, dtype in SCRATCH.values()]
        + [pltpu.SemaphoreType.DMA(shape) for shape in SEMAPHORES.values()],
        compiler_params=pltpu.CompilerParams(
            collective_id=0, has_side_effects=True, vmem_limit_bytes=60 * 2**20
        ),
    )(task_ids, counts, latents, cotangent, own, small)


def body(
    latents,
    task_ids,
    slot_counts,
    cotangent,
    task_embed,
    norms,
    attn_in,
    attn_out,
    out_biases,
    mlp_in,
    mlp_in_bias,
    mlp_out,
):
    own = shard_tiles(attn_in, attn_out, mlp_in, mlp_out)
    small = shard_small(task_embed, norms, out_biases, mlp_in_bias)
    result, grad_lat, total, s_total = whole(task_ids, slot_counts, latents, cotangent, own, small)
    s_qkv, s_out, s_up, s_down = own_weights(total)
    s_table, s_norms, s_biases, s_bias = own_small(s_total)
    return (result, grad_lat, s_table, s_norms, s_qkv, s_out, s_biases, s_up, s_bias, s_down)


def solution(mesh):
    in_specs = (
        P(("dp", "fsdp"), None, None),
        P(("dp", "fsdp")),
        P(("dp", "fsdp")),
        P(("dp", "fsdp"), None, None),
        P(None, ("dp", "fsdp")),
        P(None, ("dp", "fsdp")),
        P(("dp", "fsdp"), None),
        P(("dp", "fsdp"), None),
        P(None, ("dp", "fsdp")),
        P(("dp", "fsdp"), None),
        P(("dp", "fsdp")),
        P(("dp", "fsdp"), None),
    )
    out_specs = (
        P(("dp", "fsdp"), None, None),
        P(("dp", "fsdp"), None, None),
        P(None, ("dp", "fsdp")),
        P(None, ("dp", "fsdp")),
        P(("dp", "fsdp"), None),
        P(("dp", "fsdp"), None),
        P(None, ("dp", "fsdp")),
        P(("dp", "fsdp"), None),
        P(("dp", "fsdp")),
        P(("dp", "fsdp"), None),
    )
    return jax.shard_map(body, mesh=mesh, in_specs=in_specs, out_specs=out_specs, check_vma=False)
```

```python
import functools
import math

import jax
import jax.numpy as jnp
from jax import lax
from jax.experimental import pallas as pl
from jax.experimental.pallas import tpu as pltpu
from jax.sharding import PartitionSpec as P

HEADS = 8
EPS = 1e-05
BEST = lax.Precision.HIGHEST
MESH = pl.DeviceIdType.MESH
ALL = slice(None)
ORDERS = (("z", "y", "x"), ("y", "x", "z"), ("x", "z", "y"))
TILES = 12
WAVES = (((0, 1), (1, 1), (2, 1)), ((3, 3), (6, 3), (9, 3)))


def my_position():
    dp, fsdp = lax.axis_index("dp"), lax.axis_index("fsdp")
    return {
        "x": lax.div(dp, 2),
        "c": lax.rem(dp, 2),
        "y": lax.div(fsdp, 4),
        "z": lax.rem(fsdp, 4),
    }


def moved(pos, axis, step):
    size = 2 if axis == "c" else 4
    return {**pos, axis: lax.rem(pos[axis] + step, size)}


def device_of(pos):
    return (pos["x"] * 2 + pos["c"], pos["y"] * 4 + pos["z"])


def partners_of(pos):
    return [moved(pos, axis, k) for axis in "xyz" for k in (1, 2, 3)] + [moved(pos, "c", 1)]


def greet(pos):
    barrier = pltpu.get_barrier_semaphore()
    for other in partners_of(pos):
        pl.semaphore_signal(barrier, inc=1, device_id=device_of(other), device_id_type=MESH)


def greeted(pos):
    pl.semaphore_wait(pltpu.get_barrier_semaphore(), 10)


def remote(src, dst, send, recv, pos):
    return pltpu.make_async_remote_copy(
        src_ref=src, dst_ref=dst, send_sem=send, recv_sem=recv,
        device_id=device_of(pos), device_id_type=MESH,
    )


class Gather:
    def __init__(self, wave, own, tiles, send, recv, pos):
        self.wave, self.own, self.tiles, self.pos = wave, own, tiles, pos
        self.send, self.recv = send, recv

    def slab(self, part, free, at=None):
        first, count = WAVES[self.wave][part]
        place = {**self.pos, **(at or {})}
        index = [ALL if axis in free else place[axis] for axis in "xcyz"]
        return self.tiles.at[(pl.ds(first, count), *index)]

    def stage_copy(self, part, stage, k):
        order = ORDERS[part]
        slab = self.slab(part, order[:stage])
        src = slab
        if stage == 0:
            first, count = WAVES[self.wave][part]
            src = self.own.at[pl.ds(first, count)]
        slot = (self.wave, part, stage * 3 + k - 1)
        return remote(src, slab, self.send.at[slot], self.recv.at[slot], moved(self.pos, order[stage], k))

    def pair_copy(self, part, k):
        order = ORDERS[part]
        at = {order[2]: lax.rem(self.pos[order[2]] + 4 - k, 4)} if k else None
        slab = self.slab(part, order[:2], at)
        slot = (self.wave, part, 9 + k)
        return remote(slab, slab, self.send.at[slot], self.recv.at[slot], moved(self.pos, "c", 1))

    def start(self, stage):
        for part in range(3):
            for k in (2, 1, 3):
                self.stage_copy(part, stage, k).start()
            if stage == 2:
                self.pair_copy(part, 0).start()

    def arrive(self, stage):
        for part in range(3):
            for k in (1, 3, 2):
                self.stage_copy(part, stage, k).wait_recv()
                if stage == 2:
                    self.pair_copy(part, k).start()

    def arrive_pair(self, part):
        for k in range(4):
            self.pair_copy(part, k).wait_recv()

    def settle(self):
        for part in range(3):
            for stage in range(3):
                for k in (1, 2, 3):
                    self.stage_copy(part, stage, k).wait_send()
            for k in range(4):
                self.pair_copy(part, k).wait_send()


class SmallGather:
    def __init__(self, own, slots, kept, pair, send, recv, pos):
        self.own, self.slots, self.kept, self.pair = own, slots, kept, pair
        self.send, self.recv, self.pos = send, recv, pos

    def copy(self, stage, k):
        here = self.kept.at[self.pos["x"]]
        src = self.own if stage == 0 else here
        dst = here if stage == 2 else self.slots.at[stage, k - 1]
        slot = stage * 3 + k - 1
        return remote(src, dst, self.send.at[slot], self.recv.at[slot], moved(self.pos, "zyx"[stage], k))

    def pair_copy(self):
        return remote(self.kept, self.pair, self.send.at[9], self.recv.at[9], moved(self.pos, "c", 1))

    def start(self, stage):
        for k in (2, 1, 3):
            self.copy(stage, k).start()

    def arrive(self, stage):
        for k in (1, 3, 2):
            self.copy(stage, k).wait_recv()
        if stage == 2:
            self.pair_copy().start()
            return
        total = self.own[...] if stage == 0 else self.kept[self.pos["x"]]
        if stage == 1:
            for k in (1, 2, 3):
                self.copy(1, k).wait_send()
        for k in range(3):
            total = total + self.slots[stage, k]
        self.kept[self.pos["x"]] = total

    def arrive_pair(self, out):
        self.pair_copy().wait_recv()
        for x in range(4):
            out[:, x * 128 : (x + 1) * 128] = self.kept[x].astype(jnp.float32) + self.pair[x].astype(jnp.float32)

    def settle(self):
        for stage in (0, 2):
            for k in (1, 2, 3):
                self.copy(stage, k).wait_send()
        self.pair_copy().wait_send()


class Scatter:
    def __init__(self, wave, tiles, from1, from2, from3, send, recv, pos):
        self.wave, self.tiles, self.pos = wave, tiles, pos
        self.from_stage = (from1, from2, from3)
        self.send, self.recv = send, recv

    def order(self, part):
        return ORDERS[part][::-1]

    def span(self, part):
        return WAVES[self.wave][part]

    def index(self, part, stage, at=None):
        place = {**self.pos, **(at or {})}
        held = self.order(part)[: stage + 1]
        return tuple(place[axis] if axis in held or axis == "c" else ALL for axis in "xcyz")

    def stage_copy(self, part, stage, k):
        first, count = self.span(part)
        axis = self.order(part)[stage]
        other = moved(self.pos, axis, k)
        slot = (self.wave, part, stage * 3 + k - 1)
        src = self.tiles.at[(pl.ds(first, count), *self.index(part, stage, other))]
        dst = self.from_stage[stage].at[pl.ds(first, count), k - 1]
        return remote(src, dst, self.send.at[slot], self.recv.at[slot], other)

    def start(self, part, stage):
        for k in (2, 1, 3):
            self.stage_copy(part, stage, k).start()

    def add(self, part, stage, out=None):
        first, count = self.span(part)
        for k in (1, 3, 2):
            self.stage_copy(part, stage, k).wait_recv()
        index = self.index(part, stage)

        def add(t):
            total = self.tiles[(t, *index)].astype(jnp.float32)
            for k in range(3):
                total = total + self.from_stage[stage][t, k].astype(jnp.float32)
            if stage == 2:
                out[t] = total
            else:
                self.tiles[(t, *index)] = total.astype(jnp.bfloat16)

        for t in range(first, first + count):
            add(t)

    def settle(self):
        for part in range(3):
            for stage in range(3):
                for k in (1, 2, 3):
                    self.stage_copy(part, stage, k).wait_send()


class PairSum:
    def __init__(self, tiles, from_pair, send, recv, pos):
        self.tiles, self.from_pair, self.send, self.recv, self.pos = tiles, from_pair, send, recv, pos

    def tile(self, t):
        other = moved(self.pos, "c", 1)
        return remote(self.tiles.at[t, :, other["c"]], self.from_pair.at[t], self.send.at[t], self.recv.at[t], other)

    def down(self, j):
        other = moved(self.pos, "c", 1)
        return remote(
            self.tiles.at[pl.ds(8, 4), j, other["c"]], self.from_pair.at[pl.ds(8, 4), j],
            self.send.at[8 + j], self.recv.at[8 + j], other,
        )

    def add(self, t, x):
        core = self.pos["c"]
        total = self.tiles[t, x, core].astype(jnp.float32) + self.from_pair[t, x].astype(jnp.float32)
        self.tiles[t, x, core] = total.astype(jnp.bfloat16)

    def add_tile(self, t):
        self.tile(t).wait_recv()
        for x in range(4):
            self.add(t, x)

    def add_down(self, j):
        self.down(j).wait_recv()
        for t in range(8, 12):
            self.add(t, j)

    def settle(self):
        for t in range(8):
            self.tile(t).wait_send()
        for j in range(4):
            self.down(j).wait_send()


class SmallScatter:
    def __init__(self, own, pair, slots, held, send, recv, pos):
        self.own, self.pair, self.slots, self.held = own, pair, slots, held
        self.send, self.recv, self.pos = send, recv, pos

    def pair_copy(self):
        return remote(self.own, self.pair, self.send.at[9], self.recv.at[9], moved(self.pos, "c", 1))

    def copy(self, stage, k):
        other = moved(self.pos, "xyz"[stage], k)
        src = self.held.at[other["x"]] if stage == 0 else self.held.at[3 + stage]
        slot = stage * 3 + k - 1
        return remote(src, self.slots.at[stage, k - 1], self.send.at[slot], self.recv.at[slot], other)

    def add_pair(self):
        self.pair_copy().wait_recv()
        self.held[0:4] = self.own[...] + self.pair[...]

    def start(self, stage):
        for k in (2, 1, 3):
            self.copy(stage, k).start()

    def add(self, stage):
        for k in (1, 3, 2):
            self.copy(stage, k).wait_recv()
        total = self.held[self.pos["x"]] if stage == 0 else self.held[3 + stage]
        for k in range(3):
            total = total + self.slots[stage, k]
        self.held[4 + stage] = total

    def settle(self):
        self.pair_copy().wait_send()
        for stage in range(3):
            for k in (1, 2, 3):
                self.copy(stage, k).wait_send()


COLUMNS = (
    (0, 4, 8, 1),
    (5, 9, 2, 6),
    (10, 3, 7, 11),
    (0, 1, 2, 3),
    *(tuple(range(4 * j, 4 * j + 4)) for j in range(4)),
)


def quarter_order(transposed=False):
    a = lax.broadcasted_iota(jnp.int32, (256, 256), 1 if transposed else 0)
    b = lax.broadcasted_iota(jnp.int32, (256, 256), 0 if transposed else 1)
    source = ((a % 64) // 4) * 16 + (a // 64) * 4 + a % 4
    return (source == b).astype(jnp.float32).astype(jnp.bfloat16)


def unfold(r, t, out):
    blocks = [r.tiles[t, xc // 2, xc % 2].reshape(256, 128) for xc in range(8)]
    rows = nn(quarter_order(), jnp.concatenate(blocks, 1)).astype(jnp.bfloat16)
    for q, ct in enumerate(COLUMNS[t]):
        for xc in range(8):
            out[xc * 64 : (xc + 1) * 64, ct * 128 : (ct + 1) * 128] = rows[q * 64 : (q + 1) * 64, xc * 128 : (xc + 1) * 128]


def unfold_plain(r, out):
    def one(i):
        x, c = lax.div(i, 2), lax.rem(i, 2)
        for t in range(4):
            out[pl.ds(pl.multiple_of(i * 256, 256), 256), t * 128 : (t + 1) * 128] = r.tiles[8 + t, x, c].reshape(256, 128)

    loop(8, one)


def fold(r, columns, t):
    rows = [jnp.concatenate([block[xc * 64 : (xc + 1) * 64] for xc in range(8)], 1) for block in columns]
    blocks = nn(quarter_order(True), jnp.concatenate(rows, 0)).astype(jnp.bfloat16)
    for xc in range(8):
        r.tiles[t, xc // 2, xc % 2] = blocks[:, xc * 128 : (xc + 1) * 128].reshape(4, 4, 16, 128)


def small_place(pos):
    ring = pos["y"] * 4 + pos["z"]
    return pos["c"] * 64 + ring * 4, 24 + pos["c"] * 2 + lax.div(ring, 8), 16 * lax.rem(ring, 8)


F32, BF16 = jnp.float32, jnp.bfloat16
GELU0 = math.sqrt(2.0 / math.pi)
GELU1 = GELU0 * 0.044715


def nn(a, b):
    return jnp.dot(a, b, preferred_element_type=F32)


def nt(a, b):
    return lax.dot_general(a, b, (((1,), (1,)), ((), ())), preferred_element_type=F32)


def tn(a, b):
    return lax.dot_general(a, b, (((0,), (0,)), ((), ())), preferred_element_type=F32)


def rows_of(i):
    return pl.ds(pl.multiple_of(i * 512, 512), 512)


def normalized(h):
    centred = h - jnp.mean(h, axis=-1, keepdims=True)
    factor = lax.rsqrt(jnp.mean(centred * centred, axis=-1, keepdims=True) + EPS)
    return centred * factor, factor


def normalized_back(grad, unit, factor, gain):
    scaled = grad * gain
    inner = jnp.mean(scaled, axis=-1, keepdims=True)
    along = jnp.mean(scaled * unit, axis=-1, keepdims=True)
    return factor * (scaled - inner - unit * along)


def column_sum(v):
    return jnp.sum(v, axis=0, keepdims=True)


def embedding(r, i):
    row = lax.broadcasted_iota(jnp.int32, (24, 1), 0)
    return column_sum(jnp.where(row == r.task_ids[i], r.params[0:24], 0.0))


def head_lanes(h):
    lane = lax.broadcasted_iota(jnp.int32, (1, 128), 1)
    return ((lane >= 64) == (h == 1)).astype(F32).astype(BF16)


def first_norm(r, i):
    unit, factor = normalized(r.lat[i].astype(F32) + embedding(r, i))
    a1 = (unit * r.params[18:19] + r.params[19:20]).astype(BF16)
    r.a1[rows_of(i)] = a1
    r.u1[rows_of(i)] = unit
    r.r1[rows_of(i)] = factor
    for part in range(3):
        columns = slice(part * 512, (part + 1) * 512)
        result = nn(a1, r.w_qkv[:, columns])
        if part == 0:
            result = result * 0.125
        r.qkv[rows_of(i), columns] = result.astype(BF16)


def pair_of(r, i, hp, part):
    return r.qkv[rows_of(i), pl.ds(pl.multiple_of(part * 512 + hp * 128, 128), 128)]


def attend(r, i, hp):
    q, k, v = (pair_of(r, i, hp, part) for part in range(3))
    slots = lax.broadcasted_iota(jnp.int32, (1, 512), 1)
    bias = jnp.where(slots < r.counts[i], 0.0, -1000000000.0)
    mixed = None
    for h in range(2):
        lanes = head_lanes(h)
        scores = nt(q, k * lanes) + bias
        expo = jnp.exp(scores - jnp.max(scores, axis=-1, keepdims=True)).astype(BF16)
        r.expo[i * 8 + hp * 2 + h] = expo
        wide = jnp.concatenate((v * lanes, jnp.broadcast_to(lanes, (512, 128))), 1)
        term = nn(expo, wide)
        mixed = term if mixed is None else mixed + term
    inverse = 1.0 / mixed[:, 128:]
    columns = pl.ds(pl.multiple_of(hp * 128, 128), 128)
    r.inverse[rows_of(i), columns] = inverse
    mean = mixed[:, :128] * inverse
    r.o32[rows_of(i), columns] = mean
    r.o[rows_of(i), columns] = mean.astype(BF16)


def second_norm(r, i):
    h1 = r.lat[i].astype(F32) + embedding(r, i) + (nn(r.o[rows_of(i)], r.w_out[...]) + r.params[22:23])
    unit, factor = normalized(h1)
    r.a2[rows_of(i)] = (unit * r.params[20:21] + r.params[21:22]).astype(BF16)
    r.u2[rows_of(i)] = unit
    r.r2[rows_of(i)] = factor
    r.result[rows_of(i)] = h1


def feed_forward(r, j):
    units = pl.ds(pl.multiple_of(j * 512, 512), 512)
    tile = pl.ds(pl.multiple_of(j * 128, 128), 128)
    bias = jnp.concatenate([r.params[24 + m : 25 + m, tile] for m in range(4)], 1)
    sums = None
    for i in range(2):
        z = nn(r.a2[rows_of(i)], r.w_up[:, units]) + bias
        z2 = z * z
        half = 0.5 + 0.5 * jnp.tanh(z * (GELU0 + GELU1 * z2))
        act = (z * half).astype(BF16)
        slope = half + z * (2 * GELU0 + 6 * GELU1 * z2) * (half * (1.0 - half))
        gz = (nt(r.y[i], r.w_down[units, :]) * slope).astype(BF16)
        r.act[rows_of(i), units] = act
        r.gz[rows_of(i)] = gz
        back = nt(gz, r.w_up[:, units])

        @pl.when(j == 0)
        def _():
            r.back[rows_of(i)] = back

        @pl.when(j > 0)
        def _():
            r.back[rows_of(i)] = r.back[rows_of(i)] + back

        total = column_sum(gz.astype(F32))
        sums = total if sums is None else sums + total
    for m in range(4):
        r.small[j, 24 + m : 25 + m] = sums[:, m * 128 : (m + 1) * 128]
    g_down = tn(r.act[:, units], r.y[...].reshape(1024, 512)).astype(BF16)
    for c in range(2):
        for t in range(4):
            r.tiles[8 + t, j, c] = g_down[c * 256 : (c + 1) * 256, t * 128 : (t + 1) * 128].reshape(4, 4, 16, 128)
    g_up = tn(r.a2[...], r.gz[...]).astype(BF16)
    fold(r, [g_up[:, q * 128 : (q + 1) * 128] for q in range(4)], 4 + j)


def add_small(r, row, value):
    for x in range(4):
        r.small[x, row : row + 1] = r.small[x, row : row + 1] + value[:, x * 128 : (x + 1) * 128]


def second_norm_back(r, i):
    grad, unit = r.back[rows_of(i)], r.u2[rows_of(i)]
    add_small(r, 20, column_sum(grad * unit))
    add_small(r, 21, column_sum(grad))
    y = r.y[i].astype(F32)
    add_small(r, 23, column_sum(y))
    gh1 = y + normalized_back(grad, unit, r.r2[rows_of(i)], r.params[20:21])
    r.back[rows_of(i)] = gh1
    gb = gh1.astype(BF16)
    r.gb[rows_of(i)] = gb
    add_small(r, 22, column_sum(gb.astype(F32)))
    go = (nt(gb, r.w_out[...]) * r.inverse[rows_of(i)]).astype(BF16)
    r.go[rows_of(i)] = go
    product = go.astype(F32) * r.o32[rows_of(i)]
    high = product.astype(BF16).astype(F32)
    low = product - high
    first = lax.broadcasted_iota(jnp.int32, (1, 128), 1) < 64
    for hp in range(4):
        columns = slice(hp * 128, (hp + 1) * 128)
        swapped = pltpu.roll(low[:, columns], 64, 1)
        r.god0[rows_of(i), columns] = jnp.where(first, high[:, columns], swapped).astype(BF16)
        r.god1[rows_of(i), columns] = jnp.where(first, swapped, high[:, columns]).astype(BF16)


def out_gradient(r):
    g_out = tn(r.o[...], r.gb[...]).astype(BF16)
    fold(r, [g_out[:, q * 128 : (q + 1) * 128] for q in range(4)], 3)


def result_of(r, i):
    r.out[i] = (r.result[rows_of(i)] + nn(r.act[rows_of(i)], r.w_down[...]) + r.params[23:24]).astype(BF16)


def attend_back(r, i, hp):
    q, k, v = (pair_of(r, i, hp, part) for part in range(3))
    columns = pl.ds(pl.multiple_of(hp * 128, 128), 128)
    go = r.go[rows_of(i), columns]
    gq = gk = gv = 0.0
    for h in range(2):
        lanes = head_lanes(h)
        both = jnp.concatenate((go, (r.god0, r.god1)[h][rows_of(i), columns]), 1)
        wide = jnp.concatenate((v * lanes, jnp.full((512, 128), -1.0, BF16)), 1)
        expo = r.expo[i * 8 + hp * 2 + h]
        gs = (expo.astype(F32) * nt(both, wide)).astype(BF16)
        gq = gq + nn(gs, k * lanes)
        gk = gk + tn(gs, q * lanes)
        gv = gv + tn(expo, go * lanes)
    for part, value in enumerate((gq * 0.125, gk, gv)):
        r.qkv[rows_of(i), pl.ds(pl.multiple_of(part * 512 + hp * 128, 128), 128)] = value.astype(BF16)


def first_norm_back(r, i):
    grad, unit = nt(r.qkv[rows_of(i)], r.w_qkv[...]), r.u1[rows_of(i)]
    add_small(r, 18, column_sum(grad * unit))
    add_small(r, 19, column_sum(grad))
    gh0 = r.back[rows_of(i)] + normalized_back(grad, unit, r.r1[rows_of(i)], r.params[18:19])
    r.glat[i] = gh0.astype(BF16)
    total = column_sum(gh0)
    row = lax.broadcasted_iota(jnp.int32, (18, 1), 0)
    for x in range(4):
        mine = jnp.where(row == r.task_ids[i], total[:, x * 128 : (x + 1) * 128], 0.0)
        r.small[x, 0:18] = r.small[x, 0:18] + mine


def in_gradient(r, t):
    columns = jnp.concatenate([r.qkv[:, ct * 128 : (ct + 1) * 128] for ct in COLUMNS[t]], 1)
    g_in = tn(r.a1[...], columns).astype(BF16)
    fold(r, [g_in[:, q * 128 : (q + 1) * 128] for q in range(4)], t)


class Refs:
    def __init__(self, names, refs):
        for name, ref in zip(names, refs, strict=True):
            setattr(self, name, ref)


RAW = {
    "raw_in": ((4, 1536), BF16),
    "raw_out": ((4, 512), BF16),
    "raw_up": ((4, 2048), BF16),
    "raw_down": ((16, 512), BF16),
    "raw_table": ((18, 4), BF16),
    "raw_norms": ((4, 4), BF16),
    "raw_biases": ((2, 4), BF16),
    "raw_up_bias": ((1, 16), BF16),
}
INPUTS = ("task_ids", "counts", "lat_hbm", "y_hbm", *(f"{name}_hbm" for name in RAW))
OUTPUTS = ("out_hbm", "glat_hbm", "total", "s_total")
BLOCKS = (TILES, 4, 2, 4, 4, 16, 128)
SCRATCH = {
    **RAW,
    "own32": ((TILES, 16, 128), F32),
    "own": ((TILES, 16, 128), BF16),
    "small32": ((40, 128), F32),
    "own_small": ((32, 128), BF16),
    "lat": ((2, 512, 512), BF16),
    "y": ((2, 512, 512), BF16),
    "out": ((2, 512, 512), BF16),
    "w_qkv": ((512, 1536), BF16),
    "w_out": ((512, 512), BF16),
    "w_up": ((512, 2048), BF16),
    "w_down": ((2048, 512), BF16),
    "params": ((32, 512), F32),
    "a1": ((1024, 512), BF16),
    "u1": ((1024, 512), F32),
    "r1": ((1024, 1), F32),
    "qkv": ((1024, 1536), BF16),
    "expo": ((16, 512, 512), BF16),
    "o": ((1024, 512), BF16),
    "o32": ((1024, 512), F32),
    "inverse": ((1024, 512), F32),
    "result": ((1024, 512), F32),
    "a2": ((1024, 512), BF16),
    "u2": ((1024, 512), F32),
    "r2": ((1024, 1), F32),
    "act": ((1024, 2048), BF16),
    "gz": ((1024, 512), BF16),
    "god0": ((1024, 512), BF16),
    "back": ((1024, 512), F32),
    "gb": ((1024, 512), BF16),
    "small": ((4, 32, 128), F32),
    "tiles": (BLOCKS, BF16),
    "slots": ((2, 3, 32, 128), BF16),
    "kept": ((4, 32, 128), BF16),
    "pair": ((4, 32, 128), BF16),
    "from_pair": ((TILES, 4, 4, 4, 16, 128), BF16),
    "from1": ((TILES, 3, 4, 4, 16, 128), BF16),
    "from2": ((TILES, 3, 4, 16, 128), BF16),
    "from3": ((TILES, 3, 16, 128), BF16),
    "s_pair": ((4, 32, 128), F32),
    "s_slots": ((3, 3, 32, 128), F32),
    "s_held": ((7, 32, 128), F32),
}
SEMAPHORES = {
    "g_send": (2, 3, 13),
    "g_recv": (2, 3, 13),
    "gs_send": (10,),
    "gs_recv": (10,),
    "p_send": (12,),
    "p_recv": (12,),
    "r_send": (2, 3, 9),
    "r_recv": (2, 3, 9),
    "rs_send": (10,),
    "rs_recv": (10,),
    "local": (12,),
}


def alias(r):
    r.go, r.god1, r.glat = r.gz, r.a2, r.y


def loop(count, step):
    lax.fori_loop(0, count, lambda n, carry: (step(n), carry)[1], 0)


def pack_own(r, pos):
    for t, blocks in enumerate(COLUMNS):
        raw = (r.raw_in, r.raw_out, r.raw_up)[0 if t < 3 else 1 if t == 3 else 2]
        for q, ct in enumerate(blocks):
            r.own32[t, 4 * q : 4 * q + 4] = raw[:, ct * 128 : (ct + 1) * 128].astype(F32)
    for t in range(8):
        r.own[t] = r.own32[t].astype(BF16)
    for t in range(4):
        r.own[8 + t] = r.raw_down[:, t * 128 : (t + 1) * 128]
    r.small32[...] = jnp.zeros_like(r.small32)
    r.small32[0:18, 0:4] = r.raw_table[...].astype(F32)
    r.small32[18:22, 0:4] = r.raw_norms[...].astype(F32)
    r.small32[22:24, 0:4] = r.raw_biases[...].astype(F32)
    r.small32[32:33, 0:16] = r.raw_up_bias[...].astype(F32)
    offset, bias_row, bias_offset = small_place(pos)
    block = pltpu.roll(r.small32[0:32], offset, 1)
    bias = pltpu.roll(r.small32[32:40], bias_offset, 1)[0:1]
    row = lax.broadcasted_iota(jnp.int32, (32, 1), 0)
    r.own_small[...] = (block + jnp.where(row == bias_row, bias, 0.0)).astype(BF16)


def kernel(*refs):
    r = Refs((*INPUTS, *OUTPUTS, *SCRATCH, *SEMAPHORES), refs)
    alias(r)
    pos = my_position()
    loads = [
        pltpu.make_async_copy(getattr(r, f"{name}_hbm"), getattr(r, name), r.local.at[n])
        for n, name in enumerate((*RAW, "lat", "y"))
    ]
    store_out = pltpu.make_async_copy(r.out, r.out_hbm, r.local.at[10])
    store_glat = pltpu.make_async_copy(r.glat, r.glat_hbm, r.local.at[11])
    greet(pos)
    for load in loads:
        load.start()
    gathers = [Gather(w, r.own, r.tiles, r.g_send, r.g_recv, pos) for w in range(2)]
    tiny = SmallGather(r.own_small, r.slots, r.kept, r.pair, r.gs_send, r.gs_recv, pos)
    pairs = PairSum(r.tiles, r.from_pair, r.p_send, r.p_recv, pos)
    scatters = [Scatter(w, r.tiles, r.from1, r.from2, r.from3, r.r_send, r.r_recv, pos) for w in range(2)]
    tiny_sum = SmallScatter(r.small, r.s_pair, r.s_slots, r.s_held, r.rs_send, r.rs_recv, pos)
    for load in loads[:8]:
        load.wait()
    pack_own(r, pos)
    greeted(pos)

    gathers[0].start(0)
    tiny.start(0)
    for t in range(TILES):
        r.tiles[t, pos["x"], pos["c"], pos["y"], pos["z"]] = r.own[t]
    r.small[...] = jnp.zeros_like(r.small)
    for stage in range(3):
        gathers[0].arrive(stage)
        if stage < 2:
            gathers[0].start(stage + 1)
        tiny.arrive(stage)
        if stage < 2:
            tiny.start(stage + 1)
        if stage == 0:
            gathers[1].start(0)
    gathers[1].arrive(0)
    gathers[1].start(1)
    tiny.arrive_pair(r.params)
    for t in range(3):
        gathers[0].arrive_pair(t)
        unfold(r, t, r.w_qkv)
    loads[8].wait()
    loop(2, lambda i: first_norm(r, i))
    gathers[1].arrive(1)
    gathers[1].start(2)

    def forward(n):
        attend(r, lax.div(n, 4), lax.rem(n, 4))

        @pl.when(n == 6)
        def _():
            gathers[1].arrive(2)

    loop(8, forward)
    gathers[1].arrive_pair(0)
    unfold(r, 3, r.w_out)
    loop(2, lambda i: second_norm(r, i))
    unfold(r, 4, r.w_up)
    unfold(r, 5, r.w_up)
    for part in (1, 2):
        gathers[1].arrive_pair(part)
    unfold(r, 6, r.w_up)
    unfold(r, 7, r.w_up)
    unfold_plain(r, r.w_down)
    gathers[0].settle()
    gathers[1].settle()
    tiny.settle()
    loads[9].wait()

    def middle(j):
        feed_forward(r, j)
        pairs.tile(4 + j).start()
        pairs.down(j).start()

        @pl.when(j > 0)
        def _():
            pairs.add_tile(3 + j)
            pairs.add_down(j - 1)

    loop(4, middle)
    second_norm_back(r, 0)
    pairs.add_tile(7)
    pairs.add_down(3)
    for part in (1, 2):
        scatters[1].start(part, 0)
    second_norm_back(r, 1)
    out_gradient(r)
    pairs.tile(3).start()

    def backward(n):
        attend_back(r, lax.rem(n, 2), lax.div(n, 2))

        @pl.when(n == 0)
        def _():
            pairs.add_tile(3)
            scatters[1].start(0, 0)

        @pl.when(n == 3)
        def _():
            in_gradient(r, 0)
            pairs.tile(0).start()

        @pl.when(n == 4)
        def _():
            pairs.add_tile(0)
            scatters[0].start(0, 0)

        @pl.when(n == 5)
        def _():
            in_gradient(r, 1)
            pairs.tile(1).start()
            for part in (1, 2):
                scatters[1].add(part, 0)
                scatters[1].start(part, 1)

        @pl.when(n == 6)
        def _():
            pairs.add_tile(1)
            scatters[0].start(1, 0)
            scatters[1].add(0, 0)
            scatters[1].start(0, 1)
            scatters[0].add(0, 0)
            scatters[0].start(0, 1)

    loop(8, backward)
    in_gradient(r, 2)
    pairs.tile(2).start()
    for part in (1, 2):
        scatters[1].add(part, 1)
        scatters[1].start(part, 2)
    first_norm_back(r, 0)
    pairs.add_tile(2)
    scatters[0].start(2, 0)
    first_norm_back(r, 1)
    tiny_sum.pair_copy().start()
    store_glat.start()
    scatters[1].add(0, 1)
    scatters[1].start(0, 2)
    for part in (0, 1):
        scatters[0].add(part, 1 - part)
        scatters[0].start(part, 2 - part)
    tiny_sum.add_pair()
    tiny_sum.start(0)
    result_of(r, 0)
    scatters[0].add(2, 0)
    scatters[0].start(2, 1)
    result_of(r, 1)
    store_out.start()
    tiny_sum.add(0)
    tiny_sum.start(1)
    scatters[0].add(2, 1)
    scatters[0].start(2, 2)
    scatters[0].add(1, 1)
    scatters[0].start(1, 2)
    for part in (1, 2, 0):
        scatters[1].add(part, 2, r.total)
    tiny_sum.add(1)
    tiny_sum.start(2)
    for part in range(3):
        scatters[0].add(part, 2, r.total)
    scatters[0].settle()
    scatters[1].settle()
    pairs.settle()
    store_out.wait()
    store_glat.wait()
    tiny_sum.add(2)
    r.s_total[...] = r.s_held[6]
    tiny_sum.settle()


def finish(*refs):
    out_in, glat_in, total, small, out, glat, *rest = refs
    table, norms, w_in, w_out, biases, w_up, up_bias, w_down, held, sems = rest
    reads, writes = [], []
    for n, (source, target) in enumerate(((out_in, out), (glat_in, glat))):
        for i in range(2):
            slot = 2 * n + i
            reads.append(pltpu.make_async_copy(source.at[i], held.at[slot], sems.at[0, slot]))
            writes.append(pltpu.make_async_copy(held.at[slot], target.at[i], sems.at[1, slot]))
    for read in reads:
        read.start()
    for t, blocks in enumerate(COLUMNS):
        to = (w_in, w_out, w_up)[0 if t < 3 else 1 if t == 3 else 2]
        for q, ct in enumerate(blocks):
            to[:, ct * 128 : (ct + 1) * 128] = total[t, 4 * q : 4 * q + 4]
    for t in range(4):
        w_down[:, t * 128 : (t + 1) * 128] = total[8 + t]
    offset, bias_row, bias_offset = small_place(my_position())
    block = pltpu.roll(small[...], lax.rem(128 - offset, 128), 1)
    table[...] = block[0:18, 0:4]
    norms[...] = block[18:22, 0:4]
    biases[...] = block[22:24, 0:4]
    row = lax.broadcasted_iota(jnp.int32, (32, 1), 0)
    bias = jnp.sum(jnp.where(row == bias_row, small[...], 0.0), axis=0, keepdims=True)
    bias = pltpu.roll(jnp.broadcast_to(bias, (8, 128)), lax.rem(128 - bias_offset, 128), 1)
    up_bias[...] = bias[0:1, 0:16]
    for read, write in zip(reads, writes, strict=True):
        read.wait()
        write.start()
    for write in writes:
        write.wait()


def whole(task_ids, counts, latents, cotangent, *raw):
    vmem = pl.BlockSpec(memory_space=pltpu.VMEM)
    smem = pl.BlockSpec(memory_space=pltpu.SMEM)
    hbm = pl.BlockSpec(memory_space=pl.ANY)
    array = jax.ShapeDtypeStruct(latents.shape, BF16)
    found = pl.pallas_call(
        kernel,
        out_shape=[
            array,
            array,
            jax.ShapeDtypeStruct((TILES, 16, 128), F32),
            jax.ShapeDtypeStruct((32, 128), F32),
        ],
        in_specs=[smem, smem] + [hbm] * (2 + len(RAW)),
        out_specs=[hbm, hbm, vmem, vmem],
        scratch_shapes=[pltpu.VMEM(shape, dtype) for shape, dtype in SCRATCH.values()]
        + [pltpu.SemaphoreType.DMA(shape) for shape in SEMAPHORES.values()],
        compiler_params=pltpu.CompilerParams(
            collective_id=0, has_side_effects=True, vmem_limit_bytes=60 * 2**20
        ),
    )(task_ids, counts, latents, cotangent, *raw)
    shapes = ((18, 4), (4, 4), (4, 1536), (4, 512), (2, 4), (4, 2048), (1, 16), (16, 512))
    return pl.pallas_call(
        finish,
        out_shape=[array, array] + [jax.ShapeDtypeStruct(shape, F32) for shape in shapes],
        in_specs=[hbm, hbm, vmem, vmem],
        out_specs=[hbm, hbm] + [vmem] * 8,
        scratch_shapes=[pltpu.VMEM((4, 512, 512), BF16), pltpu.SemaphoreType.DMA((2, 4))],
    )(*found)


def body(
    latents,
    task_ids,
    slot_counts,
    cotangent,
    task_embed,
    norms,
    attn_in,
    attn_out,
    out_biases,
    mlp_in,
    mlp_in_bias,
    mlp_out,
):
    raw = (attn_in, attn_out, mlp_in, mlp_out, task_embed, norms, out_biases, mlp_in_bias.reshape(1, 16))
    found = list(whole(task_ids, slot_counts, latents, cotangent, *raw))
    found[8] = found[8].reshape(16)
    return tuple(found)


def solution(mesh):
    in_specs = (
        P(("dp", "fsdp"), None, None),
        P(("dp", "fsdp")),
        P(("dp", "fsdp")),
        P(("dp", "fsdp"), None, None),
        P(None, ("dp", "fsdp")),
        P(None, ("dp", "fsdp")),
        P(("dp", "fsdp"), None),
        P(("dp", "fsdp"), None),
        P(None, ("dp", "fsdp")),
        P(("dp", "fsdp"), None),
        P(("dp", "fsdp")),
        P(("dp", "fsdp"), None),
    )
    out_specs = (
        P(("dp", "fsdp"), None, None),
        P(("dp", "fsdp"), None, None),
        P(None, ("dp", "fsdp")),
        P(None, ("dp", "fsdp")),
        P(("dp", "fsdp"), None),
        P(("dp", "fsdp"), None),
        P(None, ("dp", "fsdp")),
        P(("dp", "fsdp"), None),
        P(("dp", "fsdp")),
        P(("dp", "fsdp"), None),
    )
    return jax.shard_map(body, mesh=mesh, in_specs=in_specs, out_specs=out_specs, check_vma=False)
```

```python
import functools
import math

import jax
import jax.numpy as jnp
from jax import lax
from jax.experimental import pallas as pl
from jax.experimental.pallas import tpu as pltpu
from jax.sharding import PartitionSpec as P

HEADS = 8
EPS = 1e-05
BEST = lax.Precision.HIGHEST
MESH = pl.DeviceIdType.MESH
ALL = slice(None)
ORDERS = (("z", "y", "x"), ("y", "x", "z"), ("x", "z", "y"))
TILES = 12
WAVES = (((0, 1), (1, 1), (2, 1)), ((3, 3), (6, 3), (9, 3)))


def my_position():
    dp, fsdp = lax.axis_index("dp"), lax.axis_index("fsdp")
    return {
        "x": lax.div(dp, 2),
        "c": lax.rem(dp, 2),
        "y": lax.div(fsdp, 4),
        "z": lax.rem(fsdp, 4),
    }


def moved(pos, axis, step):
    size = 2 if axis == "c" else 4
    return {**pos, axis: lax.rem(pos[axis] + step, size)}


def device_of(pos):
    return (pos["x"] * 2 + pos["c"], pos["y"] * 4 + pos["z"])


def partners_of(pos):
    return [moved(pos, axis, k) for axis in "xyz" for k in (1, 2, 3)] + [moved(pos, "c", 1)]


def greet(pos):
    barrier = pltpu.get_barrier_semaphore()
    for other in partners_of(pos):
        pl.semaphore_signal(barrier, inc=1, device_id=device_of(other), device_id_type=MESH)


def greeted(pos):
    pl.semaphore_wait(pltpu.get_barrier_semaphore(), 10)


def remote(src, dst, send, recv, pos):
    return pltpu.make_async_remote_copy(
        src_ref=src, dst_ref=dst, send_sem=send, recv_sem=recv,
        device_id=device_of(pos), device_id_type=MESH,
    )


class Gather:
    def __init__(self, wave, own, tiles, send, recv, pos):
        self.wave, self.own, self.tiles, self.pos = wave, own, tiles, pos
        self.send, self.recv = send, recv

    def slab(self, part, free, at=None):
        first, count = WAVES[self.wave][part]
        place = {**self.pos, **(at or {})}
        index = [ALL if axis in free else place[axis] for axis in "xcyz"]
        return self.tiles.at[(pl.ds(first, count), *index)]

    def stage_copy(self, part, stage, k):
        order = ORDERS[part]
        slab = self.slab(part, order[:stage])
        src = slab
        if stage == 0:
            first, count = WAVES[self.wave][part]
            src = self.own.at[pl.ds(first, count)]
        slot = (self.wave, part, stage * 3 + k - 1)
        return remote(src, slab, self.send.at[slot], self.recv.at[slot], moved(self.pos, order[stage], k))

    def pair_copy(self, part, k):
        order = ORDERS[part]
        at = {order[2]: lax.rem(self.pos[order[2]] + 4 - k, 4)} if k else None
        slab = self.slab(part, order[:2], at)
        slot = (self.wave, part, 9 + k)
        return remote(slab, slab, self.send.at[slot], self.recv.at[slot], moved(self.pos, "c", 1))

    def start(self, stage):
        for part in range(3):
            for k in (2, 1, 3):
                self.stage_copy(part, stage, k).start()
            if stage == 2:
                self.pair_copy(part, 0).start()

    def arrive(self, stage):
        for part in range(3):
            for k in (1, 3, 2):
                self.stage_copy(part, stage, k).wait_recv()
                if stage == 2:
                    self.pair_copy(part, k).start()

    def arrive_pair(self, part):
        for k in range(4):
            self.pair_copy(part, k).wait_recv()

    def settle(self):
        for part in range(3):
            for stage in range(3):
                for k in (1, 2, 3):
                    self.stage_copy(part, stage, k).wait_send()
            for k in range(4):
                self.pair_copy(part, k).wait_send()


class SmallGather:
    def __init__(self, own, slots, kept, pair, send, recv, pos):
        self.own, self.slots, self.kept, self.pair = own, slots, kept, pair
        self.send, self.recv, self.pos = send, recv, pos

    def copy(self, stage, k):
        here = self.kept.at[self.pos["x"]]
        src = self.own if stage == 0 else here
        dst = here if stage == 2 else self.slots.at[stage, k - 1]
        slot = stage * 3 + k - 1
        return remote(src, dst, self.send.at[slot], self.recv.at[slot], moved(self.pos, "zyx"[stage], k))

    def pair_copy(self):
        return remote(self.kept, self.pair, self.send.at[9], self.recv.at[9], moved(self.pos, "c", 1))

    def start(self, stage):
        for k in (2, 1, 3):
            self.copy(stage, k).start()

    def arrive(self, stage):
        for k in (1, 3, 2):
            self.copy(stage, k).wait_recv()
        if stage == 2:
            self.pair_copy().start()
            return
        total = self.own[...] if stage == 0 else self.kept[self.pos["x"]]
        if stage == 1:
            for k in (1, 2, 3):
                self.copy(1, k).wait_send()
        for k in range(3):
            total = total + self.slots[stage, k]
        self.kept[self.pos["x"]] = total

    def arrive_pair(self, out):
        self.pair_copy().wait_recv()
        for x in range(4):
            out[:, x * 128 : (x + 1) * 128] = self.kept[x].astype(jnp.float32) + self.pair[x].astype(jnp.float32)

    def settle(self):
        for stage in (0, 2):
            for k in (1, 2, 3):
                self.copy(stage, k).wait_send()
        self.pair_copy().wait_send()


class Piece:
    def __init__(self, r, pos, number, first, count, order, x=None, stages=(0, 1, 2)):
        self.r, self.pos, self.number, self.first, self.count = r, pos, number, first, count
        self.order, self.x, self.stages = order, x, stages
        self.paired = False

    def span(self):
        return pl.ds(self.first, self.count)

    def pair_copy(self):
        other = moved(self.pos, "c", 1)
        x = ALL if self.x is None else self.x
        self.paired = True
        return remote(
            self.r.tiles.at[self.span(), x, other["c"]], self.r.from_pair.at[self.span(), x],
            self.r.p_send.at[self.number], self.r.p_recv.at[self.number], other,
        )

    def pair_add(self):
        self.pair_copy().wait_recv()
        core = self.pos["c"]
        for t in range(self.first, self.first + self.count):
            for x in range(4) if self.x is None else (self.x,):
                total = self.r.tiles[t, x, core].astype(jnp.float32) + self.r.from_pair[t, x].astype(jnp.float32)
                self.r.tiles[t, x, core] = total.astype(jnp.bfloat16)

    def index(self, stage, place):
        held = self.order[: stage + 1]
        found = []
        for axis in "xcyz":
            if axis == "c" or axis in held:
                found.append(place[axis])
            else:
                found.append(self.x if axis == "x" and self.x is not None else ALL)
        return tuple(found)

    def left(self, stage):
        free = [axis for axis in "xyz" if axis not in self.order[: stage + 1]]
        return tuple(self.x if axis == "x" and self.x is not None else ALL for axis in free)

    def copy(self, stage, k):
        axis = self.order[stage]
        other = moved(self.pos, axis, k)
        src = self.r.tiles.at[(self.span(), *self.index(stage, other))]
        dst = (self.r.from1, self.r.from2, self.r.from3)[stage].at[(self.span(), k - 1, *self.left(stage))]
        slot = (self.number, stage * 3 + k - 1)
        return remote(src, dst, self.r.r_send.at[slot], self.r.r_recv.at[slot], other)

    def start(self, stage):
        for k in (2, 1, 3):
            self.copy(stage, k).start()

    def add(self, stage):
        for k in (1, 3, 2):
            self.copy(stage, k).wait_recv()
        index, left = self.index(stage, self.pos), self.left(stage)
        arrived = (self.r.from1, self.r.from2, self.r.from3)[stage]
        for t in range(self.first, self.first + self.count):
            total = self.r.tiles[(t, *index)].astype(jnp.float32)
            for k in range(3):
                total = total + arrived[(t, k, *left)].astype(jnp.float32)
            if stage == 2:
                self.r.total[t] = total
            else:
                self.r.tiles[(t, *index)] = total.astype(jnp.bfloat16)

    def settle(self):
        if self.paired:
            self.pair_copy().wait_send()
        for stage in self.stages:
            for k in (1, 2, 3):
                self.copy(stage, k).wait_send()


class SmallScatter:
    def __init__(self, own, pair, slots, held, send, recv, pos):
        self.own, self.pair, self.slots, self.held = own, pair, slots, held
        self.send, self.recv, self.pos = send, recv, pos

    def pair_copy(self):
        return remote(self.own, self.pair, self.send.at[9], self.recv.at[9], moved(self.pos, "c", 1))

    def copy(self, stage, k):
        other = moved(self.pos, "xyz"[stage], k)
        src = self.held.at[other["x"]] if stage == 0 else self.held.at[3 + stage]
        slot = stage * 3 + k - 1
        return remote(src, self.slots.at[stage, k - 1], self.send.at[slot], self.recv.at[slot], other)

    def add_pair(self):
        self.pair_copy().wait_recv()
        self.held[0:4] = self.own[...] + self.pair[...]

    def start(self, stage):
        for k in (2, 1, 3):
            self.copy(stage, k).start()

    def add(self, stage):
        for k in (1, 3, 2):
            self.copy(stage, k).wait_recv()
        total = self.held[self.pos["x"]] if stage == 0 else self.held[3 + stage]
        for k in range(3):
            total = total + self.slots[stage, k]
        self.held[4 + stage] = total

    def settle(self):
        self.pair_copy().wait_send()
        for stage in range(3):
            for k in (1, 2, 3):
                self.copy(stage, k).wait_send()


COLUMNS = (
    (0, 4, 8, 1),
    (5, 9, 2, 6),
    (10, 3, 7, 11),
    (0, 1, 2, 3),
    *(tuple(range(4 * j, 4 * j + 4)) for j in range(4)),
)


def quarter_order(transposed=False):
    a = lax.broadcasted_iota(jnp.int32, (256, 256), 1 if transposed else 0)
    b = lax.broadcasted_iota(jnp.int32, (256, 256), 0 if transposed else 1)
    source = ((a % 64) // 4) * 16 + (a // 64) * 4 + a % 4
    return (source == b).astype(jnp.float32).astype(jnp.bfloat16)


def unfold(r, t, out):
    blocks = [r.tiles[t, xc // 2, xc % 2].reshape(256, 128) for xc in range(8)]
    rows = nn(quarter_order(), jnp.concatenate(blocks, 1)).astype(jnp.bfloat16)
    for q, ct in enumerate(COLUMNS[t]):
        for xc in range(8):
            out[xc * 64 : (xc + 1) * 64, ct * 128 : (ct + 1) * 128] = rows[q * 64 : (q + 1) * 64, xc * 128 : (xc + 1) * 128]


def unfold_plain(r, out):
    def one(i):
        x, c = lax.div(i, 2), lax.rem(i, 2)
        for t in range(4):
            out[pl.ds(pl.multiple_of(i * 256, 256), 256), t * 128 : (t + 1) * 128] = r.tiles[8 + t, x, c].reshape(256, 128)

    loop(8, one)


def fold(r, columns, t):
    rows = [jnp.concatenate([block[xc * 64 : (xc + 1) * 64] for xc in range(8)], 1) for block in columns]
    blocks = nn(quarter_order(True), jnp.concatenate(rows, 0)).astype(jnp.bfloat16)
    for xc in range(8):
        r.tiles[t, xc // 2, xc % 2] = blocks[:, xc * 128 : (xc + 1) * 128].reshape(4, 4, 16, 128)


def small_place(pos):
    ring = pos["y"] * 4 + pos["z"]
    return pos["c"] * 64 + ring * 4, 24 + pos["c"] * 2 + lax.div(ring, 8), 16 * lax.rem(ring, 8)


F32, BF16 = jnp.float32, jnp.bfloat16
GELU0 = math.sqrt(2.0 / math.pi)
GELU1 = GELU0 * 0.044715


def nn(a, b):
    return jnp.dot(a, b, preferred_element_type=F32)


def nt(a, b):
    return lax.dot_general(a, b, (((1,), (1,)), ((), ())), preferred_element_type=F32)


def tn(a, b):
    return lax.dot_general(a, b, (((0,), (0,)), ((), ())), preferred_element_type=F32)


def rows_of(i):
    return slice(i * 512, (i + 1) * 512)


def normalized(h):
    centred = h - jnp.mean(h, axis=-1, keepdims=True)
    factor = lax.rsqrt(jnp.mean(centred * centred, axis=-1, keepdims=True) + EPS)
    return centred * factor, factor


def normalized_back(grad, unit, factor, gain):
    scaled = grad * gain
    inner = jnp.mean(scaled, axis=-1, keepdims=True)
    along = jnp.mean(scaled * unit, axis=-1, keepdims=True)
    return factor * (scaled - inner - unit * along)


def column_sum(v):
    return jnp.sum(v, axis=0, keepdims=True)


def embedding(r, i):
    row = lax.broadcasted_iota(jnp.int32, (24, 1), 0)
    return column_sum(jnp.where(row == r.task_ids[i], r.params[0:24], 0.0))


def head_lanes(h):
    lane = lax.broadcasted_iota(jnp.int32, (1, 128), 1)
    return ((lane >= 64) == (h == 1)).astype(F32).astype(BF16)


def first_norm(r, i):
    unit, factor = normalized(r.lat[i].astype(F32) + embedding(r, i))
    r.a1[rows_of(i)] = (unit * r.params[18:19] + r.params[19:20]).astype(BF16)
    r.u1[rows_of(i)] = unit
    r.r1[rows_of(i)] = factor


def project(r, i):
    a1 = r.a1[rows_of(i)]
    for part in range(3):
        columns = slice(part * 512, (part + 1) * 512)
        result = nn(a1, r.w_qkv[:, columns])
        if part == 0:
            result = result * 0.125
        r.qkv[rows_of(i), columns] = result.astype(BF16)


def pair_of(r, i, hp, part):
    return r.qkv[rows_of(i), part * 512 + hp * 128 : part * 512 + (hp + 1) * 128]


def attend(r, i, hp):
    q, k, v = (pair_of(r, i, hp, part) for part in range(3))
    slots = lax.broadcasted_iota(jnp.int32, (1, 512), 1)
    bias = jnp.where(slots < r.counts[i], 0.0, -1000000000.0)
    mixed = None
    for h in range(2):
        lanes = head_lanes(h)
        scores = nt(q, k * lanes) + bias
        expo = jnp.exp(scores - jnp.max(scores, axis=-1, keepdims=True)).astype(BF16)
        r.expo[i * 8 + hp * 2 + h] = expo
        wide = jnp.concatenate((v * lanes, jnp.broadcast_to(lanes, (512, 128))), 1)
        term = nn(expo, wide)
        mixed = term if mixed is None else mixed + term
    inverse = 1.0 / mixed[:, 128:]
    columns = slice(hp * 128, (hp + 1) * 128)
    r.inverse[rows_of(i), columns] = inverse
    mean = mixed[:, :128] * inverse
    r.o32[rows_of(i), columns] = mean
    r.o[rows_of(i), columns] = mean.astype(BF16)


def second_norm(r, i):
    h1 = r.lat[i].astype(F32) + embedding(r, i) + (nn(r.o[rows_of(i)], r.w_out[...]) + r.params[22:23])
    unit, factor = normalized(h1)
    r.a2[rows_of(i)] = (unit * r.params[20:21] + r.params[21:22]).astype(BF16)
    r.u2[rows_of(i)] = unit
    r.r2[rows_of(i)] = factor
    r.result[rows_of(i)] = h1


def feed_forward(r, j):
    units, tile = slice(j * 512, (j + 1) * 512), slice(j * 128, (j + 1) * 128)
    bias = jnp.concatenate([r.params[24 + m : 25 + m, tile] for m in range(4)], 1)
    sums = None
    for i in range(2):
        z = nn(r.a2[rows_of(i)], r.w_up[:, units]) + bias
        z2 = z * z
        half = 0.5 + 0.5 * jnp.tanh(z * (GELU0 + GELU1 * z2))
        act = (z * half).astype(BF16)
        slope = half + z * (2 * GELU0 + 6 * GELU1 * z2) * (half * (1.0 - half))
        gz = (nt(r.y[i], r.w_down[units, :]) * slope).astype(BF16)
        r.act[rows_of(i), units] = act
        r.gz[rows_of(i)] = gz
        back = nt(gz, r.w_up[:, units])

        r.back[rows_of(i)] = back if j == 0 else r.back[rows_of(i)] + back

        total = column_sum(gz.astype(F32))
        sums = total if sums is None else sums + total
    for m in range(4):
        r.small[j, 24 + m : 25 + m] = sums[:, m * 128 : (m + 1) * 128]
    g_down = tn(r.act[:, units], r.y[...].reshape(1024, 512)).astype(BF16)
    for c in range(2):
        for t in range(4):
            r.tiles[8 + t, j, c] = g_down[c * 256 : (c + 1) * 256, t * 128 : (t + 1) * 128].reshape(4, 4, 16, 128)
    g_up = tn(r.a2[...], r.gz[...]).astype(BF16)
    fold(r, [g_up[:, q * 128 : (q + 1) * 128] for q in range(4)], 4 + j)


def add_small(r, row, value):
    for x in range(4):
        r.small[x, row : row + 1] = r.small[x, row : row + 1] + value[:, x * 128 : (x + 1) * 128]


def second_norm_back(r, i):
    grad, unit = r.back[rows_of(i)], r.u2[rows_of(i)]
    add_small(r, 20, column_sum(grad * unit))
    add_small(r, 21, column_sum(grad))
    y = r.y[i].astype(F32)
    add_small(r, 23, column_sum(y))
    gh1 = y + normalized_back(grad, unit, r.r2[rows_of(i)], r.params[20:21])
    r.back[rows_of(i)] = gh1
    gb = gh1.astype(BF16)
    r.gb[rows_of(i)] = gb
    add_small(r, 22, column_sum(gb.astype(F32)))
    go = (nt(gb, r.w_out[...]) * r.inverse[rows_of(i)]).astype(BF16)
    r.go[rows_of(i)] = go
    product = go.astype(F32) * r.o32[rows_of(i)]
    high = product.astype(BF16).astype(F32)
    low = product - high
    first = lax.broadcasted_iota(jnp.int32, (1, 128), 1) < 64
    for hp in range(4):
        columns = slice(hp * 128, (hp + 1) * 128)
        swapped = pltpu.roll(low[:, columns], 64, 1)
        r.god0[rows_of(i), columns] = jnp.where(first, high[:, columns], swapped).astype(BF16)
        r.god1[rows_of(i), columns] = jnp.where(first, swapped, high[:, columns]).astype(BF16)


def out_gradient(r):
    g_out = tn(r.o[...], r.gb[...]).astype(BF16)
    fold(r, [g_out[:, q * 128 : (q + 1) * 128] for q in range(4)], 3)


def result_of(r, i):
    r.out[i] = (r.result[rows_of(i)] + nn(r.act[rows_of(i)], r.w_down[...]) + r.params[23:24]).astype(BF16)


def attend_back(r, i, hp):
    q, k, v = (pair_of(r, i, hp, part) for part in range(3))
    columns = slice(hp * 128, (hp + 1) * 128)
    go = r.go[rows_of(i), columns]
    gq = gk = gv = 0.0
    for h in range(2):
        lanes = head_lanes(h)
        both = jnp.concatenate((go, (r.god0, r.god1)[h][rows_of(i), columns]), 1)
        wide = jnp.concatenate((v * lanes, jnp.full((512, 128), -1.0, BF16)), 1)
        expo = r.expo[i * 8 + hp * 2 + h]
        gs = (expo.astype(F32) * nt(both, wide)).astype(BF16)
        gq = gq + nn(gs, k * lanes)
        gk = gk + tn(gs, q * lanes)
        gv = gv + tn(expo, go * lanes)
    for part, value in enumerate((gq * 0.125, gk, gv)):
        r.qkv[rows_of(i), part * 512 + hp * 128 : part * 512 + (hp + 1) * 128] = value.astype(BF16)


def first_norm_back(r, i):
    grad, unit = nt(r.qkv[rows_of(i)], r.w_qkv[...]), r.u1[rows_of(i)]
    add_small(r, 18, column_sum(grad * unit))
    add_small(r, 19, column_sum(grad))
    gh0 = r.back[rows_of(i)] + normalized_back(grad, unit, r.r1[rows_of(i)], r.params[18:19])
    r.glat[i] = gh0.astype(BF16)
    total = column_sum(gh0)
    row = lax.broadcasted_iota(jnp.int32, (18, 1), 0)
    for x in range(4):
        mine = jnp.where(row == r.task_ids[i], total[:, x * 128 : (x + 1) * 128], 0.0)
        r.small[x, 0:18] = r.small[x, 0:18] + mine


def in_gradient(r, t):
    columns = jnp.concatenate([r.qkv[:, ct * 128 : (ct + 1) * 128] for ct in COLUMNS[t]], 1)
    g_in = tn(r.a1[...], columns).astype(BF16)
    fold(r, [g_in[:, q * 128 : (q + 1) * 128] for q in range(4)], t)


class Refs:
    def __init__(self, names, refs):
        for name, ref in zip(names, refs, strict=True):
            setattr(self, name, ref)


RAW = {
    "raw_in": ((4, 1536), BF16),
    "raw_out": ((4, 512), BF16),
    "raw_up": ((4, 2048), BF16),
    "raw_down": ((16, 512), BF16),
    "raw_table": ((4, 18), BF16),
    "raw_norms": ((4, 4), BF16),
    "raw_biases": ((2, 4), BF16),
    "raw_up_bias": ((1, 16), BF16),
}
INPUTS = ("task_ids", "counts", "lat_hbm", "y_hbm", *(f"{name}_hbm" for name in RAW))
OUTPUTS = ("out_hbm", "glat_hbm", "total", "s_total")
BLOCKS = (TILES, 4, 2, 4, 4, 16, 128)
SCRATCH = {
    **RAW,
    "own32": ((TILES, 16, 128), F32),
    "own": ((TILES, 16, 128), BF16),
    "small32": ((40, 128), F32),
    "table32": ((128, 128), F32),
    "own_small": ((32, 128), BF16),
    "lat": ((2, 512, 512), BF16),
    "y": ((2, 512, 512), BF16),
    "out": ((2, 512, 512), BF16),
    "w_qkv": ((512, 1536), BF16),
    "w_out": ((512, 512), BF16),
    "w_up": ((512, 2048), BF16),
    "w_down": ((2048, 512), BF16),
    "params": ((32, 512), F32),
    "a1": ((1024, 512), BF16),
    "u1": ((1024, 512), F32),
    "r1": ((1024, 1), F32),
    "qkv": ((1024, 1536), BF16),
    "expo": ((16, 512, 512), BF16),
    "o": ((1024, 512), BF16),
    "o32": ((1024, 512), F32),
    "inverse": ((1024, 512), F32),
    "result": ((1024, 512), F32),
    "a2": ((1024, 512), BF16),
    "u2": ((1024, 512), F32),
    "r2": ((1024, 1), F32),
    "act": ((1024, 2048), BF16),
    "gz": ((1024, 512), BF16),
    "god0": ((1024, 512), BF16),
    "back": ((1024, 512), F32),
    "gb": ((1024, 512), BF16),
    "small": ((4, 32, 128), F32),
    "tiles": (BLOCKS, BF16),
    "slots": ((2, 3, 32, 128), BF16),
    "kept": ((4, 32, 128), BF16),
    "pair": ((4, 32, 128), BF16),
    "from_pair": ((TILES, 4, 4, 4, 16, 128), BF16),
    "from1": ((TILES, 3, 4, 4, 16, 128), BF16),
    "from2": ((TILES, 3, 4, 16, 128), BF16),
    "from3": ((TILES, 3, 16, 128), BF16),
    "s_pair": ((4, 32, 128), F32),
    "s_slots": ((3, 3, 32, 128), F32),
    "s_held": ((7, 32, 128), F32),
}
SEMAPHORES = {
    "g_send": (2, 3, 13),
    "g_recv": (2, 3, 13),
    "gs_send": (10,),
    "gs_recv": (10,),
    "p_send": (12,),
    "p_recv": (12,),
    "r_send": (17, 9),
    "r_recv": (17, 9),
    "rs_send": (10,),
    "rs_recv": (10,),
    "local": (12,),
}


def alias(r):
    r.go, r.god1, r.glat = r.gz, r.a2, r.y


def loop(count, step):
    lax.fori_loop(0, count, lambda n, carry: (step(n), carry)[1], 0)


def pack_own(r, pos):
    for t, blocks in enumerate(COLUMNS):
        raw = (r.raw_in, r.raw_out, r.raw_up)[0 if t < 3 else 1 if t == 3 else 2]
        for q, ct in enumerate(blocks):
            r.own32[t, 4 * q : 4 * q + 4] = raw[:, ct * 128 : (ct + 1) * 128].astype(F32)
    for t in range(8):
        r.own[t] = r.own32[t].astype(BF16)
    for t in range(4):
        r.own[8 + t] = r.raw_down[:, t * 128 : (t + 1) * 128]
    r.small32[...] = jnp.zeros_like(r.small32)
    r.table32[...] = jnp.zeros_like(r.table32)
    r.table32[0:4, 0:18] = r.raw_table[...].astype(F32)
    r.small32[18:22, 0:4] = r.raw_norms[...].astype(F32)
    r.small32[22:24, 0:4] = r.raw_biases[...].astype(F32)
    r.small32[32:33, 0:16] = r.raw_up_bias[...].astype(F32)
    offset, bias_row, bias_offset = small_place(pos)
    block = pltpu.roll(r.small32[0:32] + r.table32[...].T[0:32], offset, 1)
    bias = pltpu.roll(r.small32[32:40], bias_offset, 1)[0:1]
    row = lax.broadcasted_iota(jnp.int32, (32, 1), 0)
    r.own_small[...] = (block + jnp.where(row == bias_row, bias, 0.0)).astype(BF16)


def kernel(*refs):
    r = Refs((*INPUTS, *OUTPUTS, *SCRATCH, *SEMAPHORES), refs)
    alias(r)
    pos = my_position()
    loads = [
        pltpu.make_async_copy(getattr(r, f"{name}_hbm"), getattr(r, name), r.local.at[n])
        for n, name in enumerate((*RAW, "lat", "y"))
    ]
    store_out = pltpu.make_async_copy(r.out, r.out_hbm, r.local.at[10])
    store_glat = pltpu.make_async_copy(r.glat, r.glat_hbm, r.local.at[11])
    greet(pos)
    for load in loads:
        load.start()
    gathers = [Gather(w, r.own, r.tiles, r.g_send, r.g_recv, pos) for w in range(2)]
    tiny = SmallGather(r.own_small, r.slots, r.kept, r.pair, r.gs_send, r.gs_recv, pos)
    tiny_sum = SmallScatter(r.small, r.s_pair, r.s_slots, r.s_held, r.rs_send, r.rs_recv, pos)
    g_in = [Piece(r, pos, t, t, 1, ORDERS[t][::-1]) for t in range(3)]
    g_out = Piece(r, pos, 3, 3, 1, ("x", "z", "y"))
    g_up = [Piece(r, pos, 4 + j, 4 + j, 1, ORDERS[j % 3][::-1]) for j in range(4)]
    g_down = [Piece(r, pos, 8 + j, 8, 4, (), x=j, stages=()) for j in range(4)]
    down_orders = (("z", "y", "x"), ("y", "z", "x"))
    g_halves = [
        [Piece(r, pos, 8 + 2 * j + n, 8 + 2 * n, 2, down_orders[n], x=j, stages=(0, 1)) for n in range(2)]
        for j in range(4)
    ]
    g_last = Piece(r, pos, 16, 8, 4, ("z", "y", "x"), stages=(2,))
    for load in loads[:8]:
        load.wait()
    pack_own(r, pos)
    greeted(pos)

    gathers[0].start(0)
    tiny.start(0)
    gathers[1].start(0)
    for t in range(TILES):
        r.tiles[t, pos["x"], pos["c"], pos["y"], pos["z"]] = r.own[t]
    r.small[...] = jnp.zeros_like(r.small)
    gathers[0].arrive(0)
    gathers[0].start(1)
    tiny.arrive(0)
    tiny.start(1)
    gathers[1].arrive(0)
    gathers[1].start(1)
    gathers[0].arrive(1)
    gathers[0].start(2)
    tiny.arrive(1)
    tiny.start(2)
    tiny.arrive(2)
    gathers[0].arrive(2)
    gathers[1].arrive(1)
    gathers[1].start(2)
    tiny.arrive_pair(r.params)
    loads[8].wait()
    for i in range(2):
        first_norm(r, i)
    for t in range(3):
        gathers[0].arrive_pair(t)
    for t in range(3):
        unfold(r, t, r.w_qkv)
    for i in range(2):
        project(r, i)
    for n in range(8):
        attend(r, n // 4, n % 4)
    gathers[1].arrive(2)
    gathers[1].arrive_pair(0)
    unfold(r, 3, r.w_out)
    for i in range(2):
        second_norm(r, i)
    for part in (1, 2):
        gathers[1].arrive_pair(part)
    for t in range(4, 8):
        unfold(r, t, r.w_up)
    unfold_plain(r, r.w_down)
    for gather in gathers:
        gather.settle()
    tiny.settle()
    loads[9].wait()

    def leave(j):
        g_up[j].pair_copy().start()
        g_down[j].pair_copy().start()

    def begin(j):
        g_up[j].pair_add()
        g_down[j].pair_add()
        for piece in (g_up[j], *g_halves[j]):
            piece.start(0)

    def turn(piece, stage):
        piece.add(stage)
        piece.start(stage + 1)

    def second(j):
        for piece in (g_up[j], *g_halves[j]):
            turn(piece, 0)

    def third(j):
        turn(g_up[j], 1)
        for piece in g_halves[j]:
            piece.add(1)

    feed_forward(r, 0)
    leave(0)
    feed_forward(r, 1)
    leave(1)
    begin(0)
    feed_forward(r, 2)
    leave(2)
    begin(1)
    feed_forward(r, 3)
    leave(3)
    begin(2)
    second(0)
    second_norm_back(r, 0)
    second_norm_back(r, 1)
    begin(3)
    second(1)
    out_gradient(r)
    g_out.pair_copy().start()
    for n in range(8):
        attend_back(r, n % 2, n // 2)
        if n == 1:
            g_out.pair_add()
            g_out.start(0)
            second(2)
            third(0)
        if n == 3:
            in_gradient(r, 0)
            g_in[0].pair_copy().start()
            second(3)
            third(1)
        if n == 5:
            g_in[0].pair_add()
            g_in[0].start(0)
            in_gradient(r, 1)
            g_in[1].pair_copy().start()
            turn(g_out, 0)
            third(2)
    in_gradient(r, 2)
    g_in[2].pair_copy().start()
    g_in[1].pair_add()
    g_in[1].start(0)
    third(3)
    g_last.start(2)
    first_norm_back(r, 0)
    g_in[2].pair_add()
    g_in[2].start(0)
    first_norm_back(r, 1)
    tiny_sum.pair_copy().start()
    store_glat.start()
    turn(g_in[0], 0)
    turn(g_out, 1)
    tiny_sum.add_pair()
    tiny_sum.start(0)
    result_of(r, 0)
    result_of(r, 1)
    store_out.start()
    tiny_sum.add(0)
    tiny_sum.start(1)
    turn(g_in[2], 0)
    turn(g_in[1], 0)
    turn(g_in[0], 1)
    for piece in (*g_up, g_last):
        piece.add(2)
    tiny_sum.add(1)
    tiny_sum.start(2)
    turn(g_in[2], 1)
    turn(g_in[1], 1)
    g_out.add(2)
    g_in[0].add(2)
    for piece in (*g_in, g_out, *g_up, *g_down, *(half for halves in g_halves for half in halves), g_last):
        piece.settle()
    store_out.wait()
    store_glat.wait()
    g_in[1].add(2)
    g_in[2].add(2)
    tiny_sum.add(2)
    r.s_total[...] = r.s_held[6]
    tiny_sum.settle()


SHAPES = ((4, 18), (4, 4), (4, 1536), (4, 512), (2, 4), (4, 2048), (1, 16), (16, 512))


def finish(*refs):
    out_in, glat_in, total_hbm, small_hbm, out, glat, *rest = refs
    targets, (held, total, small), parts, (sems, load_sems, store_sems) = rest[:8], rest[8:11], rest[11:19], rest[19:]
    table, norms, w_in, w_out, biases, w_up, up_bias, w_down = parts
    loads = [
        pltpu.make_async_copy(total_hbm, total, load_sems.at[0]),
        pltpu.make_async_copy(small_hbm, small, load_sems.at[1]),
    ]
    for load in loads:
        load.start()
    reads, writes = [], []
    for n, (source, target) in enumerate(((out_in, out), (glat_in, glat))):
        for k in range(4):
            slot, rows = 4 * n + k, pl.ds(k % 2 * 256, 256)
            reads.append(pltpu.make_async_copy(source.at[k // 2, rows], held.at[slot], sems.at[0, slot]))
            writes.append(pltpu.make_async_copy(held.at[slot], target.at[k // 2, rows], sems.at[1, slot]))
    for read in reads:
        read.start()
    for load in loads:
        load.wait()
    for t, blocks in enumerate(COLUMNS):
        to = (w_in, w_out, w_up)[0 if t < 3 else 1 if t == 3 else 2]
        for q, ct in enumerate(blocks):
            to[:, ct * 128 : (ct + 1) * 128] = total[t, 4 * q : 4 * q + 4]
    for t in range(4):
        w_down[:, t * 128 : (t + 1) * 128] = total[8 + t]
    offset, bias_row, bias_offset = small_place(my_position())
    block = pltpu.roll(small[...], lax.rem(128 - offset, 128), 1)
    table[...] = jnp.concatenate((block, jnp.zeros((96, 128), F32))).T[0:4, 0:18]
    norms[...] = block[18:22, 0:4]
    biases[...] = block[22:24, 0:4]
    row = lax.broadcasted_iota(jnp.int32, (32, 1), 0)
    bias = jnp.sum(jnp.where(row == bias_row, small[...], 0.0), axis=0, keepdims=True)
    bias = pltpu.roll(jnp.broadcast_to(bias, (8, 128)), lax.rem(128 - bias_offset, 128), 1)
    up_bias[...] = bias[0:1, 0:16]
    stores = [
        pltpu.make_async_copy(part, target, store_sems.at[n])
        for n, (part, target) in enumerate(zip(parts, targets, strict=True))
    ]
    for store in stores:
        store.start()
    for read, write in zip(reads, writes, strict=True):
        read.wait()
        write.start()
    for copy in (*stores, *writes):
        copy.wait()


def whole(task_ids, counts, latents, cotangent, *raw):
    vmem = pl.BlockSpec(memory_space=pltpu.VMEM)
    smem = pl.BlockSpec(memory_space=pltpu.SMEM)
    hbm = pl.BlockSpec(memory_space=pl.ANY)
    array = jax.ShapeDtypeStruct(latents.shape, BF16)
    found = pl.pallas_call(
        kernel,
        out_shape=[
            array,
            array,
            jax.ShapeDtypeStruct((TILES, 16, 128), F32),
            jax.ShapeDtypeStruct((32, 128), F32),
        ],
        in_specs=[smem, smem] + [hbm] * (2 + len(RAW)),
        out_specs=[hbm, hbm, vmem, vmem],
        scratch_shapes=[pltpu.VMEM(shape, dtype) for shape, dtype in SCRATCH.values()]
        + [pltpu.SemaphoreType.DMA(shape) for shape in SEMAPHORES.values()],
        compiler_params=pltpu.CompilerParams(
            collective_id=0, has_side_effects=True, vmem_limit_bytes=60 * 2**20
        ),
    )(task_ids, counts, latents, cotangent, *raw)
    return pl.pallas_call(
        finish,
        out_shape=[array, array] + [jax.ShapeDtypeStruct(shape, F32) for shape in SHAPES],
        in_specs=[hbm] * 4,
        out_specs=[hbm] * 10,
        scratch_shapes=[
            pltpu.VMEM((8, 256, 512), BF16),
            pltpu.VMEM((TILES, 16, 128), F32),
            pltpu.VMEM((32, 128), F32),
            *(pltpu.VMEM(shape, F32) for shape in SHAPES),
            pltpu.SemaphoreType.DMA((2, 8)),
            pltpu.SemaphoreType.DMA((2,)),
            pltpu.SemaphoreType.DMA((8,)),
        ],
    )(*found)


def body(
    latents,
    task_ids,
    slot_counts,
    cotangent,
    task_embed,
    norms,
    attn_in,
    attn_out,
    out_biases,
    mlp_in,
    mlp_in_bias,
    mlp_out,
):
    raw = (attn_in, attn_out, mlp_in, mlp_out, task_embed.T, norms, out_biases, mlp_in_bias.reshape(1, 16))
    found = list(whole(task_ids, slot_counts, latents, cotangent, *raw))
    found[2] = found[2].T
    found[8] = found[8].reshape(16)
    return tuple(found)


def solution(mesh):
    in_specs = (
        P(("dp", "fsdp"), None, None),
        P(("dp", "fsdp")),
        P(("dp", "fsdp")),
        P(("dp", "fsdp"), None, None),
        P(None, ("dp", "fsdp")),
        P(None, ("dp", "fsdp")),
        P(("dp", "fsdp"), None),
        P(("dp", "fsdp"), None),
        P(None, ("dp", "fsdp")),
        P(("dp", "fsdp"), None),
        P(("dp", "fsdp")),
        P(("dp", "fsdp"), None),
    )
    out_specs = (
        P(("dp", "fsdp"), None, None),
        P(("dp", "fsdp"), None, None),
        P(None, ("dp", "fsdp")),
        P(None, ("dp", "fsdp")),
        P(("dp", "fsdp"), None),
        P(("dp", "fsdp"), None),
        P(None, ("dp", "fsdp")),
        P(("dp", "fsdp"), None),
        P(("dp", "fsdp")),
        P(("dp", "fsdp"), None),
    )
    return jax.shard_map(body, mesh=mesh, in_specs=in_specs, out_specs=out_specs, check_vma=False)
```

```python
import functools
import math

import jax
import jax.numpy as jnp
from jax import lax
from jax.experimental import pallas as pl
from jax.experimental.pallas import tpu as pltpu
from jax.sharding import PartitionSpec as P

HEADS = 8
EPS = 1e-05
BEST = lax.Precision.HIGHEST
MESH = pl.DeviceIdType.MESH
ALL = slice(None)
ORDERS = (("z", "y", "x"), ("y", "x", "z"), ("x", "z", "y"))
TILES = 12
WAVES = (((0, 1), (1, 1), (2, 1)), ((3, 3), (6, 3), (9, 3)))


def my_position():
    dp, fsdp = lax.axis_index("dp"), lax.axis_index("fsdp")
    return {
        "x": lax.div(dp, 2),
        "c": lax.rem(dp, 2),
        "y": lax.div(fsdp, 4),
        "z": lax.rem(fsdp, 4),
    }


def moved(pos, axis, step):
    size = 2 if axis == "c" else 4
    return {**pos, axis: lax.rem(pos[axis] + step, size)}


def device_of(pos):
    return (pos["x"] * 2 + pos["c"], pos["y"] * 4 + pos["z"])


def partners_of(pos):
    return [moved(pos, axis, k) for axis in "xyz" for k in (1, 2, 3)] + [moved(pos, "c", 1)]


def greet(pos):
    barrier = pltpu.get_barrier_semaphore()
    for other in partners_of(pos):
        pl.semaphore_signal(barrier, inc=1, device_id=device_of(other), device_id_type=MESH)


def greeted(pos):
    pl.semaphore_wait(pltpu.get_barrier_semaphore(), 10)


def remote(src, dst, send, recv, pos):
    return pltpu.make_async_remote_copy(
        src_ref=src, dst_ref=dst, send_sem=send, recv_sem=recv,
        device_id=device_of(pos), device_id_type=MESH,
    )


class Gather:
    def __init__(self, wave, own, tiles, send, recv, pos):
        self.wave, self.own, self.tiles, self.pos = wave, own, tiles, pos
        self.send, self.recv = send, recv

    def slab(self, part, free, at=None):
        first, count = WAVES[self.wave][part]
        place = {**self.pos, **(at or {})}
        index = [ALL if axis in free else place[axis] for axis in "xcyz"]
        return self.tiles.at[(pl.ds(first, count), *index)]

    def stage_copy(self, part, stage, k):
        order = ORDERS[part]
        slab = self.slab(part, order[:stage])
        src = slab
        if stage == 0:
            first, count = WAVES[self.wave][part]
            src = self.own.at[pl.ds(first, count)]
        slot = (self.wave, part, stage * 3 + k - 1)
        return remote(src, slab, self.send.at[slot], self.recv.at[slot], moved(self.pos, order[stage], k))

    def pair_copy(self, part, k):
        order = ORDERS[part]
        at = {order[2]: lax.rem(self.pos[order[2]] + 4 - k, 4)} if k else None
        slab = self.slab(part, order[:2], at)
        slot = (self.wave, part, 9 + k)
        return remote(slab, slab, self.send.at[slot], self.recv.at[slot], moved(self.pos, "c", 1))

    def start(self, stage):
        for part in range(3):
            for k in (2, 1, 3):
                self.stage_copy(part, stage, k).start()
            if stage == 2:
                self.pair_copy(part, 0).start()

    def arrive(self, stage):
        for part in range(3):
            for k in (1, 3, 2):
                self.stage_copy(part, stage, k).wait_recv()
                if stage == 2:
                    self.pair_copy(part, k).start()

    def arrive_pair(self, part):
        for k in range(4):
            self.pair_copy(part, k).wait_recv()

    def settle(self):
        for part in range(3):
            for stage in range(3):
                for k in (1, 2, 3):
                    self.stage_copy(part, stage, k).wait_send()
            for k in range(4):
                self.pair_copy(part, k).wait_send()


class SmallGather:
    def __init__(self, own, slots, kept, pair, send, recv, pos):
        self.own, self.slots, self.kept, self.pair = own, slots, kept, pair
        self.send, self.recv, self.pos = send, recv, pos

    def copy(self, stage, k):
        here = self.kept.at[self.pos["x"]]
        src = self.own if stage == 0 else here
        dst = here if stage == 2 else self.slots.at[stage, k - 1]
        slot = stage * 3 + k - 1
        return remote(src, dst, self.send.at[slot], self.recv.at[slot], moved(self.pos, "zyx"[stage], k))

    def pair_copy(self):
        return remote(self.kept, self.pair, self.send.at[9], self.recv.at[9], moved(self.pos, "c", 1))

    def start(self, stage):
        for k in (2, 1, 3):
            self.copy(stage, k).start()

    def arrive(self, stage):
        for k in (1, 3, 2):
            self.copy(stage, k).wait_recv()
        if stage == 2:
            self.pair_copy().start()
            return
        total = self.own[...] if stage == 0 else self.kept[self.pos["x"]]
        if stage == 1:
            for k in (1, 2, 3):
                self.copy(1, k).wait_send()
        for k in range(3):
            total = total + self.slots[stage, k]
        self.kept[self.pos["x"]] = total

    def arrive_pair(self, out):
        self.pair_copy().wait_recv()
        for x in range(4):
            out[:, x * 128 : (x + 1) * 128] = self.kept[x].astype(jnp.float32) + self.pair[x].astype(jnp.float32)

    def settle(self):
        for stage in (0, 2):
            for k in (1, 2, 3):
                self.copy(stage, k).wait_send()
        self.pair_copy().wait_send()


class Piece:
    def __init__(self, r, pos, number, first, count, order, x=None, stages=(0, 1, 2)):
        self.r, self.pos, self.number, self.first, self.count = r, pos, number, first, count
        self.order, self.x, self.stages = order, x, stages

    def span(self):
        return pl.ds(self.first, self.count)

    def pair_copy(self):
        other = moved(self.pos, "c", 1)
        x = ALL if self.x is None else self.x
        return remote(
            self.r.tiles.at[self.span(), x, other["c"]], self.r.from_pair.at[self.span(), x],
            self.r.p_send.at[self.number], self.r.p_recv.at[self.number], other,
        )

    def pair_add(self):
        self.pair_copy().wait_recv()
        core = self.pos["c"]
        for n in range(self.count):
            t = self.first + n
            for x in range(4) if self.x is None else (self.x,):
                total = self.r.tiles[t, x, core].astype(jnp.float32) + self.r.from_pair[t, x].astype(jnp.float32)
                self.r.tiles[t, x, core] = total.astype(jnp.bfloat16)

    def index(self, stage, place):
        held = self.order[: stage + 1]
        found = []
        for axis in "xcyz":
            if axis == "c" or axis in held:
                found.append(place[axis])
            else:
                found.append(self.x if axis == "x" and self.x is not None else ALL)
        return tuple(found)

    def left(self, stage):
        free = [axis for axis in "xyz" if axis not in self.order[: stage + 1]]
        return tuple(self.x if axis == "x" and self.x is not None else ALL for axis in free)

    def copy(self, stage, k):
        axis = self.order[stage]
        other = moved(self.pos, axis, k)
        src = self.r.tiles.at[(self.span(), *self.index(stage, other))]
        dst = (self.r.from1, self.r.from2, self.r.from3)[stage].at[(self.span(), k - 1, *self.left(stage))]
        slot = (self.number, stage * 3 + k - 1)
        return remote(src, dst, self.r.r_send.at[slot], self.r.r_recv.at[slot], other)

    def start(self, stage):
        for k in (2, 1, 3):
            self.copy(stage, k).start()

    def add(self, stage):
        for k in (1, 3, 2):
            self.copy(stage, k).wait_recv()
        index, left = self.index(stage, self.pos), self.left(stage)
        arrived = (self.r.from1, self.r.from2, self.r.from3)[stage]
        for n in range(self.count):
            t = self.first + n
            total = self.r.tiles[(t, *index)].astype(jnp.float32)
            for k in range(3):
                total = total + arrived[(t, k, *left)].astype(jnp.float32)
            if stage == 2:
                self.r.total[t] = total
            else:
                self.r.tiles[(t, *index)] = total.astype(jnp.bfloat16)

    def settle(self):
        if self.number < 12 and self.stages != (0, 1):
            self.pair_copy().wait_send()
        for stage in self.stages:
            for k in (1, 2, 3):
                self.copy(stage, k).wait_send()


class SmallScatter:
    def __init__(self, own, pair, slots, held, send, recv, pos):
        self.own, self.pair, self.slots, self.held = own, pair, slots, held
        self.send, self.recv, self.pos = send, recv, pos

    def pair_copy(self):
        return remote(self.own, self.pair, self.send.at[9], self.recv.at[9], moved(self.pos, "c", 1))

    def copy(self, stage, k):
        other = moved(self.pos, "xyz"[stage], k)
        src = self.held.at[other["x"]] if stage == 0 else self.held.at[3 + stage]
        slot = stage * 3 + k - 1
        return remote(src, self.slots.at[stage, k - 1], self.send.at[slot], self.recv.at[slot], other)

    def add_pair(self):
        self.pair_copy().wait_recv()
        self.held[0:4] = self.own[...] + self.pair[...]

    def start(self, stage):
        for k in (2, 1, 3):
            self.copy(stage, k).start()

    def add(self, stage):
        for k in (1, 3, 2):
            self.copy(stage, k).wait_recv()
        total = self.held[self.pos["x"]] if stage == 0 else self.held[3 + stage]
        for k in range(3):
            total = total + self.slots[stage, k]
        self.held[4 + stage] = total

    def settle(self):
        self.pair_copy().wait_send()
        for stage in range(3):
            for k in (1, 2, 3):
                self.copy(stage, k).wait_send()


COLUMNS = (
    (0, 4, 8, 1),
    (5, 9, 2, 6),
    (10, 3, 7, 11),
    (0, 1, 2, 3),
    *(tuple(range(4 * j, 4 * j + 4)) for j in range(4)),
)


def quarter_order(transposed=False):
    a = lax.broadcasted_iota(jnp.int32, (256, 256), 1 if transposed else 0)
    b = lax.broadcasted_iota(jnp.int32, (256, 256), 0 if transposed else 1)
    source = ((a % 64) // 4) * 16 + (a // 64) * 4 + a % 4
    return (source == b).astype(jnp.float32).astype(jnp.bfloat16)


def unfold(r, t, out):
    blocks = [r.tiles[t, xc // 2, xc % 2].reshape(256, 128) for xc in range(8)]
    rows = nn(quarter_order(), jnp.concatenate(blocks, 1)).astype(jnp.bfloat16)
    for q, ct in enumerate(COLUMNS[t]):
        for xc in range(8):
            out[xc * 64 : (xc + 1) * 64, ct * 128 : (ct + 1) * 128] = rows[q * 64 : (q + 1) * 64, xc * 128 : (xc + 1) * 128]


def unfold_plain(r, out):
    def one(i):
        x, c = lax.div(i, 2), lax.rem(i, 2)
        for t in range(4):
            out[pl.ds(pl.multiple_of(i * 256, 256), 256), t * 128 : (t + 1) * 128] = r.tiles[8 + t, x, c].reshape(256, 128)

    loop(8, one)


def fold(r, columns, t):
    rows = [jnp.concatenate([block[xc * 64 : (xc + 1) * 64] for xc in range(8)], 1) for block in columns]
    blocks = nn(quarter_order(True), jnp.concatenate(rows, 0)).astype(jnp.bfloat16)
    for xc in range(8):
        r.tiles[t, xc // 2, xc % 2] = blocks[:, xc * 128 : (xc + 1) * 128].reshape(4, 4, 16, 128)


def small_place(pos):
    ring = pos["y"] * 4 + pos["z"]
    return pos["c"] * 64 + ring * 4, 24 + pos["c"] * 2 + lax.div(ring, 8), 16 * lax.rem(ring, 8)


F32, BF16 = jnp.float32, jnp.bfloat16
GELU0 = math.sqrt(2.0 / math.pi)
GELU1 = GELU0 * 0.044715


def nn(a, b):
    return jnp.dot(a, b, preferred_element_type=F32)


def nt(a, b):
    return lax.dot_general(a, b, (((1,), (1,)), ((), ())), preferred_element_type=F32)


def tn(a, b):
    return lax.dot_general(a, b, (((0,), (0,)), ((), ())), preferred_element_type=F32)


def span_of(n, size):
    if isinstance(n, int):
        return slice(n * size, (n + 1) * size)
    return pl.ds(pl.multiple_of(n * size, size), size)


def rows_of(i):
    return span_of(i, 512)


def normalized(h):
    centred = h - jnp.mean(h, axis=-1, keepdims=True)
    factor = lax.rsqrt(jnp.mean(centred * centred, axis=-1, keepdims=True) + EPS)
    return centred * factor, factor


def normalized_back(grad, unit, factor, gain):
    scaled = grad * gain
    inner = jnp.mean(scaled, axis=-1, keepdims=True)
    along = jnp.mean(scaled * unit, axis=-1, keepdims=True)
    return factor * (scaled - inner - unit * along)


def column_sum(v):
    return jnp.sum(v, axis=0, keepdims=True)


def embedding(r, i):
    row = lax.broadcasted_iota(jnp.int32, (24, 1), 0)
    return column_sum(jnp.where(row == r.task_ids[i], r.params[0:24], 0.0))


def head_lanes(h):
    lane = lax.broadcasted_iota(jnp.int32, (1, 128), 1)
    return ((lane >= 64) == (h == 1)).astype(F32).astype(BF16)


def first_norm(r, i):
    unit, factor = normalized(r.lat[i].astype(F32) + embedding(r, i))
    r.a1[rows_of(i)] = (unit * r.params[18:19] + r.params[19:20]).astype(BF16)
    r.u1[rows_of(i)] = unit
    r.factors[rows_of(i), 0:1] = factor


def project(r, i):
    a1 = r.a1[rows_of(i)]
    for part in range(3):
        columns = slice(part * 512, (part + 1) * 512)
        result = nn(a1, r.w_qkv[:, columns])
        if part == 0:
            result = result * 0.125
        r.qkv[rows_of(i), columns] = result.astype(BF16)


def pair_of(r, i, hp, part):
    return r.qkv[rows_of(i), span_of(part * 4 + hp, 128)]


def attend(r, i, hp):
    q, k, v = (pair_of(r, i, hp, part) for part in range(3))
    slots = lax.broadcasted_iota(jnp.int32, (1, 512), 1)
    bias = jnp.where(slots < r.counts[i], 0.0, -1000000000.0)
    mixed = None
    for h in range(2):
        lanes = head_lanes(h)
        scores = nt(q, k * lanes) + bias
        expo = jnp.exp(scores - jnp.max(scores, axis=-1, keepdims=True)).astype(BF16)
        r.expo[i * 8 + hp * 2 + h] = expo
        wide = jnp.concatenate((v * lanes, jnp.broadcast_to(lanes, (512, 128))), 1)
        term = nn(expo, wide)
        mixed = term if mixed is None else mixed + term
    inverse = 1.0 / mixed[:, 128:]
    columns = span_of(hp, 128)
    r.inverse[rows_of(i), columns] = inverse
    mean = mixed[:, :128] * inverse
    r.o32[rows_of(i), columns] = mean
    r.o[rows_of(i), columns] = mean.astype(BF16)


def second_norm(r, i):
    h1 = r.lat[i].astype(F32) + embedding(r, i) + (nn(r.o[rows_of(i)], r.w_out[...]) + r.params[22:23])
    unit, factor = normalized(h1)
    r.a2[rows_of(i)] = (unit * r.params[20:21] + r.params[21:22]).astype(BF16)
    r.u2[rows_of(i)] = unit
    r.factors[rows_of(i), 1:2] = factor
    r.result[rows_of(i)] = h1


def feed_forward(r, j):
    units, tile = span_of(j, 512), span_of(j, 128)
    bias = jnp.concatenate([r.params[24 + m : 25 + m, tile] for m in range(4)], 1)
    sums = None
    for i in range(2):
        z = nn(r.a2[rows_of(i)], r.w_up[:, units]) + bias
        z2 = z * z
        half = 0.5 + 0.5 * jnp.tanh(z * (GELU0 + GELU1 * z2))
        act = (z * half).astype(BF16)
        slope = half + z * (2 * GELU0 + 6 * GELU1 * z2) * (half * (1.0 - half))
        gz = (nt(r.y[i], r.w_down[units, :]) * slope).astype(BF16)
        r.act[rows_of(i), units] = act
        r.gz[j % 2, rows_of(i)] = gz
        back = nt(gz, r.w_up[:, units])
        r.back[rows_of(i)] = back if isinstance(j, int) and j == 0 else r.back[rows_of(i)] + back
        total = column_sum(gz.astype(F32))
        sums = total if sums is None else sums + total
    for m in range(4):
        r.small[j, 24 + m : 25 + m] = sums[:, m * 128 : (m + 1) * 128]


def chunk_gradients(r, j):
    g_down = tn(r.act[:, span_of(j, 512)], r.y[...].reshape(1024, 512)).astype(BF16)
    for c in range(2):
        for t in range(4):
            r.tiles[8 + t, j, c] = g_down[c * 256 : (c + 1) * 256, t * 128 : (t + 1) * 128].reshape(4, 4, 16, 128)
    g_up = tn(r.a2[...], r.gz[j % 2]).astype(BF16)
    fold(r, [g_up[:, q * 128 : (q + 1) * 128] for q in range(4)], 4 + j)


def add_small(r, row, value):
    for x in range(4):
        r.small[x, row : row + 1] = r.small[x, row : row + 1] + value[:, x * 128 : (x + 1) * 128]


def second_norm_back(r, i):
    grad, unit = r.back[rows_of(i)], r.u2[rows_of(i)]
    add_small(r, 20, column_sum(grad * unit))
    add_small(r, 21, column_sum(grad))
    y = r.y[i].astype(F32)
    add_small(r, 23, column_sum(y))
    gh1 = y + normalized_back(grad, unit, r.factors[rows_of(i), 1:2], r.params[20:21])
    r.back[rows_of(i)] = gh1
    gb = gh1.astype(BF16)
    r.gb[rows_of(i)] = gb
    add_small(r, 22, column_sum(gb.astype(F32)))
    go = (nt(gb, r.w_out[...]) * r.inverse[rows_of(i)]).astype(BF16)
    r.go[rows_of(i)] = go
    product = go.astype(F32) * r.o32[rows_of(i)]
    high = product.astype(BF16).astype(F32)
    low = product - high
    first = lax.broadcasted_iota(jnp.int32, (1, 128), 1) < 64
    for hp in range(4):
        columns = slice(hp * 128, (hp + 1) * 128)
        swapped = pltpu.roll(low[:, columns], 64, 1)
        r.god0[rows_of(i), columns] = jnp.where(first, high[:, columns], swapped).astype(BF16)
        r.god1[rows_of(i), columns] = jnp.where(first, swapped, high[:, columns]).astype(BF16)


def out_gradient(r):
    g_out = tn(r.o[...], r.gb[...]).astype(BF16)
    fold(r, [g_out[:, q * 128 : (q + 1) * 128] for q in range(4)], 3)


def result_of(r, i):
    r.out[i] = (r.result[rows_of(i)] + nn(r.act[rows_of(i)], r.w_down[...]) + r.params[23:24]).astype(BF16)


def attend_back(r, i, hp):
    q, k, v = (pair_of(r, i, hp, part) for part in range(3))
    columns = span_of(hp, 128)
    go = r.go[rows_of(i), columns]
    gq = gk = gv = 0.0
    for h in range(2):
        lanes = head_lanes(h)
        both = jnp.concatenate((go, (r.god0, r.god1)[h][rows_of(i), columns]), 1)
        wide = jnp.concatenate((v * lanes, jnp.full((512, 128), -1.0, BF16)), 1)
        expo = r.expo[i * 8 + hp * 2 + h]
        gs = (expo.astype(F32) * nt(both, wide)).astype(BF16)
        gq = gq + nn(gs, k * lanes)
        gk = gk + tn(gs, q * lanes)
        gv = gv + tn(expo, go * lanes)
    for part, value in enumerate((gq * 0.125, gk, gv)):
        r.gqkv[i][part][:, span_of(hp, 128)] = value.astype(BF16)


def first_norm_back(r, i):
    grad, unit = nt(jnp.concatenate([part[...] for part in r.gqkv[i]], 1), r.w_qkv[...]), r.u1[rows_of(i)]
    add_small(r, 18, column_sum(grad * unit))
    add_small(r, 19, column_sum(grad))
    gh0 = r.back[rows_of(i)] + normalized_back(grad, unit, r.factors[rows_of(i), 0:1], r.params[18:19])
    r.glat[i] = gh0.astype(BF16)
    total = column_sum(gh0)
    row = lax.broadcasted_iota(jnp.int32, (18, 1), 0)
    for x in range(4):
        mine = jnp.where(row == r.task_ids[i], total[:, x * 128 : (x + 1) * 128], 0.0)
        r.small[x, 0:18] = r.small[x, 0:18] + mine


def in_gradient(r, t):
    columns = jnp.concatenate(
        [jnp.concatenate([r.gqkv[i][ct // 4][:, span_of(ct % 4, 128)] for ct in COLUMNS[t]], 1) for i in range(2)]
    )
    g_in = tn(r.a1[...], columns).astype(BF16)
    fold(r, [g_in[:, q * 128 : (q + 1) * 128] for q in range(4)], t)


class Refs:
    def __init__(self, names, refs):
        for name, ref in zip(names, refs, strict=True):
            setattr(self, name, ref)


RAW = {
    "raw_in": ((4, 1536), BF16),
    "raw_out": ((4, 512), BF16),
    "raw_up": ((4, 2048), BF16),
    "raw_down": ((16, 512), BF16),
    "raw_table": ((4, 18), BF16),
    "raw_norms": ((4, 4), BF16),
    "raw_biases": ((2, 4), BF16),
    "raw_up_bias": ((1, 16), BF16),
}
INPUTS = ("task_ids", "counts", "lat_hbm", "y_hbm", *(f"{name}_hbm" for name in RAW))
OUTPUTS = ("out_hbm", "glat_hbm", "total", "s_total")
BLOCKS = (TILES, 4, 2, 4, 4, 16, 128)
SCRATCH = {
    **RAW,
    "own32": ((TILES, 16, 128), F32),
    "own": ((TILES, 16, 128), BF16),
    "small32": ((40, 128), F32),
    "table32": ((128, 128), F32),
    "own_small": ((32, 128), BF16),
    "lat": ((2, 512, 512), BF16),
    "y": ((2, 512, 512), BF16),
    "w_qkv": ((512, 1536), BF16),
    "w_out": ((512, 512), BF16),
    "w_up": ((512, 2048), BF16),
    "w_down": ((2048, 512), BF16),
    "params": ((32, 512), F32),
    "a1": ((1024, 512), BF16),
    "u1": ((1024, 512), F32),
    "qkv": ((1024, 1536), BF16),
    "expo": ((16, 512, 512), BF16),
    "o": ((1024, 512), BF16),
    "o32": ((1024, 512), F32),
    "inverse": ((1024, 512), F32),
    "result": ((1024, 512), F32),
    "a2": ((1024, 512), BF16),
    "u2": ((1024, 512), F32),
    "factors": ((1024, 2), F32),
    "act": ((1024, 2048), BF16),
    "gz": ((2, 1024, 512), BF16),
    "back": ((1024, 512), F32),
    "gb": ((1024, 512), BF16),
    "small": ((4, 32, 128), F32),
    "tiles": (BLOCKS, BF16),
    "slots": ((2, 3, 32, 128), BF16),
    "kept": ((4, 32, 128), BF16),
    "pair": ((4, 32, 128), BF16),
    "from_pair": ((TILES, 4, 4, 4, 16, 128), BF16),
    "from1": ((TILES, 3, 4, 4, 16, 128), BF16),
    "from2": ((TILES, 3, 4, 16, 128), BF16),
    "from3": ((TILES, 3, 16, 128), BF16),
    "s_pair": ((4, 32, 128), F32),
    "s_slots": ((3, 3, 32, 128), F32),
    "s_held": ((7, 32, 128), F32),
}
SEMAPHORES = {
    "g_send": (2, 3, 13),
    "g_recv": (2, 3, 13),
    "gs_send": (10,),
    "gs_recv": (10,),
    "p_send": (12,),
    "p_recv": (12,),
    "r_send": (17, 9),
    "r_recv": (17, 9),
    "rs_send": (10,),
    "rs_recv": (10,),
    "local": (12,),
}


def alias(r):
    r.go, r.god0, r.god1 = r.gz.at[0], r.gz.at[1], r.a2
    r.out, r.glat = r.lat, r.y
    r.gqkv = [r.w_up.at[:, span_of(part, 512)] for part in range(3)], [r.lat.at[0], r.lat.at[1], r.w_out]


def loop(count, step):
    lax.fori_loop(0, count, lambda n, carry: (step(n), carry)[1], 0)


def pack_own(r, pos):
    for t, blocks in enumerate(COLUMNS):
        raw = (r.raw_in, r.raw_out, r.raw_up)[0 if t < 3 else 1 if t == 3 else 2]
        for q, ct in enumerate(blocks):
            r.own32[t, 4 * q : 4 * q + 4] = raw[:, ct * 128 : (ct + 1) * 128].astype(F32)
    for t in range(8):
        r.own[t] = r.own32[t].astype(BF16)
    for t in range(4):
        r.own[8 + t] = r.raw_down[:, t * 128 : (t + 1) * 128]
    r.small32[...] = jnp.zeros_like(r.small32)
    r.table32[...] = jnp.zeros_like(r.table32)
    r.table32[0:4, 0:18] = r.raw_table[...].astype(F32)
    r.small32[18:22, 0:4] = r.raw_norms[...].astype(F32)
    r.small32[22:24, 0:4] = r.raw_biases[...].astype(F32)
    r.small32[32:33, 0:16] = r.raw_up_bias[...].astype(F32)
    offset, bias_row, bias_offset = small_place(pos)
    block = pltpu.roll(r.small32[0:32] + r.table32[...].T[0:32], offset, 1)
    bias = pltpu.roll(r.small32[32:40], bias_offset, 1)[0:1]
    row = lax.broadcasted_iota(jnp.int32, (32, 1), 0)
    r.own_small[...] = (block + jnp.where(row == bias_row, bias, 0.0)).astype(BF16)


def kernel(*refs):
    r = Refs((*INPUTS, *OUTPUTS, *SCRATCH, *SEMAPHORES), refs)
    alias(r)
    pos = my_position()
    loads = [
        pltpu.make_async_copy(getattr(r, f"{name}_hbm"), getattr(r, name), r.local.at[n])
        for n, name in enumerate((*RAW, "lat", "y"))
    ]
    store_out = pltpu.make_async_copy(r.out, r.out_hbm, r.local.at[10])
    store_glat = pltpu.make_async_copy(r.glat, r.glat_hbm, r.local.at[11])
    greet(pos)
    for load in loads:
        load.start()
    gathers = [Gather(w, r.own, r.tiles, r.g_send, r.g_recv, pos) for w in range(2)]
    tiny = SmallGather(r.own_small, r.slots, r.kept, r.pair, r.gs_send, r.gs_recv, pos)
    tiny_sum = SmallScatter(r.small, r.s_pair, r.s_slots, r.s_held, r.rs_send, r.rs_recv, pos)
    g_in = [Piece(r, pos, t, t, 1, ORDERS[t][::-1]) for t in range(3)]
    g_out = Piece(r, pos, 3, 3, 1, ("x", "z", "y"))
    down_orders = (("z", "y", "x"), ("y", "z", "x"))

    def chunk(j):
        up = Piece(r, pos, 4 + j, 4 + j, 1, ("x", "y", "z"))
        down = Piece(r, pos, 8 + j, 8, 4, (), x=j, stages=())
        halves = [Piece(r, pos, 8 + 2 * j + n, 8 + 2 * n, 2, down_orders[n], x=j, stages=(0, 1)) for n in range(2)]
        return up, down, halves

    chunks = [chunk(j) for j in range(4)]
    g_up, g_down, g_halves = zip(*chunks, strict=True)
    g_last = Piece(r, pos, 16, 8, 4, ("z", "y", "x"), stages=(2,))
    for load in loads[:8]:
        load.wait()
    pack_own(r, pos)
    greeted(pos)

    gathers[0].start(0)
    tiny.start(0)
    gathers[1].start(0)
    for t in range(TILES):
        r.tiles[t, pos["x"], pos["c"], pos["y"], pos["z"]] = r.own[t]
    r.small[...] = jnp.zeros_like(r.small)
    gathers[0].arrive(0)
    gathers[0].start(1)
    tiny.arrive(0)
    tiny.start(1)
    gathers[1].arrive(0)
    gathers[1].start(1)
    gathers[0].arrive(1)
    gathers[0].start(2)
    tiny.arrive(1)
    tiny.start(2)
    tiny.arrive(2)
    gathers[0].arrive(2)
    gathers[1].arrive(1)
    gathers[1].start(2)
    tiny.arrive_pair(r.params)
    loads[8].wait()
    for i in range(2):
        first_norm(r, i)
    for t in range(3):
        gathers[0].arrive_pair(t)
    for t in range(3):
        unfold(r, t, r.w_qkv)
    for i in range(2):
        project(r, i)

    def forward(i):
        for hp in range(4):
            attend(r, i, hp)

    loop(2, forward)
    gathers[1].arrive(2)
    gathers[1].arrive_pair(0)
    unfold(r, 3, r.w_out)
    for i in range(2):
        second_norm(r, i)
    for part in (1, 2):
        gathers[1].arrive_pair(part)
    for t in range(4, 8):
        unfold(r, t, r.w_up)
    unfold_plain(r, r.w_down)
    for gather in gathers:
        gather.settle()
    tiny.settle()
    loads[9].wait()

    def leave(j):
        up, down, _ = chunk(j)
        up.pair_copy().start()
        down.pair_copy().start()

    def begin(j):
        up, down, halves = chunk(j)
        up.pair_add()
        down.pair_add()
        for piece in (up, *halves):
            piece.start(0)

    def turn(piece, stage):
        piece.add(stage)
        piece.start(stage + 1)

    def second(j):
        for piece in (g_up[j], *g_halves[j]):
            turn(piece, 0)

    def third(j):
        turn(g_up[j], 1)
        for piece in g_halves[j]:
            piece.add(1)

    feed_forward(r, 0)

    def middle(n):
        feed_forward(r, n + 1)
        chunk_gradients(r, n)
        leave(n)

        @pl.when(n > 0)
        def _():
            begin(n - 1)

    loop(3, middle)
    chunk_gradients(r, 3)
    leave(3)
    begin(2)
    second(0)
    second_norm_back(r, 0)
    second_norm_back(r, 1)
    begin(3)
    second(1)
    out_gradient(r)
    g_out.pair_copy().start()

    def backward(half):
        for n in range(4):
            attend_back(r, n % 2, half * 2 + n // 2)

        @pl.when(half == 0)
        def _():
            g_out.pair_add()
            g_out.start(0)
            second(2)
            third(0)
            in_gradient(r, 0)
            g_in[0].pair_copy().start()
            second(3)
            third(1)

    loop(2, backward)
    in_gradient(r, 1)
    g_in[1].pair_copy().start()
    g_in[0].pair_add()
    g_in[0].start(0)
    turn(g_out, 0)
    third(2)
    in_gradient(r, 2)
    g_in[2].pair_copy().start()
    g_in[1].pair_add()
    g_in[1].start(0)
    third(3)
    g_last.start(2)
    first_norm_back(r, 0)
    g_in[2].pair_add()
    g_in[2].start(0)
    first_norm_back(r, 1)
    tiny_sum.pair_copy().start()
    store_glat.start()
    turn(g_in[0], 0)
    turn(g_out, 1)
    tiny_sum.add_pair()
    tiny_sum.start(0)
    result_of(r, 0)
    result_of(r, 1)
    store_out.start()
    tiny_sum.add(0)
    tiny_sum.start(1)
    turn(g_in[2], 0)
    turn(g_in[1], 0)
    turn(g_in[0], 1)
    for piece in (*g_up, g_last):
        piece.add(2)
    tiny_sum.add(1)
    tiny_sum.start(2)
    turn(g_in[2], 1)
    turn(g_in[1], 1)
    g_out.add(2)
    g_in[0].add(2)
    for piece in (*g_in, g_out, *g_up, *g_down, *(half for halves in g_halves for half in halves), g_last):
        piece.settle()
    store_out.wait()
    store_glat.wait()
    g_in[1].add(2)
    g_in[2].add(2)
    tiny_sum.add(2)
    r.s_total[...] = r.s_held[6]
    tiny_sum.settle()


SHAPES = ((4, 18), (4, 4), (4, 1536), (4, 512), (2, 4), (4, 2048), (1, 16), (16, 512))


def finish(*refs):
    out_in, glat_in, total_hbm, small_hbm, out, glat, *rest = refs
    targets, (held, total, small), parts, (sems, load_sems, store_sems) = rest[:8], rest[8:11], rest[11:19], rest[19:]
    table, norms, w_in, w_out, biases, w_up, up_bias, w_down = parts
    loads = [
        pltpu.make_async_copy(total_hbm, total, load_sems.at[0]),
        pltpu.make_async_copy(small_hbm, small, load_sems.at[1]),
    ]
    for load in loads:
        load.start()
    reads, writes = [], []
    for n, (source, target) in enumerate(((out_in, out), (glat_in, glat))):
        for k in range(4):
            slot, rows = 4 * n + k, pl.ds(k % 2 * 256, 256)
            reads.append(pltpu.make_async_copy(source.at[k // 2, rows], held.at[slot], sems.at[0, slot]))
            writes.append(pltpu.make_async_copy(held.at[slot], target.at[k // 2, rows], sems.at[1, slot]))
    for read in reads:
        read.start()
    for load in loads:
        load.wait()
    for t, blocks in enumerate(COLUMNS):
        to = (w_in, w_out, w_up)[0 if t < 3 else 1 if t == 3 else 2]
        for q, ct in enumerate(blocks):
            to[:, ct * 128 : (ct + 1) * 128] = total[t, 4 * q : 4 * q + 4]
    for t in range(4):
        w_down[:, t * 128 : (t + 1) * 128] = total[8 + t]
    offset, bias_row, bias_offset = small_place(my_position())
    block = pltpu.roll(small[...], lax.rem(128 - offset, 128), 1)
    table[...] = jnp.concatenate((block, jnp.zeros((96, 128), F32))).T[0:4, 0:18]
    norms[...] = block[18:22, 0:4]
    biases[...] = block[22:24, 0:4]
    row = lax.broadcasted_iota(jnp.int32, (32, 1), 0)
    bias = jnp.sum(jnp.where(row == bias_row, small[...], 0.0), axis=0, keepdims=True)
    bias = pltpu.roll(jnp.broadcast_to(bias, (8, 128)), lax.rem(128 - bias_offset, 128), 1)
    up_bias[...] = bias[0:1, 0:16]
    stores = [
        pltpu.make_async_copy(part, target, store_sems.at[n])
        for n, (part, target) in enumerate(zip(parts, targets, strict=True))
    ]
    for store in stores:
        store.start()
    for read, write in zip(reads, writes, strict=True):
        read.wait()
        write.start()
    for copy in (*stores, *writes):
        copy.wait()


def whole(task_ids, counts, latents, cotangent, *raw):
    vmem = pl.BlockSpec(memory_space=pltpu.VMEM)
    smem = pl.BlockSpec(memory_space=pltpu.SMEM)
    hbm = pl.BlockSpec(memory_space=pl.ANY)
    array = jax.ShapeDtypeStruct(latents.shape, BF16)
    found = pl.pallas_call(
        kernel,
        out_shape=[
            array,
            array,
            jax.ShapeDtypeStruct((TILES, 16, 128), F32),
            jax.ShapeDtypeStruct((32, 128), F32),
        ],
        in_specs=[smem, smem] + [hbm] * (2 + len(RAW)),
        out_specs=[hbm, hbm, vmem, vmem],
        scratch_shapes=[pltpu.VMEM(shape, dtype) for shape, dtype in SCRATCH.values()]
        + [pltpu.SemaphoreType.DMA(shape) for shape in SEMAPHORES.values()],
        compiler_params=pltpu.CompilerParams(
            collective_id=0, has_side_effects=True, vmem_limit_bytes=121 * 2**19
        ),
    )(task_ids, counts, latents, cotangent, *raw)
    return pl.pallas_call(
        finish,
        out_shape=[array, array] + [jax.ShapeDtypeStruct(shape, F32) for shape in SHAPES],
        in_specs=[hbm] * 4,
        out_specs=[hbm] * 10,
        scratch_shapes=[
            pltpu.VMEM((8, 256, 512), BF16),
            pltpu.VMEM((TILES, 16, 128), F32),
            pltpu.VMEM((32, 128), F32),
            *(pltpu.VMEM(shape, F32) for shape in SHAPES),
            pltpu.SemaphoreType.DMA((2, 8)),
            pltpu.SemaphoreType.DMA((2,)),
            pltpu.SemaphoreType.DMA((8,)),
        ],
    )(*found)


def body(
    latents,
    task_ids,
    slot_counts,
    cotangent,
    task_embed,
    norms,
    attn_in,
    attn_out,
    out_biases,
    mlp_in,
    mlp_in_bias,
    mlp_out,
):
    raw = (attn_in, attn_out, mlp_in, mlp_out, task_embed.T, norms, out_biases, mlp_in_bias.reshape(1, 16))
    found = list(whole(task_ids, slot_counts, latents, cotangent, *raw))
    found[2] = found[2].T
    found[8] = found[8].reshape(16)
    return tuple(found)


def solution(mesh):
    in_specs = (
        P(("dp", "fsdp"), None, None),
        P(("dp", "fsdp")),
        P(("dp", "fsdp")),
        P(("dp", "fsdp"), None, None),
        P(None, ("dp", "fsdp")),
        P(None, ("dp", "fsdp")),
        P(("dp", "fsdp"), None),
        P(("dp", "fsdp"), None),
        P(None, ("dp", "fsdp")),
        P(("dp", "fsdp"), None),
        P(("dp", "fsdp")),
        P(("dp", "fsdp"), None),
    )
    out_specs = (
        P(("dp", "fsdp"), None, None),
        P(("dp", "fsdp"), None, None),
        P(None, ("dp", "fsdp")),
        P(None, ("dp", "fsdp")),
        P(("dp", "fsdp"), None),
        P(("dp", "fsdp"), None),
        P(None, ("dp", "fsdp")),
        P(("dp", "fsdp"), None),
        P(("dp", "fsdp")),
        P(("dp", "fsdp"), None),
    )
    return jax.shard_map(body, mesh=mesh, in_specs=in_specs, out_specs=out_specs, check_vma=False)
```

```python
import functools
import math

import jax
import jax.numpy as jnp
from jax import lax
from jax.experimental import pallas as pl
from jax.experimental.pallas import tpu as pltpu
from jax.sharding import PartitionSpec as P

HEADS = 8
EPS = 1e-05
BEST = lax.Precision.HIGHEST
MESH = pl.DeviceIdType.MESH
ALL = slice(None)
ORDERS = (("z", "y", "x"), ("y", "x", "z"), ("x", "z", "y"))
TILES = 12
WAVES = (((0, 1), (1, 1), (2, 1)), ((3, 3), (6, 3), (9, 3)))


def my_position():
    dp, fsdp = lax.axis_index("dp"), lax.axis_index("fsdp")
    return {
        "x": lax.div(dp, 2),
        "c": lax.rem(dp, 2),
        "y": lax.div(fsdp, 4),
        "z": lax.rem(fsdp, 4),
    }


def moved(pos, axis, step):
    size = 2 if axis == "c" else 4
    return {**pos, axis: lax.rem(pos[axis] + step, size)}


def device_of(pos):
    return (pos["x"] * 2 + pos["c"], pos["y"] * 4 + pos["z"])


def partners_of(pos):
    return [moved(pos, axis, k) for axis in "xyz" for k in (1, 2, 3)] + [moved(pos, "c", 1)]


def greet(pos):
    barrier = pltpu.get_barrier_semaphore()
    for other in partners_of(pos):
        pl.semaphore_signal(barrier, inc=1, device_id=device_of(other), device_id_type=MESH)


def greeted(pos):
    pl.semaphore_wait(pltpu.get_barrier_semaphore(), 10)


def remote(src, dst, send, recv, pos):
    return pltpu.make_async_remote_copy(
        src_ref=src, dst_ref=dst, send_sem=send, recv_sem=recv,
        device_id=device_of(pos), device_id_type=MESH,
    )


class Gather:
    def __init__(self, wave, own, tiles, send, recv, pos):
        self.wave, self.own, self.tiles, self.pos = wave, own, tiles, pos
        self.send, self.recv = send, recv

    def slab(self, part, free, at=None):
        first, count = WAVES[self.wave][part]
        place = {**self.pos, **(at or {})}
        index = [ALL if axis in free else place[axis] for axis in "xcyz"]
        return self.tiles.at[(pl.ds(first, count), *index)]

    def stage_copy(self, part, stage, k):
        order = ORDERS[part]
        slab = self.slab(part, order[:stage])
        src = slab
        if stage == 0:
            first, count = WAVES[self.wave][part]
            src = self.own.at[pl.ds(first, count)]
        slot = (self.wave, part, stage * 3 + k - 1)
        return remote(src, slab, self.send.at[slot], self.recv.at[slot], moved(self.pos, order[stage], k))

    def pair_copy(self, part, k):
        order = ORDERS[part]
        at = {order[2]: lax.rem(self.pos[order[2]] + 4 - k, 4)} if k else None
        slab = self.slab(part, order[:2], at)
        slot = (self.wave, part, 9 + k)
        return remote(slab, slab, self.send.at[slot], self.recv.at[slot], moved(self.pos, "c", 1))

    def start(self, stage):
        for part in range(3):
            for k in (2, 1, 3):
                self.stage_copy(part, stage, k).start()
            if stage == 2:
                self.pair_copy(part, 0).start()

    def arrive(self, stage):
        for part in range(3):
            for k in (1, 3, 2):
                self.stage_copy(part, stage, k).wait_recv()
                if stage == 2:
                    self.pair_copy(part, k).start()

    def arrive_pair(self, part):
        for k in range(4):
            self.pair_copy(part, k).wait_recv()

    def settle(self):
        for part in range(3):
            for stage in range(3):
                for k in (1, 2, 3):
                    self.stage_copy(part, stage, k).wait_send()
            for k in range(4):
                self.pair_copy(part, k).wait_send()


class SmallGather:
    def __init__(self, own, slots, kept, pair, send, recv, pos):
        self.own, self.slots, self.kept, self.pair = own, slots, kept, pair
        self.send, self.recv, self.pos = send, recv, pos

    def copy(self, stage, k):
        here = self.kept.at[self.pos["x"]]
        src = self.own if stage == 0 else here
        dst = here if stage == 2 else self.slots.at[stage, k - 1]
        slot = stage * 3 + k - 1
        return remote(src, dst, self.send.at[slot], self.recv.at[slot], moved(self.pos, "zyx"[stage], k))

    def pair_copy(self):
        return remote(self.kept, self.pair, self.send.at[9], self.recv.at[9], moved(self.pos, "c", 1))

    def start(self, stage):
        for k in (2, 1, 3):
            self.copy(stage, k).start()

    def arrive(self, stage):
        for k in (1, 3, 2):
            self.copy(stage, k).wait_recv()
        if stage == 2:
            self.pair_copy().start()
            return
        total = self.own[...] if stage == 0 else self.kept[self.pos["x"]]
        if stage == 1:
            for k in (1, 2, 3):
                self.copy(1, k).wait_send()
        for k in range(3):
            total = total + self.slots[stage, k]
        self.kept[self.pos["x"]] = total

    def arrive_pair(self, out):
        self.pair_copy().wait_recv()
        for x in range(4):
            out[:, x * 128 : (x + 1) * 128] = self.kept[x].astype(jnp.float32) + self.pair[x].astype(jnp.float32)

    def settle(self):
        for stage in (0, 2):
            for k in (1, 2, 3):
                self.copy(stage, k).wait_send()
        self.pair_copy().wait_send()


class Piece:
    def __init__(self, r, pos, number, first, count, order, x=None, stages=(0, 1, 2)):
        self.r, self.pos, self.number, self.first, self.count = r, pos, number, first, count
        self.order, self.x, self.stages = order, x, stages

    def span(self):
        return pl.ds(self.first, self.count)

    def pair_copy(self):
        other = moved(self.pos, "c", 1)
        x = ALL if self.x is None else self.x
        return remote(
            self.r.tiles.at[self.span(), x, other["c"]], self.r.from_pair.at[self.span(), x],
            self.r.p_send.at[self.number], self.r.p_recv.at[self.number], other,
        )

    def pair_add(self):
        self.pair_copy().wait_recv()
        core = self.pos["c"]
        for n in range(self.count):
            t = self.first + n
            for x in range(4) if self.x is None else (self.x,):
                total = self.r.tiles[t, x, core].astype(jnp.float32) + self.r.from_pair[t, x].astype(jnp.float32)
                self.r.tiles[t, x, core] = total.astype(jnp.bfloat16)

    def index(self, stage, place):
        held = self.order[: stage + 1]
        found = []
        for axis in "xcyz":
            if axis == "c" or axis in held:
                found.append(place[axis])
            else:
                found.append(self.x if axis == "x" and self.x is not None else ALL)
        return tuple(found)

    def left(self, stage):
        free = [axis for axis in "xyz" if axis not in self.order[: stage + 1]]
        return tuple(self.x if axis == "x" and self.x is not None else ALL for axis in free)

    def copy(self, stage, k):
        axis = self.order[stage]
        other = moved(self.pos, axis, k)
        src = self.r.tiles.at[(self.span(), *self.index(stage, other))]
        dst = (self.r.from1, self.r.from2, self.r.from3)[stage].at[(self.span(), k - 1, *self.left(stage))]
        slot = (self.number, stage * 3 + k - 1)
        return remote(src, dst, self.r.r_send.at[slot], self.r.r_recv.at[slot], other)

    def start(self, stage):
        for k in (2, 1, 3):
            self.copy(stage, k).start()

    def add(self, stage):
        for k in (1, 3, 2):
            self.copy(stage, k).wait_recv()
        index, left = self.index(stage, self.pos), self.left(stage)
        arrived = (self.r.from1, self.r.from2, self.r.from3)[stage]
        for n in range(self.count):
            t = self.first + n
            total = self.r.tiles[(t, *index)].astype(jnp.float32)
            for k in range(3):
                total = total + arrived[(t, k, *left)].astype(jnp.float32)
            if stage == 2:
                self.r.total[t] = total
            else:
                self.r.tiles[(t, *index)] = total.astype(jnp.bfloat16)

    def settle(self):
        if self.number < 12 and self.stages != (0, 1):
            self.pair_copy().wait_send()
        for stage in self.stages:
            for k in (1, 2, 3):
                self.copy(stage, k).wait_send()


class SmallScatter:
    def __init__(self, own, pair, slots, held, send, recv, pos):
        self.own, self.pair, self.slots, self.held = own, pair, slots, held
        self.send, self.recv, self.pos = send, recv, pos

    def pair_copy(self):
        return remote(self.own, self.pair, self.send.at[9], self.recv.at[9], moved(self.pos, "c", 1))

    def copy(self, stage, k):
        other = moved(self.pos, "xyz"[stage], k)
        src = self.held.at[other["x"]] if stage == 0 else self.held.at[3 + stage]
        slot = stage * 3 + k - 1
        return remote(src, self.slots.at[stage, k - 1], self.send.at[slot], self.recv.at[slot], other)

    def add_pair(self):
        self.pair_copy().wait_recv()
        self.held[0:4] = self.own[...] + self.pair[...]

    def start(self, stage):
        for k in (2, 1, 3):
            self.copy(stage, k).start()

    def add(self, stage):
        for k in (1, 3, 2):
            self.copy(stage, k).wait_recv()
        total = self.held[self.pos["x"]] if stage == 0 else self.held[3 + stage]
        for k in range(3):
            total = total + self.slots[stage, k]
        self.held[4 + stage] = total

    def settle(self):
        self.pair_copy().wait_send()
        for stage in range(3):
            for k in (1, 2, 3):
                self.copy(stage, k).wait_send()


COLUMNS = (
    (0, 4, 8, 1),
    (5, 9, 2, 6),
    (10, 3, 7, 11),
    (0, 1, 2, 3),
    *(tuple(range(4 * j, 4 * j + 4)) for j in range(4)),
)


def quarter_order(transposed=False):
    a = lax.broadcasted_iota(jnp.int32, (256, 256), 1 if transposed else 0)
    b = lax.broadcasted_iota(jnp.int32, (256, 256), 0 if transposed else 1)
    source = ((a % 64) // 4) * 16 + (a // 64) * 4 + a % 4
    return (source == b).astype(jnp.float32).astype(jnp.bfloat16)


def unfold(r, t, out):
    blocks = [r.tiles[t, xc // 2, xc % 2].reshape(256, 128) for xc in range(8)]
    rows = nn(quarter_order(), jnp.concatenate(blocks, 1)).astype(jnp.bfloat16)
    for q, ct in enumerate(COLUMNS[t]):
        for xc in range(8):
            out[xc * 64 : (xc + 1) * 64, ct * 128 : (ct + 1) * 128] = rows[q * 64 : (q + 1) * 64, xc * 128 : (xc + 1) * 128]


def unfold_plain(r, out):
    def one(i):
        x, c = lax.div(i, 2), lax.rem(i, 2)
        for t in range(4):
            out[pl.ds(pl.multiple_of(i * 256, 256), 256), t * 128 : (t + 1) * 128] = r.tiles[8 + t, x, c].reshape(256, 128)

    loop(8, one)


def fold(r, columns, t):
    rows = [jnp.concatenate([block[xc * 64 : (xc + 1) * 64] for xc in range(8)], 1) for block in columns]
    blocks = nn(quarter_order(True), jnp.concatenate(rows, 0)).astype(jnp.bfloat16)
    for xc in range(8):
        r.tiles[t, xc // 2, xc % 2] = blocks[:, xc * 128 : (xc + 1) * 128].reshape(4, 4, 16, 128)


def small_place(pos):
    ring = pos["y"] * 4 + pos["z"]
    return pos["c"] * 64 + ring * 4, 24 + pos["c"] * 2 + lax.div(ring, 8), 16 * lax.rem(ring, 8)


F32, BF16 = jnp.float32, jnp.bfloat16
GELU0 = math.sqrt(2.0 / math.pi)
GELU1 = GELU0 * 0.044715


def nn(a, b):
    return jnp.dot(a, b, preferred_element_type=F32)


def nt(a, b):
    return lax.dot_general(a, b, (((1,), (1,)), ((), ())), preferred_element_type=F32)


def tn(a, b):
    return lax.dot_general(a, b, (((0,), (0,)), ((), ())), preferred_element_type=F32)


def span_of(n, size):
    if isinstance(n, int):
        return slice(n * size, (n + 1) * size)
    return pl.ds(pl.multiple_of(n * size, size), size)


def rows_of(i):
    return span_of(i, 512)


def normalized(h):
    centred = h - jnp.mean(h, axis=-1, keepdims=True)
    factor = lax.rsqrt(jnp.mean(centred * centred, axis=-1, keepdims=True) + EPS)
    return centred * factor, factor


def normalized_back(grad, unit, factor, gain):
    scaled = grad * gain
    inner = jnp.mean(scaled, axis=-1, keepdims=True)
    along = jnp.mean(scaled * unit, axis=-1, keepdims=True)
    return factor * (scaled - inner - unit * along)


def column_sum(v):
    return jnp.sum(v, axis=0, keepdims=True)


def embedding(r, i):
    row = lax.broadcasted_iota(jnp.int32, (24, 1), 0)
    return column_sum(jnp.where(row == r.task_ids[i], r.params[0:24], 0.0))


def head_lanes(h):
    lane = lax.broadcasted_iota(jnp.int32, (1, 128), 1)
    return ((lane >= 64) == (h == 1)).astype(F32).astype(BF16)


def first_norm(r, i):
    unit, factor = normalized(r.lat[i].astype(F32) + embedding(r, i))
    r.a1[rows_of(i)] = (unit * r.params[18:19] + r.params[19:20]).astype(BF16)
    r.u1[rows_of(i)] = unit
    r.factors[rows_of(i), 0:1] = factor


def project(r, i):
    a1 = r.a1[rows_of(i)]
    for part in range(3):
        columns = slice(part * 512, (part + 1) * 512)
        result = nn(a1, r.w_qkv[:, columns])
        if part == 0:
            result = result * 0.125
        r.qkv[rows_of(i), columns] = result.astype(BF16)


def pair_of(r, i, hp, part):
    return r.qkv[rows_of(i), span_of(part * 4 + hp, 128)]


def attend(r, i, hp):
    q, k, v = (pair_of(r, i, hp, part) for part in range(3))
    slots = lax.broadcasted_iota(jnp.int32, (1, 512), 1)
    bias = jnp.where(slots < r.counts[i], 0.0, -1000000000.0)
    mixed = None
    for h in range(2):
        lanes = head_lanes(h)
        scores = nt(q, k * lanes) + bias
        expo = jnp.exp(scores - jnp.max(scores, axis=-1, keepdims=True)).astype(BF16)
        r.expo[i * 8 + hp * 2 + h] = expo
        wide = jnp.concatenate((v * lanes, jnp.broadcast_to(lanes, (512, 128))), 1)
        term = nn(expo, wide)
        mixed = term if mixed is None else mixed + term
    inverse = 1.0 / mixed[:, 128:]
    columns = span_of(hp, 128)
    r.inverse[rows_of(i), columns] = inverse
    mean = mixed[:, :128] * inverse
    r.o32[rows_of(i), columns] = mean
    r.o[rows_of(i), columns] = mean.astype(BF16)


def second_norm(r, i):
    h1 = r.lat[i].astype(F32) + embedding(r, i) + (nn(r.o[rows_of(i)], r.w_out[...]) + r.params[22:23])
    unit, factor = normalized(h1)
    r.a2[rows_of(i)] = (unit * r.params[20:21] + r.params[21:22]).astype(BF16)
    r.u2[rows_of(i)] = unit
    r.factors[rows_of(i), 1:2] = factor
    r.result[rows_of(i)] = h1


def feed_forward(r, j):
    units, tile = span_of(j, 512), span_of(j, 128)
    bias = jnp.concatenate([r.params[24 + m : 25 + m, tile] for m in range(4)], 1)
    sums = None
    for i in range(2):
        z = nn(r.a2[rows_of(i)], r.w_up[:, units]) + bias
        z2 = z * z
        half = 0.5 + 0.5 * jnp.tanh(z * (GELU0 + GELU1 * z2))
        act = (z * half).astype(BF16)
        slope = half + z * (2 * GELU0 + 6 * GELU1 * z2) * (half * (1.0 - half))
        gz = (nt(r.y[i], r.w_down[units, :]) * slope).astype(BF16)
        r.act[rows_of(i), units] = act
        r.gz[j % 2, rows_of(i)] = gz
        back = nt(gz, r.w_up[:, units])
        r.back[rows_of(i)] = back if isinstance(j, int) and j == 0 else r.back[rows_of(i)] + back
        total = column_sum(gz.astype(F32))
        sums = total if sums is None else sums + total
    for m in range(4):
        r.small[j, 24 + m : 25 + m] = sums[:, m * 128 : (m + 1) * 128]


def chunk_gradients(r, j):
    g_down = tn(r.act[:, span_of(j, 512)], r.y[...].reshape(1024, 512)).astype(BF16)
    for c in range(2):
        for t in range(4):
            r.tiles[8 + t, j, c] = g_down[c * 256 : (c + 1) * 256, t * 128 : (t + 1) * 128].reshape(4, 4, 16, 128)
    g_up = tn(r.a2[...], r.gz[j % 2]).astype(BF16)
    fold(r, [g_up[:, q * 128 : (q + 1) * 128] for q in range(4)], 4 + j)


def add_small(r, row, value):
    for x in range(4):
        r.small[x, row : row + 1] = r.small[x, row : row + 1] + value[:, x * 128 : (x + 1) * 128]


def second_norm_back(r, i):
    grad, unit = r.back[rows_of(i)], r.u2[rows_of(i)]
    add_small(r, 20, column_sum(grad * unit))
    add_small(r, 21, column_sum(grad))
    y = r.y[i].astype(F32)
    add_small(r, 23, column_sum(y))
    gh1 = y + normalized_back(grad, unit, r.factors[rows_of(i), 1:2], r.params[20:21])
    r.back[rows_of(i)] = gh1
    gb = gh1.astype(BF16)
    r.gb[rows_of(i)] = gb
    add_small(r, 22, column_sum(gb.astype(F32)))
    go = (nt(gb, r.w_out[...]) * r.inverse[rows_of(i)]).astype(BF16)
    r.go[rows_of(i)] = go
    product = go.astype(F32) * r.o32[rows_of(i)]
    high = product.astype(BF16).astype(F32)
    low = product - high
    first = lax.broadcasted_iota(jnp.int32, (1, 128), 1) < 64
    for hp in range(4):
        columns = slice(hp * 128, (hp + 1) * 128)
        swapped = pltpu.roll(low[:, columns], 64, 1)
        r.god0[rows_of(i), columns] = jnp.where(first, high[:, columns], swapped).astype(BF16)
        r.god1[rows_of(i), columns] = jnp.where(first, swapped, high[:, columns]).astype(BF16)


def out_gradient(r):
    g_out = tn(r.o[...], r.gb[...]).astype(BF16)
    fold(r, [g_out[:, q * 128 : (q + 1) * 128] for q in range(4)], 3)


def result_of(r, i):
    r.out[i] = (r.result[rows_of(i)] + nn(r.act[rows_of(i)], r.w_down[...]) + r.params[23:24]).astype(BF16)


def attend_back(r, i, hp):
    q, k, v = (pair_of(r, i, hp, part) for part in range(3))
    columns = span_of(hp, 128)
    go = r.go[rows_of(i), columns]
    gq = gk = gv = 0.0
    for h in range(2):
        lanes = head_lanes(h)
        both = jnp.concatenate((go, (r.god0, r.god1)[h][rows_of(i), columns]), 1)
        wide = jnp.concatenate((v * lanes, jnp.full((512, 128), -1.0, BF16)), 1)
        expo = r.expo[i * 8 + hp * 2 + h]
        gs = (expo.astype(F32) * nt(both, wide)).astype(BF16)
        gq = gq + nn(gs, k * lanes)
        gk = gk + tn(gs, q * lanes)
        gv = gv + tn(expo, go * lanes)
    for part, value in enumerate((gq * 0.125, gk, gv)):
        r.gqkv[i][part][:, span_of(hp, 128)] = value.astype(BF16)


def first_norm_back(r, i):
    grad, unit = nt(jnp.concatenate([part[...] for part in r.gqkv[i]], 1), r.w_qkv[...]), r.u1[rows_of(i)]
    add_small(r, 18, column_sum(grad * unit))
    add_small(r, 19, column_sum(grad))
    gh0 = r.back[rows_of(i)] + normalized_back(grad, unit, r.factors[rows_of(i), 0:1], r.params[18:19])
    r.glat[i] = gh0.astype(BF16)
    total = column_sum(gh0)
    row = lax.broadcasted_iota(jnp.int32, (18, 1), 0)
    for x in range(4):
        mine = jnp.where(row == r.task_ids[i], total[:, x * 128 : (x + 1) * 128], 0.0)
        r.small[x, 0:18] = r.small[x, 0:18] + mine


def in_gradient(r, t):
    columns = jnp.concatenate(
        [jnp.concatenate([r.gqkv[i][ct // 4][:, span_of(ct % 4, 128)] for ct in COLUMNS[t]], 1) for i in range(2)]
    )
    g_in = tn(r.a1[...], columns).astype(BF16)
    fold(r, [g_in[:, q * 128 : (q + 1) * 128] for q in range(4)], t)


class Refs:
    def __init__(self, names, refs):
        for name, ref in zip(names, refs, strict=True):
            setattr(self, name, ref)


RAW = {
    "raw_in": ((4, 1536), BF16),
    "raw_out": ((4, 512), BF16),
    "raw_up": ((4, 2048), BF16),
    "raw_down": ((16, 512), BF16),
    "raw_table": ((4, 18), BF16),
    "raw_norms": ((4, 4), BF16),
    "raw_biases": ((2, 4), BF16),
    "raw_up_bias": ((1, 16), BF16),
}
INPUTS = ("task_ids", "counts", "lat_hbm", "y_hbm", *(f"{name}_hbm" for name in RAW))
OUTPUTS = ("out_hbm", "glat_hbm", "total", "s_total")
BLOCKS = (TILES, 4, 2, 4, 4, 16, 128)
SCRATCH = {
    **RAW,
    "own32": ((TILES, 16, 128), F32),
    "own": ((TILES, 16, 128), BF16),
    "small32": ((40, 128), F32),
    "table32": ((128, 128), F32),
    "own_small": ((32, 128), BF16),
    "lat": ((2, 512, 512), BF16),
    "y": ((2, 512, 512), BF16),
    "w_qkv": ((512, 1536), BF16),
    "w_out": ((512, 512), BF16),
    "w_up": ((512, 2048), BF16),
    "w_down": ((2048, 512), BF16),
    "params": ((32, 512), F32),
    "a1": ((1024, 512), BF16),
    "u1": ((1024, 512), F32),
    "qkv": ((1024, 1536), BF16),
    "expo": ((16, 512, 512), BF16),
    "o": ((1024, 512), BF16),
    "o32": ((1024, 512), F32),
    "inverse": ((1024, 512), F32),
    "result": ((1024, 512), F32),
    "a2": ((1024, 512), BF16),
    "u2": ((1024, 512), F32),
    "factors": ((1024, 2), F32),
    "act": ((1024, 2048), BF16),
    "gz": ((2, 1024, 512), BF16),
    "back": ((1024, 512), F32),
    "gb": ((1024, 512), BF16),
    "small": ((4, 32, 128), F32),
    "tiles": (BLOCKS, BF16),
    "slots": ((2, 3, 32, 128), BF16),
    "kept": ((4, 32, 128), BF16),
    "pair": ((4, 32, 128), BF16),
    "from_pair": ((TILES, 4, 4, 4, 16, 128), BF16),
    "from1": ((TILES, 3, 4, 4, 16, 128), BF16),
    "from2": ((TILES, 3, 4, 16, 128), BF16),
    "from3": ((TILES, 3, 16, 128), BF16),
    "s_pair": ((4, 32, 128), F32),
    "s_slots": ((3, 3, 32, 128), F32),
    "s_held": ((7, 32, 128), F32),
}
SEMAPHORES = {
    "g_send": (2, 3, 13),
    "g_recv": (2, 3, 13),
    "gs_send": (10,),
    "gs_recv": (10,),
    "p_send": (12,),
    "p_recv": (12,),
    "r_send": (17, 9),
    "r_recv": (17, 9),
    "rs_send": (10,),
    "rs_recv": (10,),
    "local": (12,),
}


def alias(r):
    r.go, r.god0, r.god1 = r.gz.at[0], r.gz.at[1], r.a2
    r.out, r.glat = r.lat, r.y
    r.gqkv = [r.w_up.at[:, span_of(part, 512)] for part in range(3)], [r.lat.at[0], r.lat.at[1], r.w_out]


def loop(count, step):
    lax.fori_loop(0, count, lambda n, carry: (step(n), carry)[1], 0)


def pack_own(r, pos):
    for t, blocks in enumerate(COLUMNS):
        raw = (r.raw_in, r.raw_out, r.raw_up)[0 if t < 3 else 1 if t == 3 else 2]
        for q, ct in enumerate(blocks):
            r.own32[t, 4 * q : 4 * q + 4] = raw[:, ct * 128 : (ct + 1) * 128].astype(F32)
    for t in range(8):
        r.own[t] = r.own32[t].astype(BF16)
    for t in range(4):
        r.own[8 + t] = r.raw_down[:, t * 128 : (t + 1) * 128]
    r.small32[...] = jnp.zeros_like(r.small32)
    r.table32[...] = jnp.zeros_like(r.table32)
    r.table32[0:4, 0:18] = r.raw_table[...].astype(F32)
    r.small32[18:22, 0:4] = r.raw_norms[...].astype(F32)
    r.small32[22:24, 0:4] = r.raw_biases[...].astype(F32)
    r.small32[32:33, 0:16] = r.raw_up_bias[...].astype(F32)
    offset, bias_row, bias_offset = small_place(pos)
    block = pltpu.roll(r.small32[0:32] + r.table32[...].T[0:32], offset, 1)
    bias = pltpu.roll(r.small32[32:40], bias_offset, 1)[0:1]
    row = lax.broadcasted_iota(jnp.int32, (32, 1), 0)
    r.own_small[...] = (block + jnp.where(row == bias_row, bias, 0.0)).astype(BF16)


def kernel(*refs):
    r = Refs((*INPUTS, *OUTPUTS, *SCRATCH, *SEMAPHORES), refs)
    alias(r)
    pos = my_position()
    loads = [
        pltpu.make_async_copy(getattr(r, f"{name}_hbm"), getattr(r, name), r.local.at[n])
        for n, name in enumerate((*RAW, "lat", "y"))
    ]
    store_out = pltpu.make_async_copy(r.out, r.out_hbm, r.local.at[10])
    store_glat = pltpu.make_async_copy(r.glat, r.glat_hbm, r.local.at[11])
    greet(pos)
    for load in loads:
        load.start()
    gathers = [Gather(w, r.own, r.tiles, r.g_send, r.g_recv, pos) for w in range(2)]
    tiny = SmallGather(r.own_small, r.slots, r.kept, r.pair, r.gs_send, r.gs_recv, pos)
    tiny_sum = SmallScatter(r.small, r.s_pair, r.s_slots, r.s_held, r.rs_send, r.rs_recv, pos)
    g_in = [Piece(r, pos, t, t, 1, ORDERS[t][::-1]) for t in range(3)]
    g_out = Piece(r, pos, 3, 3, 1, ("x", "z", "y"))
    down_orders = (("z", "y", "x"), ("y", "z", "x"))

    def chunk(j):
        up = Piece(r, pos, 4 + j, 4 + j, 1, ("x", "y", "z"))
        down = Piece(r, pos, 8 + j, 8, 4, (), x=j, stages=())
        halves = [Piece(r, pos, 8 + 2 * j + n, 8 + 2 * n, 2, down_orders[n], x=j, stages=(0, 1)) for n in range(2)]
        return up, down, halves

    chunks = [chunk(j) for j in range(4)]
    g_up, g_down, g_halves = zip(*chunks, strict=True)
    g_last = Piece(r, pos, 16, 8, 4, ("z", "y", "x"), stages=(2,))
    for load in loads[:8]:
        load.wait()
    pack_own(r, pos)
    greeted(pos)

    gathers[0].start(0)
    tiny.start(0)
    gathers[1].start(0)
    for t in range(TILES):
        r.tiles[t, pos["x"], pos["c"], pos["y"], pos["z"]] = r.own[t]
    r.small[...] = jnp.zeros_like(r.small)
    gathers[0].arrive(0)
    gathers[0].start(1)
    tiny.arrive(0)
    tiny.start(1)
    gathers[1].arrive(0)
    gathers[1].start(1)
    gathers[0].arrive(1)
    gathers[0].start(2)
    tiny.arrive(1)
    tiny.start(2)
    tiny.arrive(2)
    gathers[0].arrive(2)
    gathers[1].arrive(1)
    gathers[1].start(2)
    tiny.arrive_pair(r.params)
    loads[8].wait()
    for i in range(2):
        first_norm(r, i)
    for t in range(3):
        gathers[0].arrive_pair(t)
    for t in range(3):
        unfold(r, t, r.w_qkv)
    loop(2, lambda i: project(r, i))

    for n in range(8):
        attend(r, n // 4, n % 4)
    gathers[1].arrive(2)
    gathers[1].arrive_pair(0)
    unfold(r, 3, r.w_out)
    for i in range(2):
        second_norm(r, i)
    for part in (1, 2):
        gathers[1].arrive_pair(part)
    for t in range(4, 8):
        unfold(r, t, r.w_up)
    unfold_plain(r, r.w_down)
    for gather in gathers:
        gather.settle()
    tiny.settle()
    loads[9].wait()

    def leave(j):
        up, down, _ = chunk(j)
        up.pair_copy().start()
        down.pair_copy().start()

    def begin(j):
        up, down, halves = chunk(j)
        up.pair_add()
        down.pair_add()
        for piece in (up, *halves):
            piece.start(0)

    def turn(piece, stage):
        piece.add(stage)
        piece.start(stage + 1)

    def second(j):
        for piece in (g_up[j], *g_halves[j]):
            turn(piece, 0)

    def third(j):
        turn(g_up[j], 1)
        for piece in g_halves[j]:
            piece.add(1)

    r.back[...] = jnp.zeros_like(r.back)

    def middle(j):
        feed_forward(r, j)
        chunk_gradients(r, j)
        leave(j)

        @pl.when(j > 0)
        def _():
            begin(j - 1)

    loop(4, middle)
    second(0)
    loop(2, lambda i: second_norm_back(r, i))
    begin(3)
    second(1)
    out_gradient(r)
    g_out.pair_copy().start()

    def backward(half):
        for n in range(4):
            attend_back(r, n % 2, half * 2 + n // 2)

        @pl.when(half == 0)
        def _():
            g_out.pair_add()
            g_out.start(0)
            second(2)
            third(0)
            in_gradient(r, 0)
            g_in[0].pair_copy().start()
            second(3)
            third(1)

    loop(2, backward)
    in_gradient(r, 1)
    g_in[1].pair_copy().start()
    g_in[0].pair_add()
    g_in[0].start(0)
    turn(g_out, 0)
    third(2)
    in_gradient(r, 2)
    g_in[2].pair_copy().start()
    g_in[1].pair_add()
    g_in[1].start(0)
    third(3)
    g_last.start(2)
    first_norm_back(r, 0)
    g_in[2].pair_add()
    g_in[2].start(0)
    first_norm_back(r, 1)
    tiny_sum.pair_copy().start()
    store_glat.start()
    turn(g_in[0], 0)
    turn(g_out, 1)
    tiny_sum.add_pair()
    tiny_sum.start(0)
    loop(2, lambda i: result_of(r, i))
    store_out.start()
    tiny_sum.add(0)
    tiny_sum.start(1)
    turn(g_in[2], 0)
    turn(g_in[1], 0)
    turn(g_in[0], 1)
    for piece in (*g_up, g_last):
        piece.add(2)
    tiny_sum.add(1)
    tiny_sum.start(2)
    turn(g_in[2], 1)
    turn(g_in[1], 1)
    g_out.add(2)
    g_in[0].add(2)
    for piece in (*g_in, g_out, *g_up, *g_down, *(half for halves in g_halves for half in halves), g_last):
        piece.settle()
    store_out.wait()
    store_glat.wait()
    g_in[1].add(2)
    g_in[2].add(2)
    tiny_sum.add(2)
    r.s_total[...] = r.s_held[6]
    tiny_sum.settle()


SHAPES = ((4, 18), (4, 4), (4, 1536), (4, 512), (2, 4), (4, 2048), (1, 16), (16, 512))


def finish(*refs):
    out_in, glat_in, total_hbm, small_hbm, out, glat, *rest = refs
    targets, (held, total, small), parts, (sems, load_sems, store_sems) = rest[:8], rest[8:11], rest[11:19], rest[19:]
    table, norms, w_in, w_out, biases, w_up, up_bias, w_down = parts
    loads = [
        pltpu.make_async_copy(total_hbm, total, load_sems.at[0]),
        pltpu.make_async_copy(small_hbm, small, load_sems.at[1]),
    ]
    for load in loads:
        load.start()
    reads, writes = [], []
    for n, (source, target) in enumerate(((out_in, out), (glat_in, glat))):
        for k in range(4):
            slot, rows = 4 * n + k, pl.ds(k % 2 * 256, 256)
            reads.append(pltpu.make_async_copy(source.at[k // 2, rows], held.at[slot], sems.at[0, slot]))
            writes.append(pltpu.make_async_copy(held.at[slot], target.at[k // 2, rows], sems.at[1, slot]))
    for read in reads:
        read.start()
    for load in loads:
        load.wait()
    for t, blocks in enumerate(COLUMNS):
        to = (w_in, w_out, w_up)[0 if t < 3 else 1 if t == 3 else 2]
        for q, ct in enumerate(blocks):
            to[:, ct * 128 : (ct + 1) * 128] = total[t, 4 * q : 4 * q + 4]
    for t in range(4):
        w_down[:, t * 128 : (t + 1) * 128] = total[8 + t]
    offset, bias_row, bias_offset = small_place(my_position())
    block = pltpu.roll(small[...], lax.rem(128 - offset, 128), 1)
    table[...] = jnp.concatenate((block, jnp.zeros((96, 128), F32))).T[0:4, 0:18]
    norms[...] = block[18:22, 0:4]
    biases[...] = block[22:24, 0:4]
    row = lax.broadcasted_iota(jnp.int32, (32, 1), 0)
    bias = jnp.sum(jnp.where(row == bias_row, small[...], 0.0), axis=0, keepdims=True)
    bias = pltpu.roll(jnp.broadcast_to(bias, (8, 128)), lax.rem(128 - bias_offset, 128), 1)
    up_bias[...] = bias[0:1, 0:16]
    stores = [
        pltpu.make_async_copy(part, target, store_sems.at[n])
        for n, (part, target) in enumerate(zip(parts, targets, strict=True))
    ]
    for store in stores:
        store.start()
    for read, write in zip(reads, writes, strict=True):
        read.wait()
        write.start()
    for copy in (*stores, *writes):
        copy.wait()


def whole(task_ids, counts, latents, cotangent, *raw):
    vmem = pl.BlockSpec(memory_space=pltpu.VMEM)
    smem = pl.BlockSpec(memory_space=pltpu.SMEM)
    hbm = pl.BlockSpec(memory_space=pl.ANY)
    array = jax.ShapeDtypeStruct(latents.shape, BF16)
    found = pl.pallas_call(
        kernel,
        out_shape=[
            array,
            array,
            jax.ShapeDtypeStruct((TILES, 16, 128), F32),
            jax.ShapeDtypeStruct((32, 128), F32),
        ],
        in_specs=[smem, smem] + [hbm] * (2 + len(RAW)),
        out_specs=[hbm, hbm, vmem, vmem],
        scratch_shapes=[pltpu.VMEM(shape, dtype) for shape, dtype in SCRATCH.values()]
        + [pltpu.SemaphoreType.DMA(shape) for shape in SEMAPHORES.values()],
        compiler_params=pltpu.CompilerParams(
            collective_id=0, has_side_effects=True, vmem_limit_bytes=121 * 2**19
        ),
    )(task_ids, counts, latents, cotangent, *raw)
    return pl.pallas_call(
        finish,
        out_shape=[array, array] + [jax.ShapeDtypeStruct(shape, F32) for shape in SHAPES],
        in_specs=[hbm] * 4,
        out_specs=[hbm] * 10,
        scratch_shapes=[
            pltpu.VMEM((8, 256, 512), BF16),
            pltpu.VMEM((TILES, 16, 128), F32),
            pltpu.VMEM((32, 128), F32),
            *(pltpu.VMEM(shape, F32) for shape in SHAPES),
            pltpu.SemaphoreType.DMA((2, 8)),
            pltpu.SemaphoreType.DMA((2,)),
            pltpu.SemaphoreType.DMA((8,)),
        ],
    )(*found)


def body(
    latents,
    task_ids,
    slot_counts,
    cotangent,
    task_embed,
    norms,
    attn_in,
    attn_out,
    out_biases,
    mlp_in,
    mlp_in_bias,
    mlp_out,
):
    raw = (attn_in, attn_out, mlp_in, mlp_out, task_embed.T, norms, out_biases, mlp_in_bias.reshape(1, 16))
    found = list(whole(task_ids, slot_counts, latents, cotangent, *raw))
    found[2] = found[2].T
    found[8] = found[8].reshape(16)
    return tuple(found)


def solution(mesh):
    in_specs = (
        P(("dp", "fsdp"), None, None),
        P(("dp", "fsdp")),
        P(("dp", "fsdp")),
        P(("dp", "fsdp"), None, None),
        P(None, ("dp", "fsdp")),
        P(None, ("dp", "fsdp")),
        P(("dp", "fsdp"), None),
        P(("dp", "fsdp"), None),
        P(None, ("dp", "fsdp")),
        P(("dp", "fsdp"), None),
        P(("dp", "fsdp")),
        P(("dp", "fsdp"), None),
    )
    out_specs = (
        P(("dp", "fsdp"), None, None),
        P(("dp", "fsdp"), None, None),
        P(None, ("dp", "fsdp")),
        P(None, ("dp", "fsdp")),
        P(("dp", "fsdp"), None),
        P(("dp", "fsdp"), None),
        P(None, ("dp", "fsdp")),
        P(("dp", "fsdp"), None),
        P(("dp", "fsdp")),
        P(("dp", "fsdp"), None),
    )
    return jax.shard_map(body, mesh=mesh, in_specs=in_specs, out_specs=out_specs, check_vma=False)
```

```python
import functools
import math

import jax
import jax.numpy as jnp
from jax import lax
from jax.experimental import pallas as pl
from jax.experimental.pallas import tpu as pltpu
from jax.sharding import PartitionSpec as P

HEADS = 8
EPS = 1e-05
BEST = lax.Precision.HIGHEST
MESH = pl.DeviceIdType.MESH
ALL = slice(None)
ORDERS = (("z", "y", "x"), ("y", "x", "z"), ("x", "z", "y"))
TILES = 12
WAVES = (((0, 1), (1, 1), (2, 1)), ((3, 3), (6, 3), (9, 3)))


def my_position():
    dp, fsdp = lax.axis_index("dp"), lax.axis_index("fsdp")
    return {
        "x": lax.div(dp, 2),
        "c": lax.rem(dp, 2),
        "y": lax.div(fsdp, 4),
        "z": lax.rem(fsdp, 4),
    }


def moved(pos, axis, step):
    size = 2 if axis == "c" else 4
    return {**pos, axis: lax.rem(pos[axis] + step, size)}


def device_of(pos):
    return (pos["x"] * 2 + pos["c"], pos["y"] * 4 + pos["z"])


def partners_of(pos):
    return [moved(pos, axis, k) for axis in "xyz" for k in (1, 2, 3)] + [moved(pos, "c", 1)]


def greet(pos):
    barrier = pltpu.get_barrier_semaphore()
    for other in partners_of(pos):
        pl.semaphore_signal(barrier, inc=1, device_id=device_of(other), device_id_type=MESH)


def greeted(pos):
    pl.semaphore_wait(pltpu.get_barrier_semaphore(), 10)


def remote(src, dst, send, recv, pos):
    return pltpu.make_async_remote_copy(
        src_ref=src, dst_ref=dst, send_sem=send, recv_sem=recv,
        device_id=device_of(pos), device_id_type=MESH,
    )


class Gather:
    def __init__(self, wave, own, tiles, send, recv, pos):
        self.wave, self.own, self.tiles, self.pos = wave, own, tiles, pos
        self.send, self.recv = send, recv

    def slab(self, part, free, at=None):
        first, count = WAVES[self.wave][part]
        place = {**self.pos, **(at or {})}
        index = [ALL if axis in free else place[axis] for axis in "xcyz"]
        return self.tiles.at[(pl.ds(first, count), *index)]

    def stage_copy(self, part, stage, k):
        order = ORDERS[part]
        slab = self.slab(part, order[:stage])
        src = slab
        if stage == 0:
            first, count = WAVES[self.wave][part]
            src = self.own.at[pl.ds(first, count)]
        slot = (self.wave, part, stage * 3 + k - 1)
        return remote(src, slab, self.send.at[slot], self.recv.at[slot], moved(self.pos, order[stage], k))

    def pair_copy(self, part, k):
        order = ORDERS[part]
        at = {order[2]: lax.rem(self.pos[order[2]] + 4 - k, 4)} if k else None
        slab = self.slab(part, order[:2], at)
        slot = (self.wave, part, 9 + k)
        return remote(slab, slab, self.send.at[slot], self.recv.at[slot], moved(self.pos, "c", 1))

    def start(self, stage):
        for part in range(3):
            for k in (2, 1, 3):
                self.stage_copy(part, stage, k).start()
            if stage == 2:
                self.pair_copy(part, 0).start()

    def arrive(self, stage):
        for part in range(3):
            for k in (1, 3, 2):
                self.stage_copy(part, stage, k).wait_recv()
                if stage == 2:
                    self.pair_copy(part, k).start()

    def arrive_pair(self, part):
        for k in range(4):
            self.pair_copy(part, k).wait_recv()

    def settle(self):
        for part in range(3):
            for stage in range(3):
                for k in (1, 2, 3):
                    self.stage_copy(part, stage, k).wait_send()
            for k in range(4):
                self.pair_copy(part, k).wait_send()


class SmallGather:
    def __init__(self, own, slots, kept, pair, send, recv, pos):
        self.own, self.slots, self.kept, self.pair = own, slots, kept, pair
        self.send, self.recv, self.pos = send, recv, pos

    def copy(self, stage, k):
        here = self.kept.at[self.pos["x"]]
        src = self.own if stage == 0 else here
        dst = here if stage == 2 else self.slots.at[stage, k - 1]
        slot = stage * 3 + k - 1
        return remote(src, dst, self.send.at[slot], self.recv.at[slot], moved(self.pos, "zyx"[stage], k))

    def pair_copy(self):
        return remote(self.kept, self.pair, self.send.at[9], self.recv.at[9], moved(self.pos, "c", 1))

    def start(self, stage):
        for k in (2, 1, 3):
            self.copy(stage, k).start()

    def arrive(self, stage):
        for k in (1, 3, 2):
            self.copy(stage, k).wait_recv()
        if stage == 2:
            self.pair_copy().start()
            return
        total = self.own[...] if stage == 0 else self.kept[self.pos["x"]]
        if stage == 1:
            for k in (1, 2, 3):
                self.copy(1, k).wait_send()
        for k in range(3):
            total = total + self.slots[stage, k]
        self.kept[self.pos["x"]] = total

    def arrive_pair(self, out):
        self.pair_copy().wait_recv()
        for x in range(4):
            out[:, x * 128 : (x + 1) * 128] = self.kept[x].astype(jnp.float32) + self.pair[x].astype(jnp.float32)

    def settle(self):
        for stage in (0, 2):
            for k in (1, 2, 3):
                self.copy(stage, k).wait_send()
        self.pair_copy().wait_send()


class Piece:
    def __init__(self, r, pos, number, first, count, order, x=None, stages=(0, 1, 2)):
        self.r, self.pos, self.number, self.first, self.count = r, pos, number, first, count
        self.order, self.x, self.stages = order, x, stages

    def span(self):
        return pl.ds(self.first, self.count)

    def pair_copy(self):
        other = moved(self.pos, "c", 1)
        x = ALL if self.x is None else self.x
        return remote(
            self.r.tiles.at[self.span(), x, other["c"]], self.r.from_pair.at[self.span(), x],
            self.r.p_send.at[self.number], self.r.p_recv.at[self.number], other,
        )

    def pair_add(self):
        self.pair_copy().wait_recv()
        core = self.pos["c"]
        for n in range(self.count):
            t = self.first + n
            for x in range(4) if self.x is None else (self.x,):
                total = self.r.tiles[t, x, core].astype(jnp.float32) + self.r.from_pair[t, x].astype(jnp.float32)
                self.r.tiles[t, x, core] = total.astype(jnp.bfloat16)

    def index(self, stage, place):
        held = self.order[: stage + 1]
        found = []
        for axis in "xcyz":
            if axis == "c" or axis in held:
                found.append(place[axis])
            else:
                found.append(self.x if axis == "x" and self.x is not None else ALL)
        return tuple(found)

    def left(self, stage):
        free = [axis for axis in "xyz" if axis not in self.order[: stage + 1]]
        return tuple(self.x if axis == "x" and self.x is not None else ALL for axis in free)

    def copy(self, stage, k):
        axis = self.order[stage]
        other = moved(self.pos, axis, k)
        src = self.r.tiles.at[(self.span(), *self.index(stage, other))]
        dst = (self.r.from1, self.r.from2, self.r.from3)[stage].at[(self.span(), k - 1, *self.left(stage))]
        slot = (self.number, stage * 3 + k - 1)
        return remote(src, dst, self.r.r_send.at[slot], self.r.r_recv.at[slot], other)

    def start(self, stage):
        for k in (2, 1, 3):
            self.copy(stage, k).start()

    def add(self, stage):
        for k in (1, 3, 2):
            self.copy(stage, k).wait_recv()
        index, left = self.index(stage, self.pos), self.left(stage)
        arrived = (self.r.from1, self.r.from2, self.r.from3)[stage]
        for n in range(self.count):
            t = self.first + n
            total = self.r.tiles[(t, *index)].astype(jnp.float32)
            for k in range(3):
                total = total + arrived[(t, k, *left)].astype(jnp.float32)
            if stage == 2:
                self.r.total[t] = total
            else:
                self.r.tiles[(t, *index)] = total.astype(jnp.bfloat16)

    def settle(self):
        if self.number < 12 and self.stages != (0, 1):
            self.pair_copy().wait_send()
        for stage in self.stages:
            for k in (1, 2, 3):
                self.copy(stage, k).wait_send()


class SmallScatter:
    def __init__(self, own, pair, slots, held, send, recv, pos):
        self.own, self.pair, self.slots, self.held = own, pair, slots, held
        self.send, self.recv, self.pos = send, recv, pos

    def pair_copy(self):
        return remote(self.own, self.pair, self.send.at[9], self.recv.at[9], moved(self.pos, "c", 1))

    def copy(self, stage, k):
        other = moved(self.pos, "xyz"[stage], k)
        src = self.held.at[other["x"]] if stage == 0 else self.held.at[3 + stage]
        slot = stage * 3 + k - 1
        return remote(src, self.slots.at[stage, k - 1], self.send.at[slot], self.recv.at[slot], other)

    def add_pair(self):
        self.pair_copy().wait_recv()
        self.held[0:4] = self.own[...] + self.pair[...]

    def start(self, stage):
        for k in (2, 1, 3):
            self.copy(stage, k).start()

    def add(self, stage):
        for k in (1, 3, 2):
            self.copy(stage, k).wait_recv()
        total = self.held[self.pos["x"]] if stage == 0 else self.held[3 + stage]
        for k in range(3):
            total = total + self.slots[stage, k]
        self.held[4 + stage] = total

    def settle(self):
        self.pair_copy().wait_send()
        for stage in range(3):
            for k in (1, 2, 3):
                self.copy(stage, k).wait_send()


COLUMNS = (
    (0, 4, 8, 1),
    (5, 9, 2, 6),
    (10, 3, 7, 11),
    (0, 1, 2, 3),
    *(tuple(range(4 * j, 4 * j + 4)) for j in range(4)),
)


def quarter_order(transposed=False):
    a = lax.broadcasted_iota(jnp.int32, (256, 256), 1 if transposed else 0)
    b = lax.broadcasted_iota(jnp.int32, (256, 256), 0 if transposed else 1)
    source = ((a % 64) // 4) * 16 + (a // 64) * 4 + a % 4
    return (source == b).astype(jnp.float32).astype(jnp.bfloat16)


def unfold(r, t, out):
    blocks = [r.tiles[t, xc // 2, xc % 2].reshape(256, 128) for xc in range(8)]
    rows = nn(quarter_order(), jnp.concatenate(blocks, 1)).astype(jnp.bfloat16)
    for q, ct in enumerate(COLUMNS[t]):
        for xc in range(8):
            out[xc * 64 : (xc + 1) * 64, ct * 128 : (ct + 1) * 128] = rows[q * 64 : (q + 1) * 64, xc * 128 : (xc + 1) * 128]


def unfold_plain(r, out):
    def one(i):
        x, c = lax.div(i, 2), lax.rem(i, 2)
        for t in range(4):
            out[pl.ds(pl.multiple_of(i * 256, 256), 256), t * 128 : (t + 1) * 128] = r.tiles[8 + t, x, c].reshape(256, 128)

    loop(8, one)


def fold(r, columns, t):
    rows = [jnp.concatenate([block[xc * 64 : (xc + 1) * 64] for xc in range(8)], 1) for block in columns]
    blocks = nn(quarter_order(True), jnp.concatenate(rows, 0)).astype(jnp.bfloat16)
    for xc in range(8):
        r.tiles[t, xc // 2, xc % 2] = blocks[:, xc * 128 : (xc + 1) * 128].reshape(4, 4, 16, 128)


def small_place(pos):
    ring = pos["y"] * 4 + pos["z"]
    return pos["c"] * 64 + ring * 4, 24 + pos["c"] * 2 + lax.div(ring, 8), 16 * lax.rem(ring, 8)


F32, BF16 = jnp.float32, jnp.bfloat16
GELU0 = math.sqrt(2.0 / math.pi)
GELU1 = GELU0 * 0.044715


def nn(a, b):
    return jnp.dot(a, b, preferred_element_type=F32)


def nt(a, b):
    return lax.dot_general(a, b, (((1,), (1,)), ((), ())), preferred_element_type=F32)


def tn(a, b):
    return lax.dot_general(a, b, (((0,), (0,)), ((), ())), preferred_element_type=F32)


def span_of(n, size):
    if isinstance(n, int):
        return slice(n * size, (n + 1) * size)
    return pl.ds(pl.multiple_of(n * size, size), size)


def rows_of(i):
    return span_of(i, 512)


def normalized(h):
    centred = h - jnp.mean(h, axis=-1, keepdims=True)
    factor = lax.rsqrt(jnp.mean(centred * centred, axis=-1, keepdims=True) + EPS)
    return centred * factor, factor


def normalized_back(grad, unit, factor, gain):
    scaled = grad * gain
    inner = jnp.mean(scaled, axis=-1, keepdims=True)
    along = jnp.mean(scaled * unit, axis=-1, keepdims=True)
    return factor * (scaled - inner - unit * along)


def column_sum(v):
    return jnp.sum(v, axis=0, keepdims=True)


def embedding(r, i):
    row = lax.broadcasted_iota(jnp.int32, (24, 1), 0)
    return column_sum(jnp.where(row == r.task_ids[i], r.params[0:24], 0.0))


def head_lanes(h):
    lane = lax.broadcasted_iota(jnp.int32, (1, 128), 1)
    return ((lane >= 64) == (h == 1)).astype(F32).astype(BF16)


def first_norm(r, i):
    unit, factor = normalized(r.lat[i].astype(F32) + embedding(r, i))
    r.a1[rows_of(i)] = (unit * r.params[18:19] + r.params[19:20]).astype(BF16)
    r.u1[rows_of(i)] = unit
    r.factors[rows_of(i), 0:1] = factor


def project(r, i):
    a1 = r.a1[rows_of(i)]
    for part in range(3):
        columns = slice(part * 512, (part + 1) * 512)
        result = nn(a1, r.w_qkv[:, columns])
        if part == 0:
            result = result * 0.125
        r.qkv[rows_of(i), columns] = result.astype(BF16)


def pair_of(r, i, hp, part):
    return r.qkv[rows_of(i), span_of(part * 4 + hp, 128)]


def attend(r, i, hp):
    q, k, v = (pair_of(r, i, hp, part) for part in range(3))
    slots = lax.broadcasted_iota(jnp.int32, (1, 512), 1)
    bias = jnp.where(slots < r.counts[i], 0.0, -1000000000.0)
    mixed = None
    for h in range(2):
        lanes = head_lanes(h)
        scores = nt(q, k * lanes) + bias
        expo = jnp.exp(scores - jnp.max(scores, axis=-1, keepdims=True)).astype(BF16)
        r.expo[i * 8 + hp * 2 + h] = expo
        wide = jnp.concatenate((v * lanes, jnp.broadcast_to(lanes, (512, 128))), 1)
        term = nn(expo, wide)
        mixed = term if mixed is None else mixed + term
    inverse = 1.0 / mixed[:, 128:]
    columns = span_of(hp, 128)
    r.inverse[rows_of(i), columns] = inverse
    mean = mixed[:, :128] * inverse
    r.o32[rows_of(i), columns] = mean
    r.o[rows_of(i), columns] = mean.astype(BF16)


def second_norm(r, i):
    h1 = r.lat[i].astype(F32) + embedding(r, i) + (nn(r.o[rows_of(i)], r.w_out[...]) + r.params[22:23])
    unit, factor = normalized(h1)
    r.a2[rows_of(i)] = (unit * r.params[20:21] + r.params[21:22]).astype(BF16)
    r.u2[rows_of(i)] = unit
    r.factors[rows_of(i), 1:2] = factor
    r.result[rows_of(i)] = h1


def feed_forward(r, j):
    units, tile = span_of(j, 512), span_of(j, 128)
    bias = jnp.concatenate([r.params[24 + m : 25 + m, tile] for m in range(4)], 1)
    sums = None
    for i in range(2):
        z = nn(r.a2[rows_of(i)], r.w_up[:, units]) + bias
        z2 = z * z
        half = 0.5 + 0.5 * jnp.tanh(z * (GELU0 + GELU1 * z2))
        act = (z * half).astype(BF16)
        slope = half + z * (2 * GELU0 + 6 * GELU1 * z2) * (half * (1.0 - half))
        gz = (nt(r.y[i], r.w_down[units, :]) * slope).astype(BF16)
        r.act[rows_of(i), units] = act
        r.gz[j % 2, rows_of(i)] = gz
        back = nt(gz, r.w_up[:, units])
        r.back[rows_of(i)] = back if isinstance(j, int) and j == 0 else r.back[rows_of(i)] + back
        total = column_sum(gz.astype(F32))
        sums = total if sums is None else sums + total
    for m in range(4):
        r.small[j, 24 + m : 25 + m] = sums[:, m * 128 : (m + 1) * 128]


def chunk_gradients(r, j):
    g_down = tn(r.act[:, span_of(j, 512)], r.y[...].reshape(1024, 512)).astype(BF16)
    for c in range(2):
        for t in range(4):
            r.tiles[8 + t, j, c] = g_down[c * 256 : (c + 1) * 256, t * 128 : (t + 1) * 128].reshape(4, 4, 16, 128)
    g_up = tn(r.a2[...], r.gz[j % 2]).astype(BF16)
    fold(r, [g_up[:, q * 128 : (q + 1) * 128] for q in range(4)], 4 + j)


def add_small(r, row, value):
    for x in range(4):
        r.small[x, row : row + 1] = r.small[x, row : row + 1] + value[:, x * 128 : (x + 1) * 128]


def second_norm_back(r, i):
    grad, unit = r.back[rows_of(i)], r.u2[rows_of(i)]
    add_small(r, 20, column_sum(grad * unit))
    add_small(r, 21, column_sum(grad))
    y = r.y[i].astype(F32)
    gh1 = y + normalized_back(grad, unit, r.factors[rows_of(i), 1:2], r.params[20:21])
    r.back[rows_of(i)] = gh1
    gb = gh1.astype(BF16)
    r.gb[rows_of(i)] = gb
    add_small(r, 22, column_sum(gb.astype(F32)))
    go = (nt(gb, r.w_out[...]) * r.inverse[rows_of(i)]).astype(BF16)
    r.go[rows_of(i)] = go
    product = go.astype(F32) * r.o32[rows_of(i)]
    high = product.astype(BF16).astype(F32)
    low = product - high
    first = lax.broadcasted_iota(jnp.int32, (1, 128), 1) < 64
    for hp in range(4):
        columns = slice(hp * 128, (hp + 1) * 128)
        swapped = pltpu.roll(low[:, columns], 64, 1)
        r.god0[rows_of(i), columns] = jnp.where(first, high[:, columns], swapped).astype(BF16)
        r.god1[rows_of(i), columns] = jnp.where(first, swapped, high[:, columns]).astype(BF16)


def out_gradient(r):
    g_out = tn(r.o[...], r.gb[...]).astype(BF16)
    fold(r, [g_out[:, q * 128 : (q + 1) * 128] for q in range(4)], 3)


def result_of(r, i):
    r.out[i] = (r.result[rows_of(i)] + nn(r.act[rows_of(i)], r.w_down[...]) + r.params[23:24]).astype(BF16)


def attend_back(r, i, hp):
    q, k, v = (pair_of(r, i, hp, part) for part in range(3))
    columns = span_of(hp, 128)
    go = r.go[rows_of(i), columns]
    gq = gk = gv = 0.0
    for h in range(2):
        lanes = head_lanes(h)
        both = jnp.concatenate((go, (r.god0, r.god1)[h][rows_of(i), columns]), 1)
        wide = jnp.concatenate((v * lanes, jnp.full((512, 128), -1.0, BF16)), 1)
        expo = r.expo[i * 8 + hp * 2 + h]
        gs = (expo.astype(F32) * nt(both, wide)).astype(BF16)
        gq = gq + nn(gs, k * lanes)
        gk = gk + tn(gs, q * lanes)
        gv = gv + tn(expo, go * lanes)
    for part, value in enumerate((gq * 0.125, gk, gv)):
        r.gqkv[i][part][:, span_of(hp, 128)] = value.astype(BF16)


def first_norm_back(r, i):
    grad, unit = nt(jnp.concatenate([part[...] for part in r.gqkv[i]], 1), r.w_qkv[...]), r.u1[rows_of(i)]
    add_small(r, 18, column_sum(grad * unit))
    add_small(r, 19, column_sum(grad))
    gh0 = r.back[rows_of(i)] + normalized_back(grad, unit, r.factors[rows_of(i), 0:1], r.params[18:19])
    r.glat[i] = gh0.astype(BF16)
    total = column_sum(gh0)
    row = lax.broadcasted_iota(jnp.int32, (18, 1), 0)
    for x in range(4):
        mine = jnp.where(row == r.task_ids[i], total[:, x * 128 : (x + 1) * 128], 0.0)
        r.small[x, 0:18] = r.small[x, 0:18] + mine


def in_gradient(r, t):
    columns = jnp.concatenate(
        [jnp.concatenate([r.gqkv[i][ct // 4][:, span_of(ct % 4, 128)] for ct in COLUMNS[t]], 1) for i in range(2)]
    )
    g_in = tn(r.a1[...], columns).astype(BF16)
    fold(r, [g_in[:, q * 128 : (q + 1) * 128] for q in range(4)], t)


class Refs:
    def __init__(self, names, refs):
        for name, ref in zip(names, refs, strict=True):
            setattr(self, name, ref)


RAW = {
    "raw_in": ((4, 1536), BF16),
    "raw_out": ((4, 512), BF16),
    "raw_up": ((4, 2048), BF16),
    "raw_down": ((16, 512), BF16),
    "raw_table": ((4, 18), BF16),
    "raw_norms": ((4, 4), BF16),
    "raw_biases": ((2, 4), BF16),
    "raw_up_bias": ((1, 16), BF16),
}
INPUTS = ("task_ids", "counts", "lat_hbm", "y_hbm", *(f"{name}_hbm" for name in RAW))
OUTPUTS = ("out_hbm", "glat_hbm", "total", "s_total")
BLOCKS = (TILES, 4, 2, 4, 4, 16, 128)
SCRATCH = {
    **RAW,
    "own32": ((TILES, 16, 128), F32),
    "own": ((TILES, 16, 128), BF16),
    "small32": ((40, 128), F32),
    "table32": ((128, 128), F32),
    "own_small": ((32, 128), BF16),
    "lat": ((2, 512, 512), BF16),
    "y": ((2, 512, 512), BF16),
    "w_qkv": ((512, 1536), BF16),
    "w_out": ((512, 512), BF16),
    "w_up": ((512, 2048), BF16),
    "w_down": ((2048, 512), BF16),
    "params": ((32, 512), F32),
    "a1": ((1024, 512), BF16),
    "u1": ((1024, 512), F32),
    "qkv": ((1024, 1536), BF16),
    "expo": ((16, 512, 512), BF16),
    "o": ((1024, 512), BF16),
    "o32": ((1024, 512), F32),
    "inverse": ((1024, 512), F32),
    "result": ((1024, 512), F32),
    "a2": ((1024, 512), BF16),
    "u2": ((1024, 512), F32),
    "factors": ((1024, 2), F32),
    "act": ((1024, 2048), BF16),
    "gz": ((2, 1024, 512), BF16),
    "back": ((1024, 512), F32),
    "gb": ((1024, 512), BF16),
    "small": ((4, 32, 128), F32),
    "tiles": (BLOCKS, BF16),
    "slots": ((2, 3, 32, 128), BF16),
    "kept": ((4, 32, 128), BF16),
    "pair": ((4, 32, 128), BF16),
    "from_pair": ((TILES, 4, 4, 4, 16, 128), BF16),
    "from1": ((TILES, 3, 4, 4, 16, 128), BF16),
    "from2": ((TILES, 3, 4, 16, 128), BF16),
    "from3": ((TILES, 3, 16, 128), BF16),
    "s_pair": ((4, 32, 128), F32),
    "s_slots": ((3, 3, 32, 128), F32),
    "s_held": ((7, 32, 128), F32),
}
SEMAPHORES = {
    "g_send": (2, 3, 13),
    "g_recv": (2, 3, 13),
    "gs_send": (10,),
    "gs_recv": (10,),
    "p_send": (12,),
    "p_recv": (12,),
    "r_send": (17, 9),
    "r_recv": (17, 9),
    "rs_send": (10,),
    "rs_recv": (10,),
    "local": (12,),
}


def alias(r):
    r.go, r.god0, r.god1 = r.gz.at[0], r.gz.at[1], r.a2
    r.out, r.glat = r.lat, r.y
    r.gqkv = [r.w_up.at[:, span_of(part, 512)] for part in range(3)], [r.lat.at[0], r.lat.at[1], r.w_out]


def loop(count, step):
    lax.fori_loop(0, count, lambda n, carry: (step(n), carry)[1], 0)


def pack_own(r, pos):
    for t, blocks in enumerate(COLUMNS):
        raw = (r.raw_in, r.raw_out, r.raw_up)[0 if t < 3 else 1 if t == 3 else 2]
        for q, ct in enumerate(blocks):
            r.own32[t, 4 * q : 4 * q + 4] = raw[:, ct * 128 : (ct + 1) * 128].astype(F32)
    for t in range(8):
        r.own[t] = r.own32[t].astype(BF16)
    for t in range(4):
        r.own[8 + t] = r.raw_down[:, t * 128 : (t + 1) * 128]
    r.small32[...] = jnp.zeros_like(r.small32)
    r.table32[...] = jnp.zeros_like(r.table32)
    r.table32[0:4, 0:18] = r.raw_table[...].astype(F32)
    r.small32[18:22, 0:4] = r.raw_norms[...].astype(F32)
    r.small32[22:24, 0:4] = r.raw_biases[...].astype(F32)
    r.small32[32:33, 0:16] = r.raw_up_bias[...].astype(F32)
    offset, bias_row, bias_offset = small_place(pos)
    block = pltpu.roll(r.small32[0:32] + r.table32[...].T[0:32], offset, 1)
    bias = pltpu.roll(r.small32[32:40], bias_offset, 1)[0:1]
    row = lax.broadcasted_iota(jnp.int32, (32, 1), 0)
    r.own_small[...] = (block + jnp.where(row == bias_row, bias, 0.0)).astype(BF16)


def kernel(*refs):
    r = Refs((*INPUTS, *OUTPUTS, *SCRATCH, *SEMAPHORES), refs)
    alias(r)
    pos = my_position()
    loads = [
        pltpu.make_async_copy(getattr(r, f"{name}_hbm"), getattr(r, name), r.local.at[n])
        for n, name in enumerate((*RAW, "lat", "y"))
    ]
    store_out = pltpu.make_async_copy(r.out, r.out_hbm, r.local.at[10])
    store_glat = pltpu.make_async_copy(r.glat, r.glat_hbm, r.local.at[11])
    greet(pos)
    for load in loads:
        load.start()
    gathers = [Gather(w, r.own, r.tiles, r.g_send, r.g_recv, pos) for w in range(2)]
    tiny = SmallGather(r.own_small, r.slots, r.kept, r.pair, r.gs_send, r.gs_recv, pos)
    tiny_sum = SmallScatter(r.small, r.s_pair, r.s_slots, r.s_held, r.rs_send, r.rs_recv, pos)
    g_in = [Piece(r, pos, t, t, 1, ORDERS[t][::-1]) for t in range(3)]
    g_out = Piece(r, pos, 3, 3, 1, ("x", "z", "y"))
    down_orders = (("z", "y", "x"), ("y", "z", "x"))

    def chunk(j):
        up = Piece(r, pos, 4 + j, 4 + j, 1, ("x", "y", "z"))
        down = Piece(r, pos, 8 + j, 8, 4, (), x=j, stages=())
        halves = [Piece(r, pos, 8 + 2 * j + n, 8 + 2 * n, 2, down_orders[n], x=j, stages=(0, 1)) for n in range(2)]
        return up, down, halves

    chunks = [chunk(j) for j in range(4)]
    g_up, g_down, g_halves = zip(*chunks, strict=True)
    g_last = Piece(r, pos, 16, 8, 4, ("z", "y", "x"), stages=(2,))
    for load in loads[:8]:
        load.wait()
    pack_own(r, pos)
    greeted(pos)

    gathers[0].start(0)
    tiny.start(0)
    gathers[1].start(0)
    for t in range(TILES):
        r.tiles[t, pos["x"], pos["c"], pos["y"], pos["z"]] = r.own[t]
    r.small[...] = jnp.zeros_like(r.small)
    gathers[0].arrive(0)
    gathers[0].start(1)
    tiny.arrive(0)
    tiny.start(1)
    gathers[1].arrive(0)
    gathers[1].start(1)
    gathers[0].arrive(1)
    gathers[0].start(2)
    tiny.arrive(1)
    tiny.start(2)
    loads[9].wait()
    for i in range(2):
        add_small(r, 23, column_sum(r.y[i].astype(F32)))
    tiny.arrive(2)
    gathers[0].arrive(2)
    gathers[1].arrive(1)
    gathers[1].start(2)
    tiny.arrive_pair(r.params)
    loads[8].wait()
    for i in range(2):
        first_norm(r, i)
    for t in range(3):
        gathers[0].arrive_pair(t)
    for t in range(3):
        unfold(r, t, r.w_qkv)
    loop(2, lambda i: project(r, i))

    for n in range(8):
        attend(r, n // 4, n % 4)
    gathers[1].arrive(2)
    gathers[1].arrive_pair(0)
    unfold(r, 3, r.w_out)
    for i in range(2):
        second_norm(r, i)
    for part in (1, 2):
        gathers[1].arrive_pair(part)
    for t in range(4, 8):
        unfold(r, t, r.w_up)
    unfold_plain(r, r.w_down)
    for gather in gathers:
        gather.settle()
    tiny.settle()

    def leave(j):
        up, down, _ = chunk(j)
        up.pair_copy().start()
        down.pair_copy().start()

    def begin(j):
        up, down, halves = chunk(j)
        up.pair_add()
        down.pair_add()
        for piece in (up, *halves):
            piece.start(0)

    def turn(piece, stage):
        piece.add(stage)
        piece.start(stage + 1)

    def second(j):
        for piece in (g_up[j], *g_halves[j]):
            turn(piece, 0)

    def third(j):
        turn(g_up[j], 1)
        for piece in g_halves[j]:
            piece.add(1)

    r.back[...] = jnp.zeros_like(r.back)

    def middle(j):
        feed_forward(r, j)
        chunk_gradients(r, j)
        leave(j)

        @pl.when(j > 0)
        def _():
            begin(j - 1)

    loop(4, middle)
    second(0)
    loop(2, lambda i: second_norm_back(r, i))
    begin(3)
    second(1)
    out_gradient(r)
    g_out.pair_copy().start()

    def backward(half):
        for n in range(4):
            attend_back(r, n % 2, half * 2 + n // 2)

        @pl.when(half == 0)
        def _():
            g_out.pair_add()
            g_out.start(0)
            second(2)
            third(0)
            in_gradient(r, 0)
            g_in[0].pair_copy().start()
            second(3)
            third(1)

    loop(2, backward)
    in_gradient(r, 1)
    g_in[1].pair_copy().start()
    g_in[0].pair_add()
    g_in[0].start(0)
    turn(g_out, 0)
    third(2)
    in_gradient(r, 2)
    g_in[2].pair_copy().start()
    g_in[1].pair_add()
    g_in[1].start(0)
    third(3)
    g_last.start(2)
    first_norm_back(r, 0)
    g_in[2].pair_add()
    g_in[2].start(0)
    first_norm_back(r, 1)
    tiny_sum.pair_copy().start()
    store_glat.start()
    turn(g_in[0], 0)
    turn(g_out, 1)
    tiny_sum.add_pair()
    tiny_sum.start(0)
    loop(2, lambda i: result_of(r, i))
    store_out.start()
    tiny_sum.add(0)
    tiny_sum.start(1)
    turn(g_in[2], 0)
    turn(g_in[1], 0)
    turn(g_in[0], 1)
    for piece in (*g_up, g_last):
        piece.add(2)
    tiny_sum.add(1)
    tiny_sum.start(2)
    turn(g_in[2], 1)
    turn(g_in[1], 1)
    g_out.add(2)
    g_in[0].add(2)
    for piece in (*g_in, g_out, *g_up, *g_down, *(half for halves in g_halves for half in halves), g_last):
        piece.settle()
    store_out.wait()
    store_glat.wait()
    g_in[1].add(2)
    g_in[2].add(2)
    tiny_sum.add(2)
    r.s_total[...] = r.s_held[6]
    tiny_sum.settle()


SHAPES = ((4, 18), (4, 4), (4, 1536), (4, 512), (2, 4), (4, 2048), (1, 16), (16, 512))


def finish(*refs):
    out_in, glat_in, total_hbm, small_hbm, out, glat, *rest = refs
    targets, (held, total, small), parts, (sems, load_sems, store_sems) = rest[:8], rest[8:11], rest[11:19], rest[19:]
    table, norms, w_in, w_out, biases, w_up, up_bias, w_down = parts
    loads = [
        pltpu.make_async_copy(total_hbm, total, load_sems.at[0]),
        pltpu.make_async_copy(small_hbm, small, load_sems.at[1]),
    ]
    for load in loads:
        load.start()
    reads, writes = [], []
    for n, (source, target) in enumerate(((out_in, out), (glat_in, glat))):
        for k in range(4):
            slot, rows = 4 * n + k, pl.ds(k % 2 * 256, 256)
            reads.append(pltpu.make_async_copy(source.at[k // 2, rows], held.at[slot], sems.at[0, slot]))
            writes.append(pltpu.make_async_copy(held.at[slot], target.at[k // 2, rows], sems.at[1, slot]))
    for read in reads:
        read.start()
    for load in loads:
        load.wait()
    for t, blocks in enumerate(COLUMNS):
        to = (w_in, w_out, w_up)[0 if t < 3 else 1 if t == 3 else 2]
        for q, ct in enumerate(blocks):
            to[:, ct * 128 : (ct + 1) * 128] = total[t, 4 * q : 4 * q + 4]
    for t in range(4):
        w_down[:, t * 128 : (t + 1) * 128] = total[8 + t]
    offset, bias_row, bias_offset = small_place(my_position())
    block = pltpu.roll(small[...], lax.rem(128 - offset, 128), 1)
    table[...] = jnp.concatenate((block, jnp.zeros((96, 128), F32))).T[0:4, 0:18]
    norms[...] = block[18:22, 0:4]
    biases[...] = block[22:24, 0:4]
    row = lax.broadcasted_iota(jnp.int32, (32, 1), 0)
    bias = jnp.sum(jnp.where(row == bias_row, small[...], 0.0), axis=0, keepdims=True)
    bias = pltpu.roll(jnp.broadcast_to(bias, (8, 128)), lax.rem(128 - bias_offset, 128), 1)
    up_bias[...] = bias[0:1, 0:16]
    stores = [
        pltpu.make_async_copy(part, target, store_sems.at[n])
        for n, (part, target) in enumerate(zip(parts, targets, strict=True))
    ]
    for store in stores:
        store.start()
    for read, write in zip(reads, writes, strict=True):
        read.wait()
        write.start()
    for copy in (*stores, *writes):
        copy.wait()


def whole(task_ids, counts, latents, cotangent, *raw):
    vmem = pl.BlockSpec(memory_space=pltpu.VMEM)
    smem = pl.BlockSpec(memory_space=pltpu.SMEM)
    hbm = pl.BlockSpec(memory_space=pl.ANY)
    array = jax.ShapeDtypeStruct(latents.shape, BF16)
    found = pl.pallas_call(
        kernel,
        out_shape=[
            array,
            array,
            jax.ShapeDtypeStruct((TILES, 16, 128), F32),
            jax.ShapeDtypeStruct((32, 128), F32),
        ],
        in_specs=[smem, smem] + [hbm] * (2 + len(RAW)),
        out_specs=[hbm, hbm, vmem, vmem],
        scratch_shapes=[pltpu.VMEM(shape, dtype) for shape, dtype in SCRATCH.values()]
        + [pltpu.SemaphoreType.DMA(shape) for shape in SEMAPHORES.values()],
        compiler_params=pltpu.CompilerParams(
            collective_id=0, has_side_effects=True, vmem_limit_bytes=121 * 2**19
        ),
    )(task_ids, counts, latents, cotangent, *raw)
    return pl.pallas_call(
        finish,
        out_shape=[array, array] + [jax.ShapeDtypeStruct(shape, F32) for shape in SHAPES],
        in_specs=[hbm] * 4,
        out_specs=[hbm] * 10,
        scratch_shapes=[
            pltpu.VMEM((8, 256, 512), BF16),
            pltpu.VMEM((TILES, 16, 128), F32),
            pltpu.VMEM((32, 128), F32),
            *(pltpu.VMEM(shape, F32) for shape in SHAPES),
            pltpu.SemaphoreType.DMA((2, 8)),
            pltpu.SemaphoreType.DMA((2,)),
            pltpu.SemaphoreType.DMA((8,)),
        ],
    )(*found)


def body(
    latents,
    task_ids,
    slot_counts,
    cotangent,
    task_embed,
    norms,
    attn_in,
    attn_out,
    out_biases,
    mlp_in,
    mlp_in_bias,
    mlp_out,
):
    raw = (attn_in, attn_out, mlp_in, mlp_out, task_embed.T, norms, out_biases, mlp_in_bias.reshape(1, 16))
    found = list(whole(task_ids, slot_counts, latents, cotangent, *raw))
    found[2] = found[2].T
    found[8] = found[8].reshape(16)
    return tuple(found)


def solution(mesh):
    in_specs = (
        P(("dp", "fsdp"), None, None),
        P(("dp", "fsdp")),
        P(("dp", "fsdp")),
        P(("dp", "fsdp"), None, None),
        P(None, ("dp", "fsdp")),
        P(None, ("dp", "fsdp")),
        P(("dp", "fsdp"), None),
        P(("dp", "fsdp"), None),
        P(None, ("dp", "fsdp")),
        P(("dp", "fsdp"), None),
        P(("dp", "fsdp")),
        P(("dp", "fsdp"), None),
    )
    out_specs = (
        P(("dp", "fsdp"), None, None),
        P(("dp", "fsdp"), None, None),
        P(None, ("dp", "fsdp")),
        P(None, ("dp", "fsdp")),
        P(("dp", "fsdp"), None),
        P(("dp", "fsdp"), None),
        P(None, ("dp", "fsdp")),
        P(("dp", "fsdp"), None),
        P(("dp", "fsdp")),
        P(("dp", "fsdp"), None),
    )
    return jax.shard_map(body, mesh=mesh, in_specs=in_specs, out_specs=out_specs, check_vma=False)
```

```python
import functools
import math

import jax
import jax.numpy as jnp
from jax import lax
from jax.experimental import pallas as pl
from jax.experimental.pallas import tpu as pltpu
from jax.sharding import PartitionSpec as P

HEADS = 8
EPS = 1e-05
BEST = lax.Precision.HIGHEST
MESH = pl.DeviceIdType.MESH
ALL = slice(None)
ORDERS = (("z", "y", "x"), ("y", "x", "z"), ("x", "z", "y"))
TILES = 12
WAVES = (((0, 1), (1, 1), (2, 1)), ((3, 3), (6, 3), (9, 3)))


def my_position():
    dp, fsdp = lax.axis_index("dp"), lax.axis_index("fsdp")
    return {
        "x": lax.div(dp, 2),
        "c": lax.rem(dp, 2),
        "y": lax.div(fsdp, 4),
        "z": lax.rem(fsdp, 4),
    }


def moved(pos, axis, step):
    size = 2 if axis == "c" else 4
    return {**pos, axis: lax.rem(pos[axis] + step, size)}


def device_of(pos):
    return (pos["x"] * 2 + pos["c"], pos["y"] * 4 + pos["z"])


def partners_of(pos):
    return [moved(pos, axis, k) for axis in "xyz" for k in (1, 2, 3)] + [moved(pos, "c", 1)]


def greet(pos):
    barrier = pltpu.get_barrier_semaphore()
    for other in partners_of(pos):
        pl.semaphore_signal(barrier, inc=1, device_id=device_of(other), device_id_type=MESH)


def greeted(pos):
    pl.semaphore_wait(pltpu.get_barrier_semaphore(), 10)


def remote(src, dst, send, recv, pos):
    return pltpu.make_async_remote_copy(
        src_ref=src, dst_ref=dst, send_sem=send, recv_sem=recv,
        device_id=device_of(pos), device_id_type=MESH,
    )


class Gather:
    def __init__(self, wave, own, tiles, send, recv, pos):
        self.wave, self.own, self.tiles, self.pos = wave, own, tiles, pos
        self.send, self.recv = send, recv

    def slab(self, part, free, at=None):
        first, count = WAVES[self.wave][part]
        place = {**self.pos, **(at or {})}
        index = [ALL if axis in free else place[axis] for axis in "xcyz"]
        return self.tiles.at[(pl.ds(first, count), *index)]

    def stage_copy(self, part, stage, k):
        order = ORDERS[part]
        slab = self.slab(part, order[:stage])
        src = slab
        if stage == 0:
            first, count = WAVES[self.wave][part]
            src = self.own.at[pl.ds(first, count)]
        slot = (self.wave, part, stage * 3 + k - 1)
        return remote(src, slab, self.send.at[slot], self.recv.at[slot], moved(self.pos, order[stage], k))

    def pair_copy(self, part, k):
        order = ORDERS[part]
        at = {order[2]: lax.rem(self.pos[order[2]] + 4 - k, 4)} if k else None
        slab = self.slab(part, order[:2], at)
        slot = (self.wave, part, 9 + k)
        return remote(slab, slab, self.send.at[slot], self.recv.at[slot], moved(self.pos, "c", 1))

    def start(self, stage):
        for part in range(3):
            for k in (2, 1, 3):
                self.stage_copy(part, stage, k).start()
            if stage == 2:
                self.pair_copy(part, 0).start()

    def arrive(self, stage):
        for part in range(3):
            for k in (1, 3, 2):
                self.stage_copy(part, stage, k).wait_recv()
                if stage == 2:
                    self.pair_copy(part, k).start()

    def arrive_pair(self, part):
        for k in range(4):
            self.pair_copy(part, k).wait_recv()

    def settle(self):
        for part in range(3):
            for stage in range(3):
                for k in (1, 2, 3):
                    self.stage_copy(part, stage, k).wait_send()
            for k in range(4):
                self.pair_copy(part, k).wait_send()


class SmallGather:
    def __init__(self, own, slots, kept, pair, send, recv, pos):
        self.own, self.slots, self.kept, self.pair = own, slots, kept, pair
        self.send, self.recv, self.pos = send, recv, pos

    def copy(self, stage, k):
        here = self.kept.at[self.pos["x"]]
        src = self.own if stage == 0 else here
        dst = here if stage == 2 else self.slots.at[stage, k - 1]
        slot = stage * 3 + k - 1
        return remote(src, dst, self.send.at[slot], self.recv.at[slot], moved(self.pos, "zyx"[stage], k))

    def pair_copy(self):
        return remote(self.kept, self.pair, self.send.at[9], self.recv.at[9], moved(self.pos, "c", 1))

    def start(self, stage):
        for k in (2, 1, 3):
            self.copy(stage, k).start()

    def arrive(self, stage):
        for k in (1, 3, 2):
            self.copy(stage, k).wait_recv()
        if stage == 2:
            self.pair_copy().start()
            return
        total = self.own[...] if stage == 0 else self.kept[self.pos["x"]]
        if stage == 1:
            for k in (1, 2, 3):
                self.copy(1, k).wait_send()
        for k in range(3):
            total = total + self.slots[stage, k]
        self.kept[self.pos["x"]] = total

    def arrive_pair(self, out):
        self.pair_copy().wait_recv()
        for x in range(4):
            out[:, x * 128 : (x + 1) * 128] = self.kept[x].astype(jnp.float32) + self.pair[x].astype(jnp.float32)

    def settle(self):
        for stage in (0, 2):
            for k in (1, 2, 3):
                self.copy(stage, k).wait_send()
        self.pair_copy().wait_send()


class Piece:
    def __init__(self, r, pos, number, first, count, order, x=None, stages=(0, 1, 2)):
        self.r, self.pos, self.number, self.first, self.count = r, pos, number, first, count
        self.order, self.x, self.stages = order, x, stages

    def span(self):
        return pl.ds(self.first, self.count)

    def pair_copy(self):
        other = moved(self.pos, "c", 1)
        x = ALL if self.x is None else self.x
        return remote(
            self.r.tiles.at[self.span(), x, other["c"]], self.r.from_pair.at[self.span(), x],
            self.r.p_send.at[self.number], self.r.p_recv.at[self.number], other,
        )

    def pair_add(self):
        self.pair_copy().wait_recv()
        core = self.pos["c"]
        for n in range(self.count):
            t = self.first + n
            for x in range(4) if self.x is None else (self.x,):
                total = self.r.tiles[t, x, core].astype(jnp.float32) + self.r.from_pair[t, x].astype(jnp.float32)
                self.r.tiles[t, x, core] = total.astype(jnp.bfloat16)

    def index(self, stage, place):
        held = self.order[: stage + 1]
        found = []
        for axis in "xcyz":
            if axis == "c" or axis in held:
                found.append(place[axis])
            else:
                found.append(self.x if axis == "x" and self.x is not None else ALL)
        return tuple(found)

    def left(self, stage):
        free = [axis for axis in "xyz" if axis not in self.order[: stage + 1]]
        return tuple(self.x if axis == "x" and self.x is not None else ALL for axis in free)

    def copy(self, stage, k):
        axis = self.order[stage]
        other = moved(self.pos, axis, k)
        src = self.r.tiles.at[(self.span(), *self.index(stage, other))]
        dst = (self.r.from1, self.r.from2, self.r.from3)[stage].at[(self.span(), k - 1, *self.left(stage))]
        slot = (self.number, stage * 3 + k - 1)
        return remote(src, dst, self.r.r_send.at[slot], self.r.r_recv.at[slot], other)

    def start(self, stage):
        for k in (2, 1, 3):
            self.copy(stage, k).start()

    def add(self, stage):
        for k in (1, 3, 2):
            self.copy(stage, k).wait_recv()
        index, left = self.index(stage, self.pos), self.left(stage)
        arrived = (self.r.from1, self.r.from2, self.r.from3)[stage]
        for n in range(self.count):
            t = self.first + n
            total = self.r.tiles[(t, *index)].astype(jnp.float32)
            for k in range(3):
                total = total + arrived[(t, k, *left)].astype(jnp.float32)
            if stage == 2:
                self.r.total[t] = total
            else:
                self.r.tiles[(t, *index)] = total.astype(jnp.bfloat16)

    def settle(self):
        if self.number < 12 and self.stages != (0, 1):
            self.pair_copy().wait_send()
        for stage in self.stages:
            for k in (1, 2, 3):
                self.copy(stage, k).wait_send()


class SmallScatter:
    def __init__(self, own, pair, slots, held, send, recv, pos):
        self.own, self.pair, self.slots, self.held = own, pair, slots, held
        self.send, self.recv, self.pos = send, recv, pos

    def pair_copy(self):
        return remote(self.own, self.pair, self.send.at[9], self.recv.at[9], moved(self.pos, "c", 1))

    def copy(self, stage, k):
        other = moved(self.pos, "xyz"[stage], k)
        src = self.held.at[other["x"]] if stage == 0 else self.held.at[3 + stage]
        slot = stage * 3 + k - 1
        return remote(src, self.slots.at[stage, k - 1], self.send.at[slot], self.recv.at[slot], other)

    def add_pair(self):
        self.pair_copy().wait_recv()
        self.held[0:4] = self.own[...] + self.pair[...]

    def start(self, stage):
        for k in (2, 1, 3):
            self.copy(stage, k).start()

    def add(self, stage):
        for k in (1, 3, 2):
            self.copy(stage, k).wait_recv()
        total = self.held[self.pos["x"]] if stage == 0 else self.held[3 + stage]
        for k in range(3):
            total = total + self.slots[stage, k]
        self.held[4 + stage] = total

    def settle(self):
        self.pair_copy().wait_send()
        for stage in range(3):
            for k in (1, 2, 3):
                self.copy(stage, k).wait_send()


COLUMNS = (
    (0, 4, 8, 1),
    (5, 9, 2, 6),
    (10, 3, 7, 11),
    (0, 1, 2, 3),
    *(tuple(range(4 * j, 4 * j + 4)) for j in range(4)),
)


def quarter_order(transposed=False):
    a = lax.broadcasted_iota(jnp.int32, (256, 256), 1 if transposed else 0)
    b = lax.broadcasted_iota(jnp.int32, (256, 256), 0 if transposed else 1)
    source = ((a % 64) // 4) * 16 + (a // 64) * 4 + a % 4
    return (source == b).astype(jnp.float32).astype(jnp.bfloat16)


def unfold(r, t, out):
    blocks = [r.tiles[t, xc // 2, xc % 2].reshape(256, 128) for xc in range(8)]
    rows = nn(r.orders[0], jnp.concatenate(blocks, 1)).astype(jnp.bfloat16)
    for q, ct in enumerate(COLUMNS[t]):
        for xc in range(8):
            out[xc * 64 : (xc + 1) * 64, ct * 128 : (ct + 1) * 128] = rows[q * 64 : (q + 1) * 64, xc * 128 : (xc + 1) * 128]


def unfold_plain(r, out):
    def one(i):
        x, c = lax.div(i, 2), lax.rem(i, 2)
        for t in range(4):
            out[pl.ds(pl.multiple_of(i * 256, 256), 256), t * 128 : (t + 1) * 128] = r.tiles[8 + t, x, c].reshape(256, 128)

    loop(8, one)


def fold(r, columns, t):
    rows = [jnp.concatenate([block[xc * 64 : (xc + 1) * 64] for xc in range(8)], 1) for block in columns]
    blocks = nn(r.orders[1], jnp.concatenate(rows, 0)).astype(jnp.bfloat16)
    for xc in range(8):
        r.tiles[t, xc // 2, xc % 2] = blocks[:, xc * 128 : (xc + 1) * 128].reshape(4, 4, 16, 128)


def small_place(pos):
    ring = pos["y"] * 4 + pos["z"]
    return pos["c"] * 64 + ring * 4, 24 + pos["c"] * 2 + lax.div(ring, 8), 16 * lax.rem(ring, 8)


F32, BF16 = jnp.float32, jnp.bfloat16
GELU0 = math.sqrt(2.0 / math.pi)
GELU1 = GELU0 * 0.044715


def nn(a, b):
    return jnp.dot(a, b, preferred_element_type=F32)


def nt(a, b):
    return lax.dot_general(a, b, (((1,), (1,)), ((), ())), preferred_element_type=F32)


def tn(a, b):
    return lax.dot_general(a, b, (((0,), (0,)), ((), ())), preferred_element_type=F32)


def span_of(n, size):
    if isinstance(n, int):
        return slice(n * size, (n + 1) * size)
    return pl.ds(pl.multiple_of(n * size, size), size)


def rows_of(i):
    return span_of(i, 512)


def normalized(h):
    centred = h - jnp.mean(h, axis=-1, keepdims=True)
    factor = lax.rsqrt(jnp.mean(centred * centred, axis=-1, keepdims=True) + EPS)
    return centred * factor, factor


def normalized_back(grad, unit, factor, gain):
    scaled = grad * gain
    inner = jnp.mean(scaled, axis=-1, keepdims=True)
    along = jnp.mean(scaled * unit, axis=-1, keepdims=True)
    return factor * (scaled - inner - unit * along)


def column_sum(v):
    return jnp.sum(v, axis=0, keepdims=True)


def embedding(r, i):
    row = lax.broadcasted_iota(jnp.int32, (24, 1), 0)
    return column_sum(jnp.where(row == r.task_ids[i], r.params[0:24], 0.0))


def head_lanes(h):
    lane = lax.broadcasted_iota(jnp.int32, (1, 128), 1)
    return ((lane >= 64) == (h == 1)).astype(F32).astype(BF16)


def first_norm(r, i):
    unit, factor = normalized(r.lat[i].astype(F32) + embedding(r, i))
    r.a1[rows_of(i)] = (unit * r.params[18:19] + r.params[19:20]).astype(BF16)
    r.u1[rows_of(i)] = unit
    r.factors[rows_of(i), 0:1] = factor


def project(r, i):
    a1 = r.a1[rows_of(i)]
    for part in range(3):
        columns = slice(part * 512, (part + 1) * 512)
        result = nn(a1, r.w_qkv[:, columns])
        if part == 0:
            result = result * 0.125
        r.qkv[rows_of(i), columns] = result.astype(BF16)


def pair_of(r, i, hp, part):
    return r.qkv[rows_of(i), span_of(part * 4 + hp, 128)]


def attend(r, i, hp):
    q, k, v = (pair_of(r, i, hp, part) for part in range(3))
    slots = lax.broadcasted_iota(jnp.int32, (1, 512), 1)
    bias = jnp.where(slots < r.counts[i], 0.0, -1000000000.0)
    mixed = None
    for h in range(2):
        lanes = head_lanes(h)
        scores = nt(q, k * lanes) + bias
        expo = jnp.exp(scores - jnp.max(scores, axis=-1, keepdims=True)).astype(BF16)
        r.expo[i * 8 + hp * 2 + h] = expo
        wide = jnp.concatenate((v * lanes, jnp.broadcast_to(lanes, (512, 128))), 1)
        term = nn(expo, wide)
        mixed = term if mixed is None else mixed + term
    inverse = 1.0 / mixed[:, 128:]
    columns = span_of(hp, 128)
    r.inverse[rows_of(i), columns] = inverse
    mean = mixed[:, :128] * inverse
    r.o32[rows_of(i), columns] = mean
    r.o[rows_of(i), columns] = mean.astype(BF16)


def second_norm(r, i):
    h1 = r.lat[i].astype(F32) + embedding(r, i) + (nn(r.o[rows_of(i)], r.w_out[...]) + r.params[22:23])
    unit, factor = normalized(h1)
    r.a2[rows_of(i)] = (unit * r.params[20:21] + r.params[21:22]).astype(BF16)
    r.u2[rows_of(i)] = unit
    r.factors[rows_of(i), 1:2] = factor
    r.result[rows_of(i)] = h1


def feed_forward(r, j):
    units, tile = span_of(j, 512), span_of(j, 128)
    bias = jnp.concatenate([r.params[24 + m : 25 + m, tile] for m in range(4)], 1)
    sums = None
    for i in range(2):
        z = nn(r.a2[rows_of(i)], r.w_up[:, units]) + bias
        z2 = z * z
        half = 0.5 + 0.5 * jnp.tanh(z * (GELU0 + GELU1 * z2))
        act = (z * half).astype(BF16)
        slope = half + z * (2 * GELU0 + 6 * GELU1 * z2) * (half * (1.0 - half))
        gz = (nt(r.y[i], r.w_down[units, :]) * slope).astype(BF16)
        r.act[rows_of(i), units] = act
        r.gz[j % 2, rows_of(i)] = gz
        back = nt(gz, r.w_up[:, units])
        r.back[rows_of(i)] = back if isinstance(j, int) and j == 0 else r.back[rows_of(i)] + back
        total = column_sum(gz.astype(F32))
        sums = total if sums is None else sums + total
    for m in range(4):
        r.small[j, 24 + m : 25 + m] = sums[:, m * 128 : (m + 1) * 128]


def chunk_gradients(r, j):
    g_down = tn(r.act[:, span_of(j, 512)], r.y[...].reshape(1024, 512)).astype(BF16)
    for c in range(2):
        for t in range(4):
            r.tiles[8 + t, j, c] = g_down[c * 256 : (c + 1) * 256, t * 128 : (t + 1) * 128].reshape(4, 4, 16, 128)
    g_up = tn(r.a2[...], r.gz[j % 2]).astype(BF16)
    fold(r, [g_up[:, q * 128 : (q + 1) * 128] for q in range(4)], 4 + j)


def add_small(r, row, value):
    for x in range(4):
        r.small[x, row : row + 1] = r.small[x, row : row + 1] + value[:, x * 128 : (x + 1) * 128]


def second_norm_back(r, i):
    grad, unit = r.back[rows_of(i)], r.u2[rows_of(i)]
    add_small(r, 20, column_sum(grad * unit))
    add_small(r, 21, column_sum(grad))
    y = r.y[i].astype(F32)
    gh1 = y + normalized_back(grad, unit, r.factors[rows_of(i), 1:2], r.params[20:21])
    r.back[rows_of(i)] = gh1
    gb = gh1.astype(BF16)
    r.gb[rows_of(i)] = gb
    add_small(r, 22, column_sum(gb.astype(F32)))
    go = (nt(gb, r.w_out[...]) * r.inverse[rows_of(i)]).astype(BF16)
    r.go[rows_of(i)] = go
    product = go.astype(F32) * r.o32[rows_of(i)]
    high = product.astype(BF16).astype(F32)
    low = product - high
    first = lax.broadcasted_iota(jnp.int32, (1, 128), 1) < 64
    for hp in range(4):
        columns = slice(hp * 128, (hp + 1) * 128)
        swapped = pltpu.roll(low[:, columns], 64, 1)
        r.god0[rows_of(i), columns] = jnp.where(first, high[:, columns], swapped).astype(BF16)
        r.god1[rows_of(i), columns] = jnp.where(first, swapped, high[:, columns]).astype(BF16)


def out_gradient(r):
    g_out = tn(r.o[...], r.gb[...]).astype(BF16)
    fold(r, [g_out[:, q * 128 : (q + 1) * 128] for q in range(4)], 3)


def result_of(r, i):
    r.out[i] = (r.result[rows_of(i)] + nn(r.act[rows_of(i)], r.w_down[...]) + r.params[23:24]).astype(BF16)


def attend_back(r, i, hp):
    q, k, v = (pair_of(r, i, hp, part) for part in range(3))
    columns = span_of(hp, 128)
    go = r.go[rows_of(i), columns]
    gq = gk = gv = 0.0
    for h in range(2):
        lanes = head_lanes(h)
        both = jnp.concatenate((go, (r.god0, r.god1)[h][rows_of(i), columns]), 1)
        wide = jnp.concatenate((v * lanes, jnp.full((512, 128), -1.0, BF16)), 1)
        expo = r.expo[i * 8 + hp * 2 + h]
        gs = (expo.astype(F32) * nt(both, wide)).astype(BF16)
        gq = gq + nn(gs, k * lanes)
        gk = gk + tn(gs, q * lanes)
        gv = gv + tn(expo, go * lanes)
    for part, value in enumerate((gq * 0.125, gk, gv)):
        r.gqkv[i][part][:, span_of(hp, 128)] = value.astype(BF16)


def first_norm_back(r, i):
    grad, unit = nt(jnp.concatenate([part[...] for part in r.gqkv[i]], 1), r.w_qkv[...]), r.u1[rows_of(i)]
    add_small(r, 18, column_sum(grad * unit))
    add_small(r, 19, column_sum(grad))
    gh0 = r.back[rows_of(i)] + normalized_back(grad, unit, r.factors[rows_of(i), 0:1], r.params[18:19])
    r.glat[i] = gh0.astype(BF16)
    total = column_sum(gh0)
    row = lax.broadcasted_iota(jnp.int32, (18, 1), 0)
    for x in range(4):
        mine = jnp.where(row == r.task_ids[i], total[:, x * 128 : (x + 1) * 128], 0.0)
        r.small[x, 0:18] = r.small[x, 0:18] + mine


def in_gradient(r, t):
    columns = jnp.concatenate(
        [jnp.concatenate([r.gqkv[i][ct // 4][:, span_of(ct % 4, 128)] for ct in COLUMNS[t]], 1) for i in range(2)]
    )
    g_in = tn(r.a1[...], columns).astype(BF16)
    fold(r, [g_in[:, q * 128 : (q + 1) * 128] for q in range(4)], t)


class Refs:
    def __init__(self, names, refs):
        for name, ref in zip(names, refs, strict=True):
            setattr(self, name, ref)


RAW = {
    "raw_in": ((4, 1536), BF16),
    "raw_out": ((4, 512), BF16),
    "raw_up": ((4, 2048), BF16),
    "raw_down": ((16, 512), BF16),
    "raw_table": ((4, 18), BF16),
    "raw_norms": ((4, 4), BF16),
    "raw_biases": ((2, 4), BF16),
    "raw_up_bias": ((1, 16), BF16),
}
INPUTS = ("task_ids", "counts", "lat_hbm", "y_hbm", *(f"{name}_hbm" for name in RAW))
OUTPUTS = ("out_hbm", "glat_hbm", "total", "s_total")
BLOCKS = (TILES, 4, 2, 4, 4, 16, 128)
SCRATCH = {
    **RAW,
    "own32": ((TILES, 16, 128), F32),
    "own": ((TILES, 16, 128), BF16),
    "small32": ((40, 128), F32),
    "table32": ((128, 128), F32),
    "own_small": ((32, 128), BF16),
    "orders": ((2, 256, 256), BF16),
    "lat": ((2, 512, 512), BF16),
    "y": ((2, 512, 512), BF16),
    "w_qkv": ((512, 1536), BF16),
    "w_out": ((512, 512), BF16),
    "w_up": ((512, 2048), BF16),
    "w_down": ((2048, 512), BF16),
    "params": ((32, 512), F32),
    "a1": ((1024, 512), BF16),
    "u1": ((1024, 512), F32),
    "qkv": ((1024, 1536), BF16),
    "expo": ((16, 512, 512), BF16),
    "o": ((1024, 512), BF16),
    "o32": ((1024, 512), F32),
    "inverse": ((1024, 512), F32),
    "result": ((1024, 512), F32),
    "a2": ((1024, 512), BF16),
    "u2": ((1024, 512), F32),
    "factors": ((1024, 2), F32),
    "act": ((1024, 2048), BF16),
    "gz": ((2, 1024, 512), BF16),
    "back": ((1024, 512), F32),
    "gb": ((1024, 512), BF16),
    "small": ((4, 32, 128), F32),
    "tiles": (BLOCKS, BF16),
    "slots": ((2, 3, 32, 128), BF16),
    "kept": ((4, 32, 128), BF16),
    "pair": ((4, 32, 128), BF16),
    "from_pair": ((TILES, 4, 4, 4, 16, 128), BF16),
    "from1": ((TILES, 3, 4, 4, 16, 128), BF16),
    "from2": ((TILES, 3, 4, 16, 128), BF16),
    "from3": ((TILES, 3, 16, 128), BF16),
    "s_pair": ((4, 32, 128), F32),
    "s_slots": ((3, 3, 32, 128), F32),
    "s_held": ((7, 32, 128), F32),
}
SEMAPHORES = {
    "g_send": (2, 3, 13),
    "g_recv": (2, 3, 13),
    "gs_send": (10,),
    "gs_recv": (10,),
    "p_send": (12,),
    "p_recv": (12,),
    "r_send": (17, 9),
    "r_recv": (17, 9),
    "rs_send": (10,),
    "rs_recv": (10,),
    "local": (12,),
}


def alias(r):
    r.go, r.god0, r.god1 = r.gz.at[0], r.gz.at[1], r.a2
    r.out, r.glat = r.lat, r.y
    r.gqkv = [r.w_up.at[:, span_of(part, 512)] for part in range(3)], [r.lat.at[0], r.lat.at[1], r.w_out]


def loop(count, step):
    lax.fori_loop(0, count, lambda n, carry: (step(n), carry)[1], 0)


def pack_own(r, pos):
    for t, blocks in enumerate(COLUMNS):
        raw = (r.raw_in, r.raw_out, r.raw_up)[0 if t < 3 else 1 if t == 3 else 2]
        for q, ct in enumerate(blocks):
            r.own32[t, 4 * q : 4 * q + 4] = raw[:, ct * 128 : (ct + 1) * 128].astype(F32)
    for t in range(8):
        r.own[t] = r.own32[t].astype(BF16)
    for t in range(4):
        r.own[8 + t] = r.raw_down[:, t * 128 : (t + 1) * 128]
    r.small32[...] = jnp.zeros_like(r.small32)
    r.table32[...] = jnp.zeros_like(r.table32)
    r.table32[0:4, 0:18] = r.raw_table[...].astype(F32)
    r.small32[18:22, 0:4] = r.raw_norms[...].astype(F32)
    r.small32[22:24, 0:4] = r.raw_biases[...].astype(F32)
    r.small32[32:33, 0:16] = r.raw_up_bias[...].astype(F32)
    offset, bias_row, bias_offset = small_place(pos)
    block = pltpu.roll(r.small32[0:32] + r.table32[...].T[0:32], offset, 1)
    bias = pltpu.roll(r.small32[32:40], bias_offset, 1)[0:1]
    row = lax.broadcasted_iota(jnp.int32, (32, 1), 0)
    r.own_small[...] = (block + jnp.where(row == bias_row, bias, 0.0)).astype(BF16)


def kernel(*refs):
    r = Refs((*INPUTS, *OUTPUTS, *SCRATCH, *SEMAPHORES), refs)
    alias(r)
    pos = my_position()
    loads = [
        pltpu.make_async_copy(getattr(r, f"{name}_hbm"), getattr(r, name), r.local.at[n])
        for n, name in enumerate((*RAW, "lat", "y"))
    ]
    store_out = pltpu.make_async_copy(r.out, r.out_hbm, r.local.at[10])
    store_glat = pltpu.make_async_copy(r.glat, r.glat_hbm, r.local.at[11])
    greet(pos)
    for load in loads:
        load.start()
    gathers = [Gather(w, r.own, r.tiles, r.g_send, r.g_recv, pos) for w in range(2)]
    tiny = SmallGather(r.own_small, r.slots, r.kept, r.pair, r.gs_send, r.gs_recv, pos)
    tiny_sum = SmallScatter(r.small, r.s_pair, r.s_slots, r.s_held, r.rs_send, r.rs_recv, pos)
    g_in = [Piece(r, pos, t, t, 1, ORDERS[t][::-1]) for t in range(3)]
    g_out = Piece(r, pos, 3, 3, 1, ("x", "z", "y"))
    down_orders = (("z", "y", "x"), ("y", "z", "x"))

    def chunk(j):
        up = Piece(r, pos, 4 + j, 4 + j, 1, ("x", "y", "z"))
        down = Piece(r, pos, 8 + j, 8, 4, (), x=j, stages=())
        halves = [Piece(r, pos, 8 + 2 * j + n, 8 + 2 * n, 2, down_orders[n], x=j, stages=(0, 1)) for n in range(2)]
        return up, down, halves

    chunks = [chunk(j) for j in range(4)]
    g_up, g_down, g_halves = zip(*chunks, strict=True)
    g_last = Piece(r, pos, 16, 8, 4, ("z", "y", "x"), stages=(2,))
    for load in loads[:8]:
        load.wait()
    pack_own(r, pos)
    greeted(pos)

    gathers[0].start(0)
    tiny.start(0)
    gathers[1].start(0)
    for t in range(TILES):
        r.tiles[t, pos["x"], pos["c"], pos["y"], pos["z"]] = r.own[t]
    r.small[...] = jnp.zeros_like(r.small)
    gathers[0].arrive(0)
    gathers[0].start(1)
    tiny.arrive(0)
    tiny.start(1)
    gathers[1].arrive(0)
    gathers[1].start(1)
    gathers[0].arrive(1)
    gathers[0].start(2)
    tiny.arrive(1)
    tiny.start(2)
    r.orders[0] = quarter_order()
    r.orders[1] = quarter_order(True)
    loads[9].wait()
    for i in range(2):
        add_small(r, 23, column_sum(r.y[i].astype(F32)))
    tiny.arrive(2)
    gathers[0].arrive(2)
    gathers[1].arrive(1)
    gathers[1].start(2)
    tiny.arrive_pair(r.params)
    loads[8].wait()
    for i in range(2):
        first_norm(r, i)
    for t in range(3):
        gathers[0].arrive_pair(t)
    for t in range(3):
        unfold(r, t, r.w_qkv)
    loop(2, lambda i: project(r, i))

    for n in range(8):
        attend(r, n // 4, n % 4)
    gathers[1].arrive(2)
    gathers[1].arrive_pair(0)
    unfold(r, 3, r.w_out)
    for i in range(2):
        second_norm(r, i)
    for part in (1, 2):
        gathers[1].arrive_pair(part)
    for t in range(4, 8):
        unfold(r, t, r.w_up)
    unfold_plain(r, r.w_down)
    for gather in gathers:
        gather.settle()
    tiny.settle()

    def leave(j):
        up, down, _ = chunk(j)
        up.pair_copy().start()
        down.pair_copy().start()

    def begin(j):
        up, down, halves = chunk(j)
        up.pair_add()
        down.pair_add()
        for piece in (up, *halves):
            piece.start(0)

    def turn(piece, stage):
        piece.add(stage)
        piece.start(stage + 1)

    def second(j):
        for piece in (g_up[j], *g_halves[j]):
            turn(piece, 0)

    def third(j):
        turn(g_up[j], 1)
        for piece in g_halves[j]:
            piece.add(1)

    r.back[...] = jnp.zeros_like(r.back)

    def middle(j):
        feed_forward(r, j)
        chunk_gradients(r, j)
        leave(j)

        @pl.when(j > 0)
        def _():
            begin(j - 1)

    loop(4, middle)
    second(0)
    loop(2, lambda i: second_norm_back(r, i))
    begin(3)
    second(1)
    out_gradient(r)
    g_out.pair_copy().start()

    def backward(half):
        for n in range(4):
            attend_back(r, n % 2, half * 2 + n // 2)

        @pl.when(half == 0)
        def _():
            g_out.pair_add()
            g_out.start(0)
            second(2)
            third(0)
            in_gradient(r, 0)
            g_in[0].pair_copy().start()
            second(3)
            third(1)

    loop(2, backward)
    in_gradient(r, 1)
    g_in[1].pair_copy().start()
    g_in[0].pair_add()
    g_in[0].start(0)
    turn(g_out, 0)
    third(2)
    in_gradient(r, 2)
    g_in[2].pair_copy().start()
    g_in[1].pair_add()
    g_in[1].start(0)
    third(3)
    g_last.start(2)
    first_norm_back(r, 0)
    g_in[2].pair_add()
    g_in[2].start(0)
    first_norm_back(r, 1)
    tiny_sum.pair_copy().start()
    store_glat.start()
    turn(g_in[0], 0)
    turn(g_out, 1)
    tiny_sum.add_pair()
    tiny_sum.start(0)
    loop(2, lambda i: result_of(r, i))
    store_out.start()
    tiny_sum.add(0)
    tiny_sum.start(1)
    turn(g_in[2], 0)
    turn(g_in[1], 0)
    turn(g_in[0], 1)
    for piece in (*g_up, g_last):
        piece.add(2)
    tiny_sum.add(1)
    tiny_sum.start(2)
    turn(g_in[2], 1)
    turn(g_in[1], 1)
    g_out.add(2)
    g_in[0].add(2)
    for piece in (*g_in, g_out, *g_up, *g_down, *(half for halves in g_halves for half in halves), g_last):
        piece.settle()
    store_out.wait()
    store_glat.wait()
    g_in[1].add(2)
    g_in[2].add(2)
    tiny_sum.add(2)
    r.s_total[...] = r.s_held[6]
    tiny_sum.settle()


SHAPES = ((4, 18), (4, 4), (4, 1536), (4, 512), (2, 4), (4, 2048), (1, 16), (16, 512))


def finish(*refs):
    out_in, glat_in, total_hbm, small_hbm, out, glat, *rest = refs
    targets, (held, total, small), parts, (sems, load_sems, store_sems) = rest[:8], rest[8:11], rest[11:19], rest[19:]
    table, norms, w_in, w_out, biases, w_up, up_bias, w_down = parts
    loads = [
        pltpu.make_async_copy(total_hbm, total, load_sems.at[0]),
        pltpu.make_async_copy(small_hbm, small, load_sems.at[1]),
    ]
    for load in loads:
        load.start()
    reads, writes = [], []
    for n, (source, target) in enumerate(((out_in, out), (glat_in, glat))):
        for k in range(4):
            slot, rows = 4 * n + k, pl.ds(k % 2 * 256, 256)
            reads.append(pltpu.make_async_copy(source.at[k // 2, rows], held.at[slot], sems.at[0, slot]))
            writes.append(pltpu.make_async_copy(held.at[slot], target.at[k // 2, rows], sems.at[1, slot]))
    for read in reads:
        read.start()
    for load in loads:
        load.wait()
    for t, blocks in enumerate(COLUMNS):
        to = (w_in, w_out, w_up)[0 if t < 3 else 1 if t == 3 else 2]
        for q, ct in enumerate(blocks):
            to[:, ct * 128 : (ct + 1) * 128] = total[t, 4 * q : 4 * q + 4]
    for t in range(4):
        w_down[:, t * 128 : (t + 1) * 128] = total[8 + t]
    offset, bias_row, bias_offset = small_place(my_position())
    block = pltpu.roll(small[...], lax.rem(128 - offset, 128), 1)
    table[...] = jnp.concatenate((block, jnp.zeros((96, 128), F32))).T[0:4, 0:18]
    norms[...] = block[18:22, 0:4]
    biases[...] = block[22:24, 0:4]
    row = lax.broadcasted_iota(jnp.int32, (32, 1), 0)
    bias = jnp.sum(jnp.where(row == bias_row, small[...], 0.0), axis=0, keepdims=True)
    bias = pltpu.roll(jnp.broadcast_to(bias, (8, 128)), lax.rem(128 - bias_offset, 128), 1)
    up_bias[...] = bias[0:1, 0:16]
    stores = [
        pltpu.make_async_copy(part, target, store_sems.at[n])
        for n, (part, target) in enumerate(zip(parts, targets, strict=True))
    ]
    for store in stores:
        store.start()
    for read, write in zip(reads, writes, strict=True):
        read.wait()
        write.start()
    for copy in (*stores, *writes):
        copy.wait()


def whole(task_ids, counts, latents, cotangent, *raw):
    vmem = pl.BlockSpec(memory_space=pltpu.VMEM)
    smem = pl.BlockSpec(memory_space=pltpu.SMEM)
    hbm = pl.BlockSpec(memory_space=pl.ANY)
    array = jax.ShapeDtypeStruct(latents.shape, BF16)
    found = pl.pallas_call(
        kernel,
        out_shape=[
            array,
            array,
            jax.ShapeDtypeStruct((TILES, 16, 128), F32),
            jax.ShapeDtypeStruct((32, 128), F32),
        ],
        in_specs=[smem, smem] + [hbm] * (2 + len(RAW)),
        out_specs=[hbm, hbm, vmem, vmem],
        scratch_shapes=[pltpu.VMEM(shape, dtype) for shape, dtype in SCRATCH.values()]
        + [pltpu.SemaphoreType.DMA(shape) for shape in SEMAPHORES.values()],
        compiler_params=pltpu.CompilerParams(
            collective_id=0, has_side_effects=True, vmem_limit_bytes=121 * 2**19
        ),
    )(task_ids, counts, latents, cotangent, *raw)
    return pl.pallas_call(
        finish,
        out_shape=[array, array] + [jax.ShapeDtypeStruct(shape, F32) for shape in SHAPES],
        in_specs=[hbm] * 4,
        out_specs=[hbm] * 10,
        scratch_shapes=[
            pltpu.VMEM((8, 256, 512), BF16),
            pltpu.VMEM((TILES, 16, 128), F32),
            pltpu.VMEM((32, 128), F32),
            *(pltpu.VMEM(shape, F32) for shape in SHAPES),
            pltpu.SemaphoreType.DMA((2, 8)),
            pltpu.SemaphoreType.DMA((2,)),
            pltpu.SemaphoreType.DMA((8,)),
        ],
    )(*found)


def body(
    latents,
    task_ids,
    slot_counts,
    cotangent,
    task_embed,
    norms,
    attn_in,
    attn_out,
    out_biases,
    mlp_in,
    mlp_in_bias,
    mlp_out,
):
    raw = (attn_in, attn_out, mlp_in, mlp_out, task_embed.T, norms, out_biases, mlp_in_bias.reshape(1, 16))
    found = list(whole(task_ids, slot_counts, latents, cotangent, *raw))
    found[2] = found[2].T
    found[8] = found[8].reshape(16)
    return tuple(found)


def solution(mesh):
    in_specs = (
        P(("dp", "fsdp"), None, None),
        P(("dp", "fsdp")),
        P(("dp", "fsdp")),
        P(("dp", "fsdp"), None, None),
        P(None, ("dp", "fsdp")),
        P(None, ("dp", "fsdp")),
        P(("dp", "fsdp"), None),
        P(("dp", "fsdp"), None),
        P(None, ("dp", "fsdp")),
        P(("dp", "fsdp"), None),
        P(("dp", "fsdp")),
        P(("dp", "fsdp"), None),
    )
    out_specs = (
        P(("dp", "fsdp"), None, None),
        P(("dp", "fsdp"), None, None),
        P(None, ("dp", "fsdp")),
        P(None, ("dp", "fsdp")),
        P(("dp", "fsdp"), None),
        P(("dp", "fsdp"), None),
        P(None, ("dp", "fsdp")),
        P(("dp", "fsdp"), None),
        P(("dp", "fsdp")),
        P(("dp", "fsdp"), None),
    )
    return jax.shard_map(body, mesh=mesh, in_specs=in_specs, out_specs=out_specs, check_vma=False)
```

```python
import functools
import math

import jax
import jax.numpy as jnp
from jax import lax
from jax.experimental import pallas as pl
from jax.experimental.pallas import tpu as pltpu
from jax.sharding import PartitionSpec as P

HEADS = 8
EPS = 1e-05
BEST = lax.Precision.HIGHEST
MESH = pl.DeviceIdType.MESH
ALL = slice(None)
ORDERS = (("z", "y", "x"), ("y", "x", "z"), ("x", "z", "y"))
TILES = 12
WAVES = (((0, 1), (1, 1), (2, 1)), ((3, 3), (6, 3), (9, 3)))


def my_position():
    dp, fsdp = lax.axis_index("dp"), lax.axis_index("fsdp")
    return {
        "x": lax.div(dp, 2),
        "c": lax.rem(dp, 2),
        "y": lax.div(fsdp, 4),
        "z": lax.rem(fsdp, 4),
    }


def moved(pos, axis, step):
    size = 2 if axis == "c" else 4
    return {**pos, axis: lax.rem(pos[axis] + step, size)}


def device_of(pos):
    return (pos["x"] * 2 + pos["c"], pos["y"] * 4 + pos["z"])


def partners_of(pos):
    return [moved(pos, axis, k) for axis in "xyz" for k in (1, 2, 3)] + [moved(pos, "c", 1)]


def greet(pos):
    barrier = pltpu.get_barrier_semaphore()
    for other in partners_of(pos):
        pl.semaphore_signal(barrier, inc=1, device_id=device_of(other), device_id_type=MESH)


def greeted(pos):
    pl.semaphore_wait(pltpu.get_barrier_semaphore(), 10)


def remote(src, dst, send, recv, pos):
    return pltpu.make_async_remote_copy(
        src_ref=src, dst_ref=dst, send_sem=send, recv_sem=recv,
        device_id=device_of(pos), device_id_type=MESH,
    )


class Gather:
    def __init__(self, wave, own, tiles, send, recv, pos):
        self.wave, self.own, self.tiles, self.pos = wave, own, tiles, pos
        self.send, self.recv = send, recv

    def slab(self, part, free, at=None):
        first, count = WAVES[self.wave][part]
        place = {**self.pos, **(at or {})}
        index = [ALL if axis in free else place[axis] for axis in "xcyz"]
        return self.tiles.at[(pl.ds(first, count), *index)]

    def stage_copy(self, part, stage, k):
        order = ORDERS[part]
        slab = self.slab(part, order[:stage])
        src = slab
        if stage == 0:
            first, count = WAVES[self.wave][part]
            src = self.own.at[pl.ds(first, count)]
        slot = (self.wave, part, stage * 3 + k - 1)
        return remote(src, slab, self.send.at[slot], self.recv.at[slot], moved(self.pos, order[stage], k))

    def pair_copy(self, part, k):
        order = ORDERS[part]
        at = {order[2]: lax.rem(self.pos[order[2]] + 4 - k, 4)} if k else None
        slab = self.slab(part, order[:2], at)
        slot = (self.wave, part, 9 + k)
        return remote(slab, slab, self.send.at[slot], self.recv.at[slot], moved(self.pos, "c", 1))

    def start(self, stage):
        for part in range(3):
            for k in (2, 1, 3):
                self.stage_copy(part, stage, k).start()
            if stage == 2:
                self.pair_copy(part, 0).start()

    def arrive(self, stage):
        for part in range(3):
            for k in (1, 3, 2):
                self.stage_copy(part, stage, k).wait_recv()
                if stage == 2:
                    self.pair_copy(part, k).start()

    def arrive_pair(self, part):
        for k in range(4):
            self.pair_copy(part, k).wait_recv()

    def settle(self):
        for part in range(3):
            for stage in range(3):
                for k in (1, 2, 3):
                    self.stage_copy(part, stage, k).wait_send()
            for k in range(4):
                self.pair_copy(part, k).wait_send()


class SmallGather:
    def __init__(self, own, slots, kept, pair, send, recv, pos):
        self.own, self.slots, self.kept, self.pair = own, slots, kept, pair
        self.send, self.recv, self.pos = send, recv, pos

    def copy(self, stage, k):
        here = self.kept.at[self.pos["x"]]
        src = self.own if stage == 0 else here
        dst = here if stage == 2 else self.slots.at[stage, k - 1]
        slot = stage * 3 + k - 1
        return remote(src, dst, self.send.at[slot], self.recv.at[slot], moved(self.pos, "zyx"[stage], k))

    def pair_copy(self):
        return remote(self.kept, self.pair, self.send.at[9], self.recv.at[9], moved(self.pos, "c", 1))

    def start(self, stage):
        for k in (2, 1, 3):
            self.copy(stage, k).start()

    def arrive(self, stage):
        for k in (1, 3, 2):
            self.copy(stage, k).wait_recv()
        if stage == 2:
            self.pair_copy().start()
            return
        total = self.own[...] if stage == 0 else self.kept[self.pos["x"]]
        if stage == 1:
            for k in (1, 2, 3):
                self.copy(1, k).wait_send()
        for k in range(3):
            total = total + self.slots[stage, k]
        self.kept[self.pos["x"]] = total

    def arrive_pair(self, out):
        self.pair_copy().wait_recv()
        for x in range(4):
            out[:, x * 128 : (x + 1) * 128] = self.kept[x].astype(jnp.float32) + self.pair[x].astype(jnp.float32)

    def settle(self):
        for stage in (0, 2):
            for k in (1, 2, 3):
                self.copy(stage, k).wait_send()
        self.pair_copy().wait_send()


class Piece:
    def __init__(self, r, pos, number, first, count, order, x=None, stages=(0, 1, 2)):
        self.r, self.pos, self.number, self.first, self.count = r, pos, number, first, count
        self.order, self.x, self.stages = order, x, stages

    def span(self):
        return pl.ds(self.first, self.count)

    def pair_copy(self):
        other = moved(self.pos, "c", 1)
        x = ALL if self.x is None else self.x
        return remote(
            self.r.tiles.at[self.span(), x, other["c"]], self.r.from_pair.at[self.span(), x],
            self.r.p_send.at[self.number], self.r.p_recv.at[self.number], other,
        )

    def pair_add(self):
        self.pair_copy().wait_recv()
        core = self.pos["c"]
        for n in range(self.count):
            t = self.first + n
            for x in range(4) if self.x is None else (self.x,):
                total = self.r.tiles[t, x, core].astype(jnp.float32) + self.r.from_pair[t, x].astype(jnp.float32)
                self.r.tiles[t, x, core] = total.astype(jnp.bfloat16)

    def index(self, stage, place):
        held = self.order[: stage + 1]
        found = []
        for axis in "xcyz":
            if axis == "c" or axis in held:
                found.append(place[axis])
            else:
                found.append(self.x if axis == "x" and self.x is not None else ALL)
        return tuple(found)

    def left(self, stage):
        free = [axis for axis in "xyz" if axis not in self.order[: stage + 1]]
        return tuple(self.x if axis == "x" and self.x is not None else ALL for axis in free)

    def copy(self, stage, k):
        axis = self.order[stage]
        other = moved(self.pos, axis, k)
        src = self.r.tiles.at[(self.span(), *self.index(stage, other))]
        dst = (self.r.from1, self.r.from2, self.r.from3)[stage].at[(self.span(), k - 1, *self.left(stage))]
        slot = (self.number, stage * 3 + k - 1)
        return remote(src, dst, self.r.r_send.at[slot], self.r.r_recv.at[slot], other)

    def start(self, stage):
        for k in (2, 1, 3):
            self.copy(stage, k).start()

    def add(self, stage):
        for k in (1, 3, 2):
            self.copy(stage, k).wait_recv()
        index, left = self.index(stage, self.pos), self.left(stage)
        arrived = (self.r.from1, self.r.from2, self.r.from3)[stage]
        for n in range(self.count):
            t = self.first + n
            total = self.r.tiles[(t, *index)].astype(jnp.float32)
            for k in range(3):
                total = total + arrived[(t, k, *left)].astype(jnp.float32)
            if stage == 2:
                self.r.total[t] = total
            else:
                self.r.tiles[(t, *index)] = total.astype(jnp.bfloat16)

    def settle(self):
        if self.number < 12 and self.stages != (0, 1):
            self.pair_copy().wait_send()
        for stage in self.stages:
            for k in (1, 2, 3):
                self.copy(stage, k).wait_send()


class SmallScatter:
    def __init__(self, own, pair, slots, held, send, recv, pos):
        self.own, self.pair, self.slots, self.held = own, pair, slots, held
        self.send, self.recv, self.pos = send, recv, pos

    def pair_copy(self):
        return remote(self.own, self.pair, self.send.at[9], self.recv.at[9], moved(self.pos, "c", 1))

    def copy(self, stage, k):
        other = moved(self.pos, "xyz"[stage], k)
        src = self.held.at[other["x"]] if stage == 0 else self.held.at[3 + stage]
        slot = stage * 3 + k - 1
        return remote(src, self.slots.at[stage, k - 1], self.send.at[slot], self.recv.at[slot], other)

    def add_pair(self):
        self.pair_copy().wait_recv()
        self.held[0:4] = self.own[...] + self.pair[...]

    def start(self, stage):
        for k in (2, 1, 3):
            self.copy(stage, k).start()

    def add(self, stage):
        for k in (1, 3, 2):
            self.copy(stage, k).wait_recv()
        total = self.held[self.pos["x"]] if stage == 0 else self.held[3 + stage]
        for k in range(3):
            total = total + self.slots[stage, k]
        self.held[4 + stage] = total

    def settle(self):
        self.pair_copy().wait_send()
        for stage in range(3):
            for k in (1, 2, 3):
                self.copy(stage, k).wait_send()


COLUMNS = (
    (0, 4, 8, 1),
    (5, 9, 2, 6),
    (10, 3, 7, 11),
    (0, 1, 2, 3),
    *(tuple(range(4 * j, 4 * j + 4)) for j in range(4)),
)


def quarter_order(transposed=False):
    a = lax.broadcasted_iota(jnp.int32, (256, 256), 1 if transposed else 0)
    b = lax.broadcasted_iota(jnp.int32, (256, 256), 0 if transposed else 1)
    source = ((a % 64) // 4) * 16 + (a // 64) * 4 + a % 4
    return (source == b).astype(jnp.float32).astype(jnp.bfloat16)


def unfold(r, t, out):
    blocks = [r.tiles[t, xc // 2, xc % 2].reshape(256, 128) for xc in range(8)]
    rows = nn(r.orders[0], jnp.concatenate(blocks, 1)).astype(jnp.bfloat16)
    for q, ct in enumerate(COLUMNS[t]):
        for xc in range(8):
            out[xc * 64 : (xc + 1) * 64, ct * 128 : (ct + 1) * 128] = rows[q * 64 : (q + 1) * 64, xc * 128 : (xc + 1) * 128]


def unfold_plain(r, out):
    def one(i):
        x, c = lax.div(i, 2), lax.rem(i, 2)
        for t in range(4):
            out[pl.ds(pl.multiple_of(i * 256, 256), 256), t * 128 : (t + 1) * 128] = r.tiles[8 + t, x, c].reshape(256, 128)

    loop(8, one)


def fold(r, columns, t):
    rows = [jnp.concatenate([block[xc * 64 : (xc + 1) * 64] for xc in range(8)], 1) for block in columns]
    blocks = nn(r.orders[1], jnp.concatenate(rows, 0)).astype(jnp.bfloat16)
    for xc in range(8):
        r.tiles[t, xc // 2, xc % 2] = blocks[:, xc * 128 : (xc + 1) * 128].reshape(4, 4, 16, 128)


def small_place(pos):
    ring = pos["y"] * 4 + pos["z"]
    return pos["c"] * 64 + ring * 4, 24 + pos["c"] * 2 + lax.div(ring, 8), 16 * lax.rem(ring, 8)


F32, BF16 = jnp.float32, jnp.bfloat16
GELU0 = math.sqrt(2.0 / math.pi)
GELU1 = GELU0 * 0.044715


def nn(a, b):
    return jnp.dot(a, b, preferred_element_type=F32)


def nt(a, b):
    return lax.dot_general(a, b, (((1,), (1,)), ((), ())), preferred_element_type=F32)


def tn(a, b):
    return lax.dot_general(a, b, (((0,), (0,)), ((), ())), preferred_element_type=F32)


def span_of(n, size):
    if isinstance(n, int):
        return slice(n * size, (n + 1) * size)
    return pl.ds(pl.multiple_of(n * size, size), size)


def rows_of(i):
    return span_of(i, 512)


def normalized(h):
    centred = h - jnp.mean(h, axis=-1, keepdims=True)
    factor = lax.rsqrt(jnp.mean(centred * centred, axis=-1, keepdims=True) + EPS)
    return centred * factor, factor


def normalized_back(grad, unit, factor, gain):
    scaled = grad * gain
    inner = jnp.mean(scaled, axis=-1, keepdims=True)
    along = jnp.mean(scaled * unit, axis=-1, keepdims=True)
    return factor * (scaled - inner - unit * along)


def column_sum(v):
    return jnp.sum(v, axis=0, keepdims=True)


def embedding(r, i):
    row = lax.broadcasted_iota(jnp.int32, (24, 1), 0)
    return column_sum(jnp.where(row == r.task_ids[i], r.params[0:24], 0.0))


def head_lanes(h):
    lane = lax.broadcasted_iota(jnp.int32, (1, 128), 1)
    return ((lane >= 64) == (h == 1)).astype(F32).astype(BF16)


def first_norm(r, i):
    unit, factor = normalized(r.lat[i].astype(F32) + embedding(r, i))
    r.a1[rows_of(i)] = (unit * r.params[18:19] + r.params[19:20]).astype(BF16)
    r.u1[rows_of(i)] = unit
    r.factors[rows_of(i), 0:1] = factor


def project(r, i):
    a1 = r.a1[rows_of(i)]
    for part in range(3):
        columns = slice(part * 512, (part + 1) * 512)
        result = nn(a1, r.w_qkv[:, columns])
        if part == 0:
            result = result * 0.125
        r.qkv[rows_of(i), columns] = result.astype(BF16)


def pair_of(r, i, hp, part):
    return r.qkv[rows_of(i), span_of(part * 4 + hp, 128)]


def attend(r, i, hp):
    q, k, v = (pair_of(r, i, hp, part) for part in range(3))
    slots = lax.broadcasted_iota(jnp.int32, (1, 512), 1)
    bias = jnp.where(slots < r.counts[i], 0.0, -1000000000.0)
    mixed = None
    for h in range(2):
        lanes = head_lanes(h)
        scores = nt(q, k * lanes) + bias
        expo = jnp.exp(scores - jnp.max(scores, axis=-1, keepdims=True)).astype(BF16)
        r.expo[i * 8 + hp * 2 + h] = expo
        wide = jnp.concatenate((v * lanes, jnp.broadcast_to(lanes, (512, 128))), 1)
        term = nn(expo, wide)
        mixed = term if mixed is None else mixed + term
    inverse = 1.0 / mixed[:, 128:]
    columns = span_of(hp, 128)
    r.inverse[rows_of(i), columns] = inverse
    mean = mixed[:, :128] * inverse
    r.o32[rows_of(i), columns] = mean
    r.o[rows_of(i), columns] = mean.astype(BF16)


def second_norm(r, i):
    h1 = r.lat[i].astype(F32) + embedding(r, i) + (nn(r.o[rows_of(i)], r.w_out[...]) + r.params[22:23])
    unit, factor = normalized(h1)
    r.a2[rows_of(i)] = (unit * r.params[20:21] + r.params[21:22]).astype(BF16)
    r.u2[rows_of(i)] = unit
    r.factors[rows_of(i), 1:2] = factor
    r.result[rows_of(i)] = h1


def feed_forward(r, j):
    units, tile = span_of(j, 512), span_of(j, 128)
    bias = jnp.concatenate([r.params[24 + m : 25 + m, tile] for m in range(4)], 1)
    sums = None
    for i in range(2):
        z = nn(r.a2[rows_of(i)], r.w_up[:, units]) + bias
        z2 = z * z
        half = 0.5 + 0.5 * jnp.tanh(z * (GELU0 + GELU1 * z2))
        act = (z * half).astype(BF16)
        slope = half + z * (2 * GELU0 + 6 * GELU1 * z2) * (half * (1.0 - half))
        gz = (nt(r.y[i], r.w_down[units, :]) * slope).astype(BF16)
        r.act[rows_of(i), units] = act
        r.gz[j % 2, rows_of(i)] = gz
        back = nt(gz, r.w_up[:, units])
        r.back[rows_of(i)] = back if isinstance(j, int) and j == 0 else r.back[rows_of(i)] + back
        total = column_sum(gz.astype(F32))
        sums = total if sums is None else sums + total
    for m in range(4):
        r.small[j, 24 + m : 25 + m] = sums[:, m * 128 : (m + 1) * 128]


def chunk_gradients(r, j):
    g_down = tn(r.act[:, span_of(j, 512)], r.y[...].reshape(1024, 512)).astype(BF16)
    for c in range(2):
        for t in range(4):
            r.tiles[8 + t, j, c] = g_down[c * 256 : (c + 1) * 256, t * 128 : (t + 1) * 128].reshape(4, 4, 16, 128)
    g_up = tn(r.a2[...], r.gz[j % 2]).astype(BF16)
    fold(r, [g_up[:, q * 128 : (q + 1) * 128] for q in range(4)], 4 + j)


def add_small(r, row, value):
    for x in range(4):
        r.small[x, row : row + 1] = r.small[x, row : row + 1] + value[:, x * 128 : (x + 1) * 128]


def second_norm_back(r, i):
    grad, unit = r.back[rows_of(i)], r.u2[rows_of(i)]
    add_small(r, 20, column_sum(grad * unit))
    add_small(r, 21, column_sum(grad))
    y = r.y[i].astype(F32)
    gh1 = y + normalized_back(grad, unit, r.factors[rows_of(i), 1:2], r.params[20:21])
    r.back[rows_of(i)] = gh1
    gb = gh1.astype(BF16)
    r.gb[rows_of(i)] = gb
    add_small(r, 22, column_sum(gb.astype(F32)))
    go = (nt(gb, r.w_out[...]) * r.inverse[rows_of(i)]).astype(BF16)
    r.go[rows_of(i)] = go
    product = go.astype(F32) * r.o32[rows_of(i)]
    high = product.astype(BF16).astype(F32)
    low = product - high
    first = lax.broadcasted_iota(jnp.int32, (1, 128), 1) < 64
    for hp in range(4):
        columns = slice(hp * 128, (hp + 1) * 128)
        swapped = pltpu.roll(low[:, columns], 64, 1)
        r.god0[rows_of(i), columns] = jnp.where(first, high[:, columns], swapped).astype(BF16)
        r.god1[rows_of(i), columns] = jnp.where(first, swapped, high[:, columns]).astype(BF16)


def out_gradient(r):
    g_out = tn(r.o[...], r.gb[...]).astype(BF16)
    fold(r, [g_out[:, q * 128 : (q + 1) * 128] for q in range(4)], 3)


def result_of(r, i):
    r.out[i] = (r.result[rows_of(i)] + nn(r.act[rows_of(i)], r.w_down[...]) + r.params[23:24]).astype(BF16)


def attend_back(r, i, hp):
    q, k, v = (pair_of(r, i, hp, part) for part in range(3))
    columns = span_of(hp, 128)
    go = r.go[rows_of(i), columns]
    gq = gk = gv = 0.0
    for h in range(2):
        lanes = head_lanes(h)
        both = jnp.concatenate((go, (r.god0, r.god1)[h][rows_of(i), columns]), 1)
        wide = jnp.concatenate((v * lanes, jnp.full((512, 128), -1.0, BF16)), 1)
        expo = r.expo[i * 8 + hp * 2 + h]
        gs = (expo.astype(F32) * nt(both, wide)).astype(BF16)
        gq = gq + nn(gs, k * lanes)
        gk = gk + tn(gs, q * lanes)
        gv = gv + tn(expo, go * lanes)
    for part, value in enumerate((gq * 0.125, gk, gv)):
        r.gqkv[i][part][:, span_of(hp, 128)] = value.astype(BF16)


def first_norm_back(r, i):
    grad, unit = nt(jnp.concatenate([part[...] for part in r.gqkv[i]], 1), r.w_qkv[...]), r.u1[rows_of(i)]
    add_small(r, 18, column_sum(grad * unit))
    add_small(r, 19, column_sum(grad))
    gh0 = r.back[rows_of(i)] + normalized_back(grad, unit, r.factors[rows_of(i), 0:1], r.params[18:19])
    r.glat[i] = gh0.astype(BF16)
    total = column_sum(gh0)
    row = lax.broadcasted_iota(jnp.int32, (18, 1), 0)
    for x in range(4):
        mine = jnp.where(row == r.task_ids[i], total[:, x * 128 : (x + 1) * 128], 0.0)
        r.small[x, 0:18] = r.small[x, 0:18] + mine


def in_gradient(r, t):
    columns = jnp.concatenate(
        [jnp.concatenate([r.gqkv[i][ct // 4][:, span_of(ct % 4, 128)] for ct in COLUMNS[t]], 1) for i in range(2)]
    )
    g_in = tn(r.a1[...], columns).astype(BF16)
    fold(r, [g_in[:, q * 128 : (q + 1) * 128] for q in range(4)], t)


class Refs:
    def __init__(self, names, refs):
        for name, ref in zip(names, refs, strict=True):
            setattr(self, name, ref)


RAW = {
    "raw_in": ((4, 1536), BF16),
    "raw_out": ((4, 512), BF16),
    "raw_up": ((4, 2048), BF16),
    "raw_down": ((16, 512), BF16),
    "raw_table": ((4, 18), BF16),
    "raw_norms": ((4, 4), BF16),
    "raw_biases": ((2, 4), BF16),
    "raw_up_bias": ((1, 16), BF16),
}
INPUTS = ("task_ids", "counts", "lat_hbm", "y_hbm", *(f"{name}_hbm" for name in RAW))
OUTPUTS = ("out_hbm", "glat_hbm", "total", "s_total")
BLOCKS = (TILES, 4, 2, 4, 4, 16, 128)
SCRATCH = {
    **RAW,
    "own32": ((TILES, 16, 128), F32),
    "own": ((TILES, 16, 128), BF16),
    "small32": ((40, 128), F32),
    "table32": ((128, 128), F32),
    "own_small": ((32, 128), BF16),
    "orders": ((2, 256, 256), BF16),
    "lat": ((2, 512, 512), BF16),
    "y": ((2, 512, 512), BF16),
    "w_qkv": ((512, 1536), BF16),
    "w_out": ((512, 512), BF16),
    "w_up": ((512, 2048), BF16),
    "w_down": ((2048, 512), BF16),
    "params": ((32, 512), F32),
    "a1": ((1024, 512), BF16),
    "u1": ((1024, 512), F32),
    "qkv": ((1024, 1536), BF16),
    "expo": ((16, 512, 512), BF16),
    "o": ((1024, 512), BF16),
    "o32": ((1024, 512), F32),
    "inverse": ((1024, 512), F32),
    "result": ((1024, 512), F32),
    "a2": ((1024, 512), BF16),
    "u2": ((1024, 512), F32),
    "factors": ((1024, 2), F32),
    "act": ((1024, 2048), BF16),
    "gz": ((2, 1024, 512), BF16),
    "back": ((1024, 512), F32),
    "gb": ((1024, 512), BF16),
    "small": ((4, 32, 128), F32),
    "tiles": (BLOCKS, BF16),
    "slots": ((2, 3, 32, 128), BF16),
    "kept": ((4, 32, 128), BF16),
    "pair": ((4, 32, 128), BF16),
    "from_pair": ((TILES, 4, 4, 4, 16, 128), BF16),
    "from1": ((TILES, 3, 4, 4, 16, 128), BF16),
    "from2": ((TILES, 3, 4, 16, 128), BF16),
    "from3": ((TILES, 3, 16, 128), BF16),
    "s_pair": ((4, 32, 128), F32),
    "s_slots": ((3, 3, 32, 128), F32),
    "s_held": ((7, 32, 128), F32),
}
SEMAPHORES = {
    "g_send": (2, 3, 13),
    "g_recv": (2, 3, 13),
    "gs_send": (10,),
    "gs_recv": (10,),
    "p_send": (12,),
    "p_recv": (12,),
    "r_send": (17, 9),
    "r_recv": (17, 9),
    "rs_send": (10,),
    "rs_recv": (10,),
    "local": (12,),
}


def alias(r):
    r.go, r.god0, r.god1 = r.gz.at[0], r.gz.at[1], r.a2
    r.out, r.glat = r.lat, r.y
    r.gqkv = [r.w_up.at[:, span_of(part, 512)] for part in range(3)], [r.lat.at[0], r.lat.at[1], r.w_out]


def loop(count, step):
    lax.fori_loop(0, count, lambda n, carry: (step(n), carry)[1], 0)


def pack_own(r, pos):
    for t, blocks in enumerate(COLUMNS):
        raw = (r.raw_in, r.raw_out, r.raw_up)[0 if t < 3 else 1 if t == 3 else 2]
        for q, ct in enumerate(blocks):
            r.own32[t, 4 * q : 4 * q + 4] = raw[:, ct * 128 : (ct + 1) * 128].astype(F32)
    for t in range(8):
        r.own[t] = r.own32[t].astype(BF16)
    for t in range(4):
        r.own[8 + t] = r.raw_down[:, t * 128 : (t + 1) * 128]
    r.small32[...] = jnp.zeros_like(r.small32)
    r.table32[...] = jnp.zeros_like(r.table32)
    r.table32[0:4, 0:18] = r.raw_table[...].astype(F32)
    r.small32[18:22, 0:4] = r.raw_norms[...].astype(F32)
    r.small32[22:24, 0:4] = r.raw_biases[...].astype(F32)
    r.small32[32:33, 0:16] = r.raw_up_bias[...].astype(F32)
    offset, bias_row, bias_offset = small_place(pos)
    block = pltpu.roll(r.small32[0:32] + r.table32[...].T[0:32], offset, 1)
    bias = pltpu.roll(r.small32[32:40], bias_offset, 1)[0:1]
    row = lax.broadcasted_iota(jnp.int32, (32, 1), 0)
    r.own_small[...] = (block + jnp.where(row == bias_row, bias, 0.0)).astype(BF16)


def kernel(*refs):
    r = Refs((*INPUTS, *OUTPUTS, *SCRATCH, *SEMAPHORES), refs)
    alias(r)
    pos = my_position()
    loads = [
        pltpu.make_async_copy(getattr(r, f"{name}_hbm"), getattr(r, name), r.local.at[n])
        for n, name in enumerate((*RAW, "lat", "y"))
    ]
    store_out = pltpu.make_async_copy(r.out, r.out_hbm, r.local.at[10])
    store_glat = pltpu.make_async_copy(r.glat, r.glat_hbm, r.local.at[11])
    greet(pos)
    for load in loads:
        load.start()
    gathers = [Gather(w, r.own, r.tiles, r.g_send, r.g_recv, pos) for w in range(2)]
    tiny = SmallGather(r.own_small, r.slots, r.kept, r.pair, r.gs_send, r.gs_recv, pos)
    tiny_sum = SmallScatter(r.small, r.s_pair, r.s_slots, r.s_held, r.rs_send, r.rs_recv, pos)
    g_in = [Piece(r, pos, t, t, 1, ORDERS[t][::-1]) for t in range(3)]
    g_out = Piece(r, pos, 3, 3, 1, ("x", "z", "y"))
    down_orders = (("z", "y", "x"), ("y", "z", "x"))

    def chunk(j):
        up = Piece(r, pos, 4 + j, 4 + j, 1, ("x", "y", "z"))
        down = Piece(r, pos, 8 + j, 8, 4, (), x=j, stages=())
        halves = [Piece(r, pos, 8 + 2 * j + n, 8 + 2 * n, 2, down_orders[n], x=j, stages=(0, 1)) for n in range(2)]
        return up, down, halves

    chunks = [chunk(j) for j in range(4)]
    g_up, g_down, g_halves = zip(*chunks, strict=True)
    g_last = Piece(r, pos, 16, 8, 4, ("z", "y", "x"), stages=(2,))
    for load in loads[:8]:
        load.wait()
    pack_own(r, pos)
    greeted(pos)

    gathers[0].start(0)
    tiny.start(0)
    gathers[1].start(0)
    for t in range(TILES):
        r.tiles[t, pos["x"], pos["c"], pos["y"], pos["z"]] = r.own[t]
    r.small[...] = jnp.zeros_like(r.small)
    gathers[0].arrive(0)
    gathers[0].start(1)
    tiny.arrive(0)
    tiny.start(1)
    gathers[1].arrive(0)
    gathers[1].start(1)
    gathers[0].arrive(1)
    gathers[0].start(2)
    tiny.arrive(1)
    tiny.start(2)
    r.orders[0] = quarter_order()
    r.orders[1] = quarter_order(True)
    loads[9].wait()
    for i in range(2):
        add_small(r, 23, column_sum(r.y[i].astype(F32)))
    tiny.arrive(2)
    gathers[0].arrive(2)
    gathers[1].arrive(1)
    gathers[1].start(2)
    tiny.arrive_pair(r.params)
    loads[8].wait()
    for i in range(2):
        first_norm(r, i)
    for t in range(3):
        gathers[0].arrive_pair(t)
    for t in range(3):
        unfold(r, t, r.w_qkv)
    loop(2, lambda i: project(r, i))

    for n in range(8):
        attend(r, n // 4, n % 4)
    gathers[1].arrive(2)
    gathers[1].arrive_pair(0)
    unfold(r, 3, r.w_out)
    for i in range(2):
        second_norm(r, i)
    for part in (1, 2):
        gathers[1].arrive_pair(part)
    for t in range(4, 8):
        unfold(r, t, r.w_up)
    unfold_plain(r, r.w_down)
    for gather in gathers:
        gather.settle()
    tiny.settle()

    def leave(j):
        up, down, _ = chunk(j)
        up.pair_copy().start()
        down.pair_copy().start()

    def begin(j):
        up, down, halves = chunk(j)
        up.pair_add()
        down.pair_add()
        for piece in (up, *halves):
            piece.start(0)

    def turn(piece, stage):
        piece.add(stage)
        piece.start(stage + 1)

    def second(j):
        for piece in (g_up[j], *g_halves[j]):
            turn(piece, 0)

    def third(j):
        turn(g_up[j], 1)
        for piece in g_halves[j]:
            piece.add(1)

    r.back[...] = jnp.zeros_like(r.back)

    def middle(j):
        feed_forward(r, j)
        chunk_gradients(r, j)
        leave(j)

        @pl.when(j > 0)
        def _():
            begin(j - 1)

    loop(4, middle)
    second(0)
    loop(2, lambda i: second_norm_back(r, i))
    begin(3)
    second(1)
    out_gradient(r)
    g_out.pair_copy().start()

    def backward(half):
        for n in range(4):
            attend_back(r, n % 2, half * 2 + n // 2)

        @pl.when(half == 0)
        def _():
            g_out.pair_add()
            g_out.start(0)
            second(2)
            third(0)
            in_gradient(r, 0)
            g_in[0].pair_copy().start()
            second(3)
            third(1)

    loop(2, backward)
    in_gradient(r, 1)
    g_in[1].pair_copy().start()
    g_in[0].pair_add()
    g_in[0].start(0)
    turn(g_out, 0)
    third(2)
    in_gradient(r, 2)
    g_in[2].pair_copy().start()
    g_in[1].pair_add()
    g_in[1].start(0)
    third(3)
    g_last.start(2)
    first_norm_back(r, 0)
    g_in[2].pair_add()
    g_in[2].start(0)
    first_norm_back(r, 1)
    tiny_sum.pair_copy().start()
    store_glat.start()
    turn(g_in[0], 0)
    turn(g_out, 1)
    tiny_sum.add_pair()
    tiny_sum.start(0)
    loop(2, lambda i: result_of(r, i))
    store_out.start()
    tiny_sum.add(0)
    tiny_sum.start(1)
    turn(g_in[2], 0)
    turn(g_in[1], 0)
    turn(g_in[0], 1)
    for piece in (*g_up, g_last):
        piece.add(2)
    tiny_sum.add(1)
    tiny_sum.start(2)
    turn(g_in[2], 1)
    turn(g_in[1], 1)
    g_out.add(2)
    g_in[0].add(2)
    for piece in (*g_in, g_out, *g_up, *g_down, *(half for halves in g_halves for half in halves), g_last):
        piece.settle()
    store_out.wait()
    store_glat.wait()
    g_in[1].add(2)
    g_in[2].add(2)
    tiny_sum.add(2)
    r.s_total[...] = r.s_held[6]
    tiny_sum.settle()


SHAPES = ((4, 18), (4, 4), (4, 1536), (4, 512), (2, 4), (4, 2048), (1, 16), (16, 512))


def finish(*refs):
    out_in, glat_in, total_hbm, small_hbm, out, glat, *rest = refs
    targets, (held, total, small), parts, (sems, load_sems, store_sems) = rest[:8], rest[8:11], rest[11:19], rest[19:]
    table, norms, w_in, w_out, biases, w_up, up_bias, w_down = parts
    loads = [
        pltpu.make_async_copy(total_hbm, total, load_sems.at[0]),
        pltpu.make_async_copy(small_hbm, small, load_sems.at[1]),
    ]
    for load in loads:
        load.start()
    reads, writes = [], []
    for n, (source, target) in enumerate(((out_in, out), (glat_in, glat))):
        for k in range(4):
            slot, rows = 4 * n + k, pl.ds(k % 2 * 256, 256)
            reads.append(pltpu.make_async_copy(source.at[k // 2, rows], held.at[slot], sems.at[0, slot]))
            writes.append(pltpu.make_async_copy(held.at[slot], target.at[k // 2, rows], sems.at[1, slot]))
    for read in reads:
        read.start()
    for n in range(4):
        reads[n].wait()
        writes[n].start()
    for load in loads:
        load.wait()
    for t, blocks in enumerate(COLUMNS):
        to = (w_in, w_out, w_up)[0 if t < 3 else 1 if t == 3 else 2]
        for q, ct in enumerate(blocks):
            to[:, ct * 128 : (ct + 1) * 128] = total[t, 4 * q : 4 * q + 4]
    for t in range(4):
        w_down[:, t * 128 : (t + 1) * 128] = total[8 + t]
    offset, bias_row, bias_offset = small_place(my_position())
    block = pltpu.roll(small[...], lax.rem(128 - offset, 128), 1)
    table[...] = jnp.concatenate((block, jnp.zeros((96, 128), F32))).T[0:4, 0:18]
    norms[...] = block[18:22, 0:4]
    biases[...] = block[22:24, 0:4]
    row = lax.broadcasted_iota(jnp.int32, (32, 1), 0)
    bias = jnp.sum(jnp.where(row == bias_row, small[...], 0.0), axis=0, keepdims=True)
    bias = pltpu.roll(jnp.broadcast_to(bias, (8, 128)), lax.rem(128 - bias_offset, 128), 1)
    up_bias[...] = bias[0:1, 0:16]
    stores = [
        pltpu.make_async_copy(part, target, store_sems.at[n])
        for n, (part, target) in enumerate(zip(parts, targets, strict=True))
    ]
    for store in stores:
        store.start()
    for n in range(4, 8):
        reads[n].wait()
        writes[n].start()
    for copy in (*stores, *writes):
        copy.wait()


def whole(task_ids, counts, latents, cotangent, *raw):
    vmem = pl.BlockSpec(memory_space=pltpu.VMEM)
    smem = pl.BlockSpec(memory_space=pltpu.SMEM)
    hbm = pl.BlockSpec(memory_space=pl.ANY)
    array = jax.ShapeDtypeStruct(latents.shape, BF16)
    found = pl.pallas_call(
        kernel,
        out_shape=[
            array,
            array,
            jax.ShapeDtypeStruct((TILES, 16, 128), F32),
            jax.ShapeDtypeStruct((32, 128), F32),
        ],
        in_specs=[smem, smem] + [hbm] * (2 + len(RAW)),
        out_specs=[hbm, hbm, vmem, vmem],
        scratch_shapes=[pltpu.VMEM(shape, dtype) for shape, dtype in SCRATCH.values()]
        + [pltpu.SemaphoreType.DMA(shape) for shape in SEMAPHORES.values()],
        compiler_params=pltpu.CompilerParams(
            collective_id=0, has_side_effects=True, vmem_limit_bytes=121 * 2**19
        ),
    )(task_ids, counts, latents, cotangent, *raw)
    return pl.pallas_call(
        finish,
        out_shape=[array, array] + [jax.ShapeDtypeStruct(shape, F32) for shape in SHAPES],
        in_specs=[hbm] * 4,
        out_specs=[hbm] * 10,
        scratch_shapes=[
            pltpu.VMEM((8, 256, 512), BF16),
            pltpu.VMEM((TILES, 16, 128), F32),
            pltpu.VMEM((32, 128), F32),
            *(pltpu.VMEM(shape, F32) for shape in SHAPES),
            pltpu.SemaphoreType.DMA((2, 8)),
            pltpu.SemaphoreType.DMA((2,)),
            pltpu.SemaphoreType.DMA((8,)),
        ],
    )(*found)


def body(
    latents,
    task_ids,
    slot_counts,
    cotangent,
    task_embed,
    norms,
    attn_in,
    attn_out,
    out_biases,
    mlp_in,
    mlp_in_bias,
    mlp_out,
):
    raw = (attn_in, attn_out, mlp_in, mlp_out, task_embed.T, norms, out_biases, mlp_in_bias.reshape(1, 16))
    found = list(whole(task_ids, slot_counts, latents, cotangent, *raw))
    found[2] = found[2].T
    found[8] = found[8].reshape(16)
    return tuple(found)


def solution(mesh):
    in_specs = (
        P(("dp", "fsdp"), None, None),
        P(("dp", "fsdp")),
        P(("dp", "fsdp")),
        P(("dp", "fsdp"), None, None),
        P(None, ("dp", "fsdp")),
        P(None, ("dp", "fsdp")),
        P(("dp", "fsdp"), None),
        P(("dp", "fsdp"), None),
        P(None, ("dp", "fsdp")),
        P(("dp", "fsdp"), None),
        P(("dp", "fsdp")),
        P(("dp", "fsdp"), None),
    )
    out_specs = (
        P(("dp", "fsdp"), None, None),
        P(("dp", "fsdp"), None, None),
        P(None, ("dp", "fsdp")),
        P(None, ("dp", "fsdp")),
        P(("dp", "fsdp"), None),
        P(("dp", "fsdp"), None),
        P(None, ("dp", "fsdp")),
        P(("dp", "fsdp"), None),
        P(("dp", "fsdp")),
        P(("dp", "fsdp"), None),
    )
    return jax.shard_map(body, mesh=mesh, in_specs=in_specs, out_specs=out_specs, check_vma=False)
```
